128 devices in a mesh: dom: 128 (over y, x, z, core).
Axes of the slice: x: 4, y: 4, z: 4, core: 2. Of those that a mesh axis runs over, the one named last changes fastest.
Arguments:
- node_features: bfloat16 [262144, 128], P('dom'), may hold values from -6 to 6
- w_self: bfloat16 [128, 128], replicated, may hold values from -0.5 to 0.5
- w_neigh: bfloat16 [128, 128], replicated, may hold values from -4 to 4
- output_bias: float32 [128], replicated, may hold values from -3 to 3
- local_tiles: bfloat16 [2048, 22, 128, 128], P('dom'), may hold values from 0 to 1, as said below
- halo_tiles: bfloat16 [2048, 20, 128, 128], P('dom'), may hold values from 0 to 1, as said below
- local_cols: int32 [2048, 22], P('dom'), may hold values from 0 to 15
- halo_cols: int32 [2048, 20], P('dom'), may hold values from 0 to 29
- send_rows: int32 [640, 768], P('dom'), may hold values from 0 to 2047
- degree: int32 [262144], P('dom'), may hold values from 56 to 112, as said below
- cotangent: bfloat16 [262144, 128], P('dom'), may hold values from -6 to 6
Outputs:
- output: bfloat16 [262144, 128], P('dom')
- grad_features: float32 [262144, 128], P('dom')
- grad_self: float32 [128, 128], replicated
- grad_neigh: float32 [128, 128], replicated
The draws below stay inside these ranges and needn't reach their ends.
Inputs may be any that keep to these rules, and one draw needn't show every extreme that they name: `local_tiles`: entries are 0 or 1. `halo_tiles`: entries are 0 or 1. `send_rows`: row numbers within the sending partition; a row may be listed more than once. A node's degree is the number of ones in its row over its 22 local and 20 boundary tiles.
All inputs are finite; a program needn't handle non-finite values.
Results may differ from the reference program's by a relative error of at most 0.0052.
Values may be sent and summed in bfloat16 or wider, within the bound.
No kernel may reach another device: no remote copies, remote signals or barrier semaphores. Data moves between devices by JAX's collectives and lax.ppermute only.
A program may use at most 192 MiB of HBM per device.

```python
import math
import jax
import jax.numpy as jnp
import numpy as np
from jax import lax

F = 128
H = 128
TILE = 128
BLK_DEV = 16
TL = 22
TH = 20
ROUNDS = 5
BROWS = 768
ROWS_DEV = 2048
NODES = 262144
BLOCKS = 2048
HB = 30
DLO = 56
N_DOM = 128


def node_params(key):
    key_degree, key_offset, key_stride = jax.random.split(key, 3)
    slot_total = (TL + TH) * TILE
    degrees = jax.random.randint(key_degree, (NODES,), DLO, 2 * DLO + 1).astype(jnp.int32)
    degrees = degrees.at[0].set(2 * DLO).at[1].set(DLO)
    offsets = jax.random.randint(key_offset, (NODES,), 0, slot_total).astype(jnp.int32)
    primes = jnp.array([11, 13, 17, 19, 23, 29, 31, 37, 41, 43, 47, 53], jnp.int32)
    strides = primes[jax.random.randint(key_stride, (NODES,), 0, 12)]
    return (degrees, offsets, strides)


def edge_mask(key, first_slot, tile_count):
    degrees, offsets, strides = node_params(key)
    slot_total = (TL + TH) * TILE
    shape_rows = (BLOCKS, 1, TILE, 1)
    degrees = degrees.reshape(shape_rows)
    offsets = offsets.reshape(shape_rows)
    strides = strides.reshape(shape_rows)
    tile_index = jnp.arange(tile_count, dtype=jnp.int32).reshape(1, tile_count, 1, 1)
    column_index = jnp.arange(TILE, dtype=jnp.int32).reshape(1, 1, 1, TILE)
    slots = first_slot + tile_index * TILE + column_index
    ranks = (slots - offsets) % slot_total * strides % slot_total
    return (ranks < degrees).astype(jnp.float32).astype(jnp.bfloat16)


def draw_local_tiles(key, part):
    return edge_mask(key, 0, TL)


def draw_halo_tiles(key, part):
    return edge_mask(key, TL * TILE, TH)


def draw_degree(key, part):
    return node_params(key)[0]


def with_ends(values, stream_key, least, high):
    shape = values.shape
    index_at = [jax.random.randint(jax.random.fold_in(stream_key, axis), (), 0, shape[axis]) for axis in range(len(shape))]
    values = values.at[tuple(index_at)].set(least)
    longest = shape.index(max(shape))
    index_at[longest] = (index_at[longest] + 1) % shape[longest]
    return values.at[tuple(index_at)].set(high)


def steps_of(key, extent, cuts, low, largest):
    def one(axis_at, blocks):
        draws = jax.random.uniform(jax.random.fold_in(jax.random.fold_in(key, 6), axis_at), (blocks,), jnp.float32, low / len(cuts), largest / len(cuts))
        return jnp.repeat(jnp.exp(draws), extent[axis_at] // blocks).reshape((-1,) + (1,) * (len(extent) - axis_at - 1))

    gain = one(*cuts[0])
    for cut in cuts[1:]:
        gain = gain * one(*cut)
    return gain


def noise(key, dims, spread, limit, cuts=(), held_as=jnp.bfloat16):
    entries = jax.random.normal(key, dims, jnp.float32) * spread
    if len(cuts) > 0:
        entries = steps_of(key, dims, cuts, -0.22, 0.18) * entries
    return jnp.clip(entries, min=-limit, max=limit).astype(held_as)


def setup_inputs(seed: int = 0) -> dict:
    key_of = jax.random.split(jax.random.key(seed), 12)
    return {
        "node_features": noise(key_of[0], (NODES, F), 1.0, 6.0, ((0, 128),)),
        "w_self": noise(key_of[1], (F, H), F ** -0.5, 0.5),
        "w_neigh": noise(key_of[2], (F, H), (max(1, F // 64)) ** -0.5, 4.0),
        "output_bias": noise(key_of[3], (H,), 0.5, 3.0, (), jnp.float32),
        "local_tiles": draw_local_tiles(jax.random.fold_in(key_of[11], 71), 0),
        "halo_tiles": draw_halo_tiles(jax.random.fold_in(key_of[11], 71), 0),
        "local_cols": with_ends(jax.random.randint(key_of[6], (BLOCKS, TL), 0, BLK_DEV), jax.random.fold_in(key_of[6], 1), 0, BLK_DEV - 1).astype(jnp.int32),
        "halo_cols": with_ends(jax.random.randint(key_of[7], (BLOCKS, TH), 0, HB), jax.random.fold_in(key_of[7], 1), 0, HB - 1).astype(jnp.int32),
        "send_rows": with_ends(jax.random.randint(key_of[8], (N_DOM * ROUNDS, BROWS), 0, ROWS_DEV), jax.random.fold_in(key_of[8], 1), 0, ROWS_DEV - 1).astype(jnp.int32),
        "degree": draw_degree(jax.random.fold_in(key_of[11], 71), 0),
        "cotangent": noise(key_of[10], (NODES, H), 1.0, 6.0, ((0, 128),)),
    }


def partition_pass(packed_args, w_self, w_neigh, output_bias):
    feature_part, halo_rows, local_tiles, halo_tiles, local_cols, halo_cols, degree, cotangent = packed_args
    feature_blocks = feature_part.reshape(BLK_DEV, TILE, F)
    summed = jnp.einsum('btij,btjf->bif', local_tiles.astype(jnp.float32), feature_blocks[local_cols].astype(jnp.float32))
    summed = summed + jnp.einsum('btij,btjf->bif', halo_tiles.astype(jnp.float32), halo_rows[halo_cols].astype(jnp.float32))
    degrees = degree.astype(jnp.float32)[:, None]
    aggregate = (summed.reshape(ROWS_DEV, F) / degrees).astype(jnp.bfloat16)
    preact = jnp.dot(feature_part, w_self, preferred_element_type=jnp.float32) + jnp.dot(aggregate, w_neigh, preferred_element_type=jnp.float32) + output_bias.astype(jnp.float32)
    output = jax.nn.silu(preact).astype(jnp.bfloat16)
    sigmoid_pre = jax.nn.sigmoid(preact)
    grad_pre = (cotangent.astype(jnp.float32) * sigmoid_pre * (1.0 + preact * (1.0 - sigmoid_pre))).astype(jnp.bfloat16)
    self_part = jnp.dot(feature_part.T, grad_pre, preferred_element_type=jnp.float32)
    neigh_part = jnp.dot(aggregate.T, grad_pre, preferred_element_type=jnp.float32)
    grad_own = jnp.dot(grad_pre, w_self.T, preferred_element_type=jnp.float32)
    scaled = (jnp.dot(grad_pre, w_neigh.T, preferred_element_type=jnp.float32) / degrees).astype(jnp.bfloat16)
    scaled = scaled.reshape(BLK_DEV, TILE, F).astype(jnp.float32)
    local_products = jnp.einsum('btij,bif->btjf', local_tiles.astype(jnp.float32), scaled)
    halo_products = jnp.einsum('btij,bif->btjf', halo_tiles.astype(jnp.float32), scaled)
    local_table = (local_cols[..., None] == jnp.arange(BLK_DEV, dtype=jnp.int32)).astype(jnp.float32)
    halo_table = (halo_cols[..., None] == jnp.arange(HB, dtype=jnp.int32)).astype(jnp.float32)
    local_grad = jnp.einsum('btc,btjf->cjf', local_table, local_products, precision=lax.Precision.HIGHEST)
    halo_grad = jnp.einsum('btc,btjf->cjf', halo_table, halo_products, precision=lax.Precision.HIGHEST)
    grad_part = grad_own + local_grad.reshape(ROWS_DEV, F)
    return (output, grad_part, self_part, neigh_part, halo_grad.reshape(ROUNDS, BROWS, F))

def reference(node_features, w_self, w_neigh, output_bias, local_tiles, halo_tiles, local_cols, halo_cols, send_rows, degree, cotangent):
    feature_parts = node_features.reshape(N_DOM, ROWS_DEV, F)
    send_lists = send_rows.reshape(N_DOM, ROUNDS, BROWS)
    sent_rows = jax.vmap(lambda part_rows, picked_rows: part_rows[picked_rows])(feature_parts, send_lists)
    partners = [np.arange(N_DOM) ^ 1 << index for index in range(ROUNDS)]
    halo = jnp.stack([sent_rows[partners[index], index] for index in range(ROUNDS)], axis=1)
    halo = halo.reshape(N_DOM, HB, TILE, F)
    packed = (feature_parts, halo, local_tiles.reshape(N_DOM, BLK_DEV, TL, TILE, TILE), halo_tiles.reshape(N_DOM, BLK_DEV, TH, TILE, TILE), local_cols.reshape(N_DOM, BLK_DEV, TL), halo_cols.reshape(N_DOM, BLK_DEV, TH), degree.reshape(N_DOM, ROWS_DEV), cotangent.reshape(N_DOM, ROWS_DEV, H))
    output, grad_part, self_part, neigh_part, halo_grad = lax.map(lambda packed_args: partition_pass(packed_args, w_self, w_neigh, output_bias), packed)
    returned = jnp.stack([halo_grad[partners[index], index] for index in range(ROUNDS)], axis=1)
    grad_part = jax.vmap(lambda target, picked_rows, values: target.at[picked_rows.reshape(-1)].add(values.reshape(-1, F)))(grad_part, send_lists, returned)
    grad_scale = 1.0 / math.sqrt(NODES)
    grad_self = lax.optimization_barrier(jnp.sum(self_part, axis=0)) * grad_scale
    grad_neigh = lax.optimization_barrier(jnp.sum(neigh_part, axis=0)) * grad_scale
    return (output.reshape(NODES, H), grad_part.reshape(NODES, F), grad_self, grad_neigh)
```

```python
import functools
import math

import jax
import jax.numpy as jnp
from jax import lax
from jax.experimental import pallas as pl
from jax.experimental.pallas import tpu as pltpu
from jax.sharding import PartitionSpec as P

TILE = 128
VMEM = pltpu.VMEM
KEEP = True
LIMIT = 28 * 1024 * 1024


def vspec():
    return pl.BlockSpec(memory_space=VMEM)


def sspec():
    return pl.BlockSpec(memory_space=pltpu.SMEM)


def params(limit=LIMIT):
    return pltpu.CompilerParams(vmem_limit_bytes=limit)


def kept(shape, dtype):
    return VMEM(shape, dtype) if KEEP else jax.ShapeDtypeStruct(shape, dtype)


def pinned(array):
    return pltpu.with_memory_space_constraint(array, VMEM) if KEEP else array


def nt_dot(left, right):
    return lax.dot_general(
        left, right, (((1,), (1,)), ((), ())), preferred_element_type=jnp.float32
    )


def nn_dot(left, right):
    return jnp.dot(left, right, preferred_element_type=jnp.float32)


def pick_kernel(rounds, rows_ref, x_ref, *refs):
    outs, (wide, picked) = refs[: len(rounds)], refs[len(rounds) :]
    wide[...] = x_ref[...].astype(jnp.float32)
    count = picked.shape[0]
    step = 32

    for place, round_index in enumerate(rounds):

        def body(j, carry, round_index=round_index):
            base = pl.multiple_of(j * step, step)
            for u in range(step):
                row = rows_ref[round_index, base + u]
                picked[pl.ds(base + u, 1), :] = wide[pl.ds(row, 1), :]
            return carry

        lax.fori_loop(0, count // step, body, 0)
        outs[place][...] = picked[...].astype(jnp.bfloat16)


def pick_rows(rounds, send_rows, features):
    row_count, width = features.shape
    boundary = send_rows.shape[1]
    return pl.pallas_call(
        functools.partial(pick_kernel, rounds),
        out_shape=[jax.ShapeDtypeStruct((boundary, width), jnp.bfloat16) for _ in rounds],
        in_specs=[sspec(), vspec()],
        out_specs=[vspec() for _ in rounds],
        scratch_shapes=[VMEM((row_count, width), jnp.float32), VMEM((boundary, width), jnp.float32)],
        compiler_params=params(),
        cost_estimate=pl.CostEstimate(
            flops=4_000_000 * len(rounds), bytes_accessed=1_000_000, transcendentals=0
        ),
    )(send_rows, features)


def densify_kernel(cols_ref, tiles_ref, dense_ref, slots, sems):
    nblocks, count = tiles_ref.shape[:2]
    slabs = dense_ref.shape[0]
    depth = slots.shape[0]

    def fetch(i, slot):
        return pltpu.make_async_copy(tiles_ref.at[i], slots.at[slot], sems.at[slot])

    for d in range(depth - 1):
        fetch(d, d).start()

    def body(i, carry):
        slot = lax.rem(i, depth)

        @pl.when(i + depth - 1 < nblocks)
        def _():
            fetch(i + depth - 1, lax.rem(i + depth - 1, depth)).start()

        rows = pl.ds(pl.multiple_of(i * TILE, TILE), TILE)
        for c in range(slabs):
            dense_ref[c, rows, :] = jnp.zeros((TILE, TILE), jnp.bfloat16)
        fetch(i, slot).wait()
        for t in range(count):
            col = cols_ref[i, t]
            dense_ref[col, rows, :] = dense_ref[col, rows, :] + slots[slot, t]
        return carry

    lax.fori_loop(0, nblocks, body, 0)


def densify(cols, tiles, slabs):
    nblocks, count = cols.shape
    depth = 4
    return pl.pallas_call(
        densify_kernel,
        out_shape=kept((slabs, nblocks * TILE, TILE), jnp.bfloat16),
        in_specs=[sspec(), pl.BlockSpec(memory_space=pl.ANY)],
        out_specs=vspec(),
        scratch_shapes=[
            VMEM((depth, count, TILE, TILE), jnp.bfloat16),
            pltpu.SemaphoreType.DMA((depth,)),
        ],
        compiler_params=params(),
        cost_estimate=pl.CostEstimate(
            flops=16_000_000, bytes_accessed=nblocks * count * TILE * TILE * 2, transcendentals=0
        ),
    )(cols, tiles)


def forward_kernel(first, n, has_acc, dense_ref, x_ref, *refs):
    acc_ref, out_ref = refs if has_acc else (None, refs[0])
    chunk = 512

    def body(j, carry):
        rows = pl.ds(pl.multiple_of(j * chunk, chunk), chunk)
        left = jnp.concatenate([dense_ref[first + c, rows, :] for c in range(n)], axis=1)
        total = nn_dot(left, x_ref[...])
        if has_acc:
            total = total + acc_ref[rows, :]
        out_ref[rows, :] = total
        return carry

    lax.fori_loop(0, out_ref.shape[0] // chunk, body, 0)


def forward(dense, first, blocks, acc):
    n = blocks.shape[0] // TILE
    rows = dense.shape[1]
    args = [pinned(dense), blocks] + ([] if acc is None else [acc])
    return pl.pallas_call(
        functools.partial(forward_kernel, first, n, acc is not None),
        out_shape=jax.ShapeDtypeStruct((rows, TILE), jnp.float32),
        in_specs=[vspec()] * len(args),
        out_specs=vspec(),
        compiler_params=params(),
        cost_estimate=pl.CostEstimate(
            flops=2 * rows * n * TILE * TILE, bytes_accessed=rows * TILE * 4, transcendentals=0
        ),
    )(*args)


def across(degree_ref, i):
    line = degree_ref[pl.ds(i, 1), :].astype(jnp.float32)
    return line, jnp.broadcast_to(line, (TILE, TILE)).T


def middle_kernel(
    sum_ref, x_ref, ct_ref, deg_ref, ws_ref, wn_ref, bias_ref, out_ref, agg_ref, gp_ref, st_ref
):
    for i in range(sum_ref.shape[0] // TILE):
        rows = pl.ds(i * TILE, TILE)
        line, column = across(deg_ref, i)
        agg = (sum_ref[rows, :] / column).astype(jnp.bfloat16)
        agg_ref[rows, :] = agg
        preact = nn_dot(x_ref[rows, :], ws_ref[...]) + nn_dot(agg, wn_ref[...]) + bias_ref[...]
        sig = jax.nn.sigmoid(preact)
        out_ref[rows, :] = (preact * sig).astype(jnp.bfloat16)
        grad = ct_ref[rows, :].astype(jnp.float32) * sig * (1.0 + preact * (1.0 - sig))
        grad = grad.astype(jnp.bfloat16)
        gp_ref[rows, :] = grad
        st_ref[:, rows] = (nt_dot(wn_ref[...], grad) / line).astype(jnp.bfloat16)


def middle(summed, features, cotangent, degree, w_self, w_neigh, bias):
    rows, width = features.shape
    half = jax.ShapeDtypeStruct((rows, width), jnp.bfloat16)
    return pl.pallas_call(
        middle_kernel,
        out_shape=[half, half, half, jax.ShapeDtypeStruct((width, rows), jnp.bfloat16)],
        in_specs=[vspec()] * 7,
        out_specs=[vspec()] * 4,
        compiler_params=params(),
        cost_estimate=pl.CostEstimate(
            flops=2 * rows * 3 * width * width, bytes_accessed=5_000_000, transcendentals=rows * width
        ),
    )(summed, features, cotangent, degree, w_self, w_neigh, bias)


def weights_kernel(x_ref, agg_ref, gp_ref, out_ref):
    both = jnp.concatenate([x_ref[...], agg_ref[...]], axis=1)
    out_ref[...] = lax.dot_general(
        both, gp_ref[...], (((0,), (0,)), ((), ())), preferred_element_type=jnp.float32
    )


def weight_parts(features, aggregate, grad_pre):
    rows, width = features.shape
    return pl.pallas_call(
        weights_kernel,
        out_shape=jax.ShapeDtypeStruct((2 * width, width), jnp.float32),
        in_specs=[vspec()] * 3,
        out_specs=vspec(),
        compiler_params=params(),
        cost_estimate=pl.CostEstimate(
            flops=4 * rows * width * width, bytes_accessed=1_500_000, transcendentals=0
        ),
    )(features, aggregate, grad_pre)


def back_kernel(rounds, per, st_ref, dense_ref, *outs):
    for place, round_index in enumerate(rounds):
        for c in range(0, per, 2):
            slab = round_index * per + c
            right = jnp.concatenate([dense_ref[slab], dense_ref[slab + 1]], axis=1)
            product = nn_dot(st_ref[...], right)
            outs[place][pl.ds(c * TILE, 2 * TILE), :] = product.T.astype(jnp.bfloat16)


def back(rounds, per, scaled_t, dense):
    width, rows = scaled_t.shape
    return pl.pallas_call(
        functools.partial(back_kernel, rounds, per),
        out_shape=[jax.ShapeDtypeStruct((per * TILE, width), jnp.bfloat16) for _ in rounds],
        in_specs=[vspec()] * 2,
        out_specs=[vspec() for _ in rounds],
        compiler_params=params(),
        cost_estimate=pl.CostEstimate(
            flops=2 * rows * len(rounds) * per * TILE * width, bytes_accessed=500_000, transcendentals=0
        ),
    )(scaled_t, pinned(dense))


def own_kernel(st_ref, dense_ref, gp_ref, ws_ref, out_ref):
    for c in range(0, dense_ref.shape[0], 2):
        rows = pl.ds(c * TILE, 2 * TILE)
        right = jnp.concatenate([dense_ref[c], dense_ref[c + 1]], axis=1)
        product = nn_dot(st_ref[...], right)
        out_ref[rows, :] = product.T + nt_dot(gp_ref[rows, :], ws_ref[...])


def own(scaled_t, dense, grad_pre, w_self):
    width, rows = scaled_t.shape
    return pl.pallas_call(
        own_kernel,
        out_shape=jax.ShapeDtypeStruct((rows, width), jnp.float32),
        in_specs=[vspec()] * 4,
        out_specs=vspec(),
        compiler_params=params(),
        cost_estimate=pl.CostEstimate(
            flops=2 * rows * rows * width, bytes_accessed=1_500_000, transcendentals=0
        ),
    )(scaled_t, pinned(dense), grad_pre, w_self)


def place_kernel(rounds, rows_ref, acc_ref, *refs):
    returned, out_ref = refs[:-1], refs[-1]
    chunk = 256
    boundary = rows_ref.shape[1]

    def body(j, carry):
        base = pl.multiple_of(j * chunk, chunk)
        total = acc_ref[pl.ds(base, chunk), :]
        for place, round_index in enumerate(rounds):
            wanted = rows_ref[pl.ds(round_index, 1), :] - base
            index = lax.broadcasted_iota(jnp.int32, (chunk, boundary), 0)
            onehot = jnp.where(index == wanted, 1.0, 0.0).astype(jnp.bfloat16)
            total = total + nn_dot(onehot, returned[place][...])
        out_ref[pl.ds(base, chunk), :] = total
        return carry

    lax.fori_loop(0, out_ref.shape[0] // chunk, body, 0)


def place_rows(rounds, send_rows, acc, returned):
    rows, width = acc.shape
    return pl.pallas_call(
        functools.partial(place_kernel, rounds),
        out_shape=jax.ShapeDtypeStruct((rows, width), jnp.float32),
        in_specs=[vspec()] * (2 + len(rounds)),
        out_specs=vspec(),
        compiler_params=params(),
        cost_estimate=pl.CostEstimate(
            flops=2 * rows * len(rounds) * send_rows.shape[1] * width,
            bytes_accessed=2_000_000,
            transcendentals=0,
        ),
    )(send_rows, acc, *returned)


def swapped(shard, mask):
    return lax.ppermute(shard, "dom", [(i, i ^ mask) for i in range(lax.axis_size("dom"))])


def summed_everywhere(parts):
    me = lax.axis_index("dom")
    core, z = me & 1, (me >> 1) & 3
    halves = parts.reshape(2, -1, parts.shape[1])
    own_half = halves[core] + swapped(halves[1 - core], 1)
    quarters = own_half.reshape(4, -1, parts.shape[1])
    got = [swapped(quarters[z ^ d], d << 1) for d in (1, 2, 3)]
    total = (quarters[z] + got[0]) + (got[1] + got[2])
    for bit in (3, 5):
        got = [swapped(total, d << bit) for d in (1, 2, 3)]
        total = (total + got[0]) + (got[1] + got[2])
    pieces = jnp.stack([total] + [swapped(total, d << 1) for d in (1, 2, 3)])
    half = pieces[z ^ jnp.arange(4, dtype=jnp.int32)].reshape(own_half.shape)
    other = swapped(half, 1)
    first = jnp.where(core == 0, half, other)
    second = jnp.where(core == 0, other, half)
    return first, second


def local(
    node_features,
    w_self,
    w_neigh,
    output_bias,
    local_tiles,
    halo_tiles,
    local_cols,
    halo_cols,
    send_rows,
    degree,
    cotangent,
):
    row_count, width = node_features.shape
    nblocks = local_tiles.shape[0]
    round_count, boundary = send_rows.shape
    per = boundary // TILE
    order = (2, 4, 1, 3, 0)
    received = {}
    for rounds in ((2, 4), (1, 3, 0)):
        picked = pick_rows(rounds, send_rows, node_features)
        for round_index, rows in zip(rounds, picked):
            received[round_index] = swapped(rows, 1 << round_index)
    dense_local = densify(local_cols, local_tiles, nblocks)
    summed = forward(dense_local, 0, node_features, None)
    dense_halo = densify(halo_cols, halo_tiles, round_count * per)
    for round_index in reversed(order):
        summed = forward(dense_halo, round_index * per, received[round_index], summed)
    output, aggregate, grad_pre, scaled_t = middle(
        summed,
        node_features,
        cotangent,
        degree.reshape(nblocks, TILE),
        w_self,
        w_neigh,
        output_bias.reshape(1, width),
    )
    returned = {}
    for rounds in ((2,), (4,), (1, 3, 0)):
        grads = back(rounds, per, scaled_t, dense_halo)
        for round_index, rows in zip(rounds, grads):
            returned[round_index] = swapped(rows, 1 << round_index)
    parts = weight_parts(node_features, aggregate, grad_pre)
    grad_self, grad_neigh = summed_everywhere(parts)
    grad_scale = 1.0 / math.sqrt(row_count * lax.axis_size("dom"))
    grad_features = own(scaled_t, dense_local, grad_pre, w_self)
    for rounds in ((0, 3), (1, 4, 2)):
        grad_features = place_rows(rounds, send_rows, grad_features, [returned[r] for r in rounds])
    return (output, grad_features, grad_self * grad_scale, grad_neigh * grad_scale)


def solution(mesh):
    in_specs = (
        P("dom", None),
        P(),
        P(),
        P(),
        P("dom", None, None, None),
        P("dom", None, None, None),
        P("dom", None),
        P("dom", None),
        P("dom", None),
        P("dom"),
        P("dom", None),
    )
    out_specs = (P("dom", None), P("dom", None), P(), P())
    return jax.shard_map(local, mesh=mesh, in_specs=in_specs, out_specs=out_specs, check_vma=False)
```

```python
import functools
import math

import jax
import jax.numpy as jnp
from jax import lax
from jax.experimental import pallas as pl
from jax.experimental.pallas import tpu as pltpu
from jax.sharding import PartitionSpec as P

TILE = 128
VMEM = pltpu.VMEM
LIMIT = 16 * 1024 * 1024


def vspec():
    return pl.BlockSpec(memory_space=VMEM)


def sspec():
    return pl.BlockSpec(memory_space=pltpu.SMEM)


def params(limit=LIMIT):
    return pltpu.CompilerParams(vmem_limit_bytes=limit)


def cost(flops, size, transcendentals=0):
    return pl.CostEstimate(flops=flops, bytes_accessed=size, transcendentals=transcendentals)


def pinned(array):
    return pltpu.with_memory_space_constraint(array, VMEM)


def nt_dot(left, right):
    return lax.dot_general(
        left, right, (((1,), (1,)), ((), ())), preferred_element_type=jnp.float32
    )


def nn_dot(left, right):
    return jnp.dot(left, right, preferred_element_type=jnp.float32)


def onehot(listed, base, rows):
    numbers = lax.broadcasted_iota(jnp.int32, (rows, listed.shape[1]), 0)
    return jnp.where(numbers == listed - base, 1.0, 0.0).astype(jnp.bfloat16)


def pick_kernel(rounds, turn, rows_ref, x_ref, *refs):
    outs = refs[: len(rounds)]
    if turn:
        xt_ref = refs[-1]
        for i in range(x_ref.shape[0] // TILE):
            xt_ref[:, i * TILE : (i + 1) * TILE] = x_ref[i * TILE : (i + 1) * TILE, :].T
    else:
        xt_ref = x_ref
    step = 2 * TILE
    for out_ref, r in zip(outs, rounds):
        for k in range(0, rows_ref.shape[1], step):
            table = onehot(rows_ref[r : r + 1, k : k + step], 0, xt_ref.shape[1])
            out_ref[:, k : k + step] = nn_dot(xt_ref[...], table).astype(jnp.bfloat16)


def pick_rows(rounds, send_rows, features, turn):
    rows, width = features.shape if turn else features.shape[::-1]
    boundary = send_rows.shape[1]
    outs = [jax.ShapeDtypeStruct((width, boundary), jnp.bfloat16) for _ in rounds]
    if turn:
        outs.append(jax.ShapeDtypeStruct((width, rows), jnp.bfloat16))
    return pl.pallas_call(
        functools.partial(pick_kernel, rounds, turn),
        out_shape=outs,
        in_specs=[vspec()] * 2,
        out_specs=[vspec()] * len(outs),
        compiler_params=params(),
        cost_estimate=cost(2 * rows * boundary * len(rounds) * width, 1_000_000),
    )(send_rows, features)


def densify_kernel(lc, hc, lt, ht, dl0, dl1, dh0, dh1, lslots, hslots, zeros, sems, zsems):
    half = lt.shape[0] // 2
    depth = lslots.shape[0]
    dense = (dl0, dl1, dh0, dh1)

    def fetch(i, slot):
        return [
            pltpu.make_async_copy(
                src.at[i + p * half], dst.at[slot, p], sems.at[slot, 2 * q + p]
            )
            for q, (src, dst) in enumerate(((lt, lslots), (ht, hslots)))
            for p in range(2)
        ]

    def clear(i, slot):
        rows = pl.ds(pl.multiple_of(i * TILE, TILE), TILE)
        return [
            pltpu.make_async_copy(
                zeros.at[pl.ds(0, d.shape[0])], d.at[:, rows, :], zsems.at[slot, k]
            )
            for k, d in enumerate(dense)
        ]

    for d in range(depth - 1):
        for copy in fetch(d, d):
            copy.start()
    zeros[...] = jnp.zeros_like(zeros)
    for copy in clear(0, 0):
        copy.start()

    def body(i, carry):
        slot, zslot = lax.rem(i, depth), lax.rem(i, 2)

        @pl.when(i + depth - 1 < half)
        def _():
            for copy in fetch(i + depth - 1, lax.rem(i + depth - 1, depth)):
                copy.start()

        @pl.when(i + 1 < half)
        def _():
            for copy in clear(i + 1, 1 - zslot):
                copy.start()

        for copy in clear(i, zslot):
            copy.wait()
        for copy in fetch(i, slot):
            copy.wait()
        rows = pl.ds(pl.multiple_of(i * TILE, TILE), TILE)
        for t in range(max(lt.shape[1], ht.shape[1])):
            jobs = []
            if t < lt.shape[1]:
                jobs += [(dl0, lc[i, t], lslots, 0), (dl1, lc[i + half, t], lslots, 1)]
            if t < ht.shape[1]:
                jobs += [(dh0, hc[i, t], hslots, 0), (dh1, hc[i + half, t], hslots, 1)]
            sums = [d[c, rows, :] + s[slot, p, t] for d, c, s, p in jobs]
            for (d, c, _, _), total in zip(jobs, sums):
                d[c, rows, :] = total
        return carry

    lax.fori_loop(0, half, body, 0)


def densify(local_cols, halo_cols, local_tiles, halo_tiles, halo_blocks):
    nblocks, local_count = local_cols.shape
    halo_count = halo_cols.shape[1]
    half = nblocks // 2 * TILE
    depth = 3
    slabs = (nblocks, nblocks, halo_blocks, halo_blocks)
    return pl.pallas_call(
        densify_kernel,
        out_shape=[VMEM((n, half, TILE), jnp.bfloat16) for n in slabs],
        in_specs=[sspec(), sspec()] + [pl.BlockSpec(memory_space=pltpu.HBM)] * 2,
        out_specs=[vspec()] * 4,
        scratch_shapes=[
            VMEM((depth, 2, local_count, TILE, TILE), jnp.bfloat16),
            VMEM((depth, 2, halo_count, TILE, TILE), jnp.bfloat16),
            VMEM((max(slabs), TILE, TILE), jnp.bfloat16),
            pltpu.SemaphoreType.DMA((depth, 4)),
            pltpu.SemaphoreType.DMA((2, 4)),
        ],
        compiler_params=params(34 * 1024 * 1024),
        cost_estimate=cost(16_000_000, nblocks * (local_count + halo_count) * TILE * TILE * 2),
    )(local_cols, halo_cols, local_tiles, halo_tiles)


def forward_kernel(first, n, has_acc, turned, d0_ref, d1_ref, x_ref, *refs):
    acc_ref, out_ref = refs if has_acc else (None, refs[0])
    right = x_ref[...].T if turned else x_ref[...]
    half, step = d0_ref.shape[1], 512
    for p, dense_ref in enumerate((d0_ref, d1_ref)):
        for j in range(0, half, step):
            left = jnp.concatenate(
                [dense_ref[first + c, j : j + step, :] for c in range(n)], axis=1
            )
            total = nn_dot(left, right)
            rows = slice(p * half + j, p * half + j + step)
            out_ref[rows, :] = total + acc_ref[rows, :] if has_acc else total


def forward(d0, d1, first, blocks, acc, turned):
    n = max(blocks.shape) // TILE
    rows = 2 * d0.shape[1]
    args = [pinned(d0), pinned(d1), blocks] + ([] if acc is None else [acc])
    return pl.pallas_call(
        functools.partial(forward_kernel, first, n, acc is not None, turned),
        out_shape=jax.ShapeDtypeStruct((rows, TILE), jnp.float32),
        in_specs=[vspec()] * len(args),
        out_specs=vspec(),
        compiler_params=params(),
        cost_estimate=cost(2 * rows * n * TILE * TILE, rows * TILE * 4),
    )(*args)


def middle_kernel(
    sum_ref, x_ref, ct_ref, deg_ref, ws_ref, wn_ref, bias_ref, out_ref, gp_ref, st_ref, wg_ref, both
):
    for i in range(sum_ref.shape[0] // TILE):
        rows = slice(i * TILE, (i + 1) * TILE)
        line = deg_ref[i : i + 1, :].astype(jnp.float32)
        column = jnp.broadcast_to(line, (TILE, TILE)).T
        agg = (sum_ref[rows, :] / column).astype(jnp.bfloat16)
        both[rows, :TILE] = x_ref[rows, :]
        both[rows, TILE:] = agg
        preact = nn_dot(x_ref[rows, :], ws_ref[...]) + nn_dot(agg, wn_ref[...]) + bias_ref[...]
        sig = jax.nn.sigmoid(preact)
        out_ref[rows, :] = (preact * sig).astype(jnp.bfloat16)
        grad = ct_ref[rows, :].astype(jnp.float32) * sig * (1.0 + preact * (1.0 - sig))
        grad = grad.astype(jnp.bfloat16)
        gp_ref[rows, :] = grad
        st_ref[:, rows] = (nt_dot(wn_ref[...], grad) / line).astype(jnp.bfloat16)
    wg_ref[...] = lax.dot_general(
        both[...], gp_ref[...], (((0,), (0,)), ((), ())), preferred_element_type=jnp.float32
    )


def middle(summed, features, cotangent, degree, w_self, w_neigh, bias):
    rows, width = features.shape
    half = jax.ShapeDtypeStruct((rows, width), jnp.bfloat16)
    return pl.pallas_call(
        middle_kernel,
        out_shape=[
            half,
            half,
            jax.ShapeDtypeStruct((width, rows), jnp.bfloat16),
            jax.ShapeDtypeStruct((2 * width, width), jnp.float32),
        ],
        in_specs=[vspec()] * 7,
        out_specs=[vspec()] * 4,
        scratch_shapes=[VMEM((rows, 2 * width), jnp.bfloat16)],
        compiler_params=params(),
        cost_estimate=cost(2 * rows * 5 * width * width, 5_000_000, rows * width),
    )(summed, features, cotangent, degree, w_self, w_neigh, bias)


def beside(d0_ref, d1_ref, slab):
    return jnp.concatenate(
        [jnp.concatenate([d[slab], d[slab + 1]], axis=1) for d in (d0_ref, d1_ref)], axis=0
    )


def back_kernel(first, n, st_ref, d0_ref, d1_ref, before_ref, out_ref):
    for c in range(0, n, 2):
        product = nn_dot(st_ref[...], beside(d0_ref, d1_ref, first + c))
        out_ref[:, c * TILE : (c + 2) * TILE] = product.astype(jnp.bfloat16)


def back(first, n, scaled_t, d0, d1, before):
    width, rows = scaled_t.shape
    return pl.pallas_call(
        functools.partial(back_kernel, first, n),
        out_shape=jax.ShapeDtypeStruct((width, n * TILE), jnp.bfloat16),
        in_specs=[vspec()] * 3 + [pl.BlockSpec(memory_space=pl.ANY)],
        out_specs=vspec(),
        compiler_params=params(),
        cost_estimate=cost(2 * rows * n * TILE * width, 500_000),
    )(scaled_t, pinned(d0), pinned(d1), before)


def own_kernel(st_ref, d0_ref, d1_ref, gp_ref, ws_ref, before_ref, out_ref):
    for c in range(0, d0_ref.shape[0], 2):
        rows = slice(c * TILE, (c + 2) * TILE)
        product = nn_dot(st_ref[...], beside(d0_ref, d1_ref, c))
        out_ref[:, rows] = product + nt_dot(ws_ref[...], gp_ref[rows, :])


def own(scaled_t, d0, d1, grad_pre, w_self, before):
    width, rows = scaled_t.shape
    return pl.pallas_call(
        own_kernel,
        out_shape=jax.ShapeDtypeStruct((width, rows), jnp.float32),
        in_specs=[vspec()] * 5 + [pl.BlockSpec(memory_space=pl.ANY)],
        out_specs=vspec(),
        compiler_params=params(),
        cost_estimate=cost(2 * rows * rows * width, 1_500_000),
    )(scaled_t, pinned(d0), pinned(d1), grad_pre, w_self, before)


def place_kernel(rounds, last, rows_ref, acc_ref, *refs):
    returned, out_ref = refs[:-1], refs[-1]
    step = 2 * TILE
    for j in range(0, acc_ref.shape[1], step):
        total = acc_ref[:, j : j + step]
        for got_ref, r in zip(returned, rounds):
            total = total + nt_dot(got_ref[...], onehot(rows_ref[r : r + 1, :], j, step))
        if last:
            out_ref[j : j + step, :] = total.T
        else:
            out_ref[:, j : j + step] = total


def place_rows(rounds, last, send_rows, acc, returned):
    width, rows = acc.shape
    return pl.pallas_call(
        functools.partial(place_kernel, rounds, last),
        out_shape=jax.ShapeDtypeStruct((rows, width) if last else (width, rows), jnp.float32),
        in_specs=[vspec()] * (2 + len(rounds)),
        out_specs=vspec(),
        compiler_params=params(),
        cost_estimate=cost(2 * rows * len(rounds) * send_rows.shape[1] * width, 2_000_000),
    )(send_rows, acc, *returned)


def swapped(shard, mask):
    return lax.ppermute(shard, "dom", [(i, i ^ mask) for i in range(lax.axis_size("dom"))])


def summed_everywhere(parts):
    core = lax.axis_index("dom") & 1
    halves = parts.reshape(2, -1, parts.shape[1])
    total = halves[core] + swapped(halves[1 - core], 1)
    mask = 2
    while mask < lax.axis_size("dom"):
        total = total + swapped(total, mask)
        mask *= 2
    other = swapped(total, 1)
    return jnp.where(core == 0, total, other), jnp.where(core == 0, other, total)


def local(
    node_features,
    w_self,
    w_neigh,
    output_bias,
    local_tiles,
    halo_tiles,
    local_cols,
    halo_cols,
    send_rows,
    degree,
    cotangent,
):
    row_count, width = node_features.shape
    nblocks = local_tiles.shape[0]
    round_count, boundary = send_rows.shape
    per = boundary // TILE
    received = {}
    *picked, features_t = pick_rows((2, 4), send_rows, node_features, True)
    picked += pick_rows((1, 3, 0), send_rows, features_t, False)
    for r, rows in zip((2, 4, 1, 3, 0), picked):
        received[r] = swapped(rows, 1 << r)
    dl0, dl1, dh0, dh1 = densify(
        local_cols, halo_cols, local_tiles, halo_tiles, round_count * per
    )
    summed = forward(dl0, dl1, 0, node_features, None, False)
    for r in (0, 3, 1, 4, 2):
        summed = forward(dh0, dh1, r * per, received[r], summed, True)
    output, grad_pre, scaled_t, parts = middle(
        summed,
        node_features,
        cotangent,
        degree.reshape(nblocks, TILE),
        w_self,
        w_neigh,
        output_bias.reshape(1, width),
    )
    returned = {}
    before = scaled_t
    for r in (2, 4, 1, 3, 0):
        before = back(r * per, per, scaled_t, dh0, dh1, before)
        returned[r] = swapped(before, 1 << r)
    grad_self, grad_neigh = summed_everywhere(parts)
    grad_scale = 1.0 / math.sqrt(row_count * lax.axis_size("dom"))
    grads_t = own(scaled_t, dl0, dl1, grad_pre, w_self, before)
    for rounds in ((0, 3), (1, 4, 2)):
        grads_t = place_rows(
            rounds, 2 in rounds, send_rows, grads_t, [returned[r] for r in rounds]
        )
    return (output, grads_t, grad_self * grad_scale, grad_neigh * grad_scale)


def solution(mesh):
    in_specs = (
        P("dom", None),
        P(),
        P(),
        P(),
        P("dom", None, None, None),
        P("dom", None, None, None),
        P("dom", None),
        P("dom", None),
        P("dom", None),
        P("dom"),
        P("dom", None),
    )
    out_specs = (P("dom", None), P("dom", None), P(), P())
    return jax.shard_map(local, mesh=mesh, in_specs=in_specs, out_specs=out_specs, check_vma=False)
```

```python
import functools
import math

import jax
import jax.numpy as jnp
from jax import lax
from jax.experimental import pallas as pl
from jax.experimental.pallas import tpu as pltpu
from jax.sharding import PartitionSpec as P

TILE = 128
VMEM = pltpu.VMEM
LIMIT = 8 * 1024 * 1024


def vspec():
    return pl.BlockSpec(memory_space=VMEM)


def sspec():
    return pl.BlockSpec(memory_space=pltpu.SMEM)


def params(limit=LIMIT):
    return pltpu.CompilerParams(vmem_limit_bytes=limit)


def in_hbm(array):
    return pltpu.with_memory_space_constraint(array, pltpu.HBM)


def cost(flops, size, transcendentals=0):
    return pl.CostEstimate(flops=flops, bytes_accessed=size, transcendentals=transcendentals)


def pinned(array):
    return pltpu.with_memory_space_constraint(array, VMEM)


def nt_dot(left, right):
    return lax.dot_general(
        left, right, (((1,), (1,)), ((), ())), preferred_element_type=jnp.float32
    )


def nn_dot(left, right):
    return jnp.dot(left, right, preferred_element_type=jnp.float32)


def pick_kernel(rows_hbm, x_hbm, *refs):
    rounds = (len(refs) - 5) // 2
    outs, tables = refs[:rounds], refs[rounds : 2 * rounds]
    rows_ref, x_ref, xt_ref, rows_sem, x_sem = refs[2 * rounds :]
    rows_copy = pltpu.make_async_copy(rows_hbm, rows_ref, rows_sem)
    x_copy = pltpu.make_async_copy(x_hbm, x_ref, x_sem)
    rows_copy.start()
    x_copy.start()
    rows_copy.wait()
    count, step = x_ref.shape[0], 2 * TILE
    numbers = lax.broadcasted_iota(jnp.int32, (count, step), 0)
    for r in range(rounds):
        for k in range(0, rows_ref.shape[1], step):
            listed = rows_ref[r : r + 1, k : k + step]
            table = jnp.where(numbers == listed, 1.0, 0.0).astype(jnp.bfloat16)
            tables[r][:, k : k + step] = table
            if r == 0 and k == 0:
                x_copy.wait()
                for i in range(0, count, TILE):
                    xt_ref[:, i : i + TILE] = x_ref[i : i + TILE, :].T
            outs[r][:, k : k + step] = nn_dot(xt_ref[...], table).astype(jnp.bfloat16)


def pick_rows(send_rows, features):
    rows, width = features.shape
    rounds, boundary = send_rows.shape
    outs = [jax.ShapeDtypeStruct((width, boundary), jnp.bfloat16) for _ in range(rounds)]
    outs += [VMEM((rows, boundary), jnp.bfloat16) for _ in range(rounds)]
    results = pl.pallas_call(
        pick_kernel,
        out_shape=outs,
        in_specs=[pl.BlockSpec(memory_space=pltpu.HBM)] * 2,
        out_specs=[vspec()] * len(outs),
        scratch_shapes=[
            VMEM(send_rows.shape, jnp.int32),
            VMEM(features.shape, jnp.bfloat16),
            VMEM((width, rows), jnp.bfloat16),
            pltpu.SemaphoreType.DMA,
            pltpu.SemaphoreType.DMA,
        ],
        compiler_params=params(),
        cost_estimate=cost(2 * rows * boundary * rounds * width, 1_000_000),
    )(in_hbm(send_rows), in_hbm(features))
    return results[:rounds], results[rounds:]


def densify_kernel(lc, hc, lt, ht, dl0, dl1, dh0, dh1, lslots, hslots, zeros, sems, zsems):
    half = lt.shape[0] // 2
    depth = lslots.shape[0]
    dense = (dl0, dl1, dh0, dh1)

    def fetch(i, slot):
        return [
            pltpu.make_async_copy(
                src.at[i + p * half], dst.at[slot, p], sems.at[slot, 2 * q + p]
            )
            for q, (src, dst) in enumerate(((lt, lslots), (ht, hslots)))
            for p in range(2)
        ]

    def clear(i, slot):
        rows = pl.ds(pl.multiple_of(i * TILE, TILE), TILE)
        return [
            pltpu.make_async_copy(
                zeros.at[pl.ds(0, d.shape[0])], d.at[:, rows, :], zsems.at[slot, k]
            )
            for k, d in enumerate(dense)
        ]

    for d in range(depth - 1):
        for copy in fetch(d, d):
            copy.start()
    zeros[...] = jnp.zeros_like(zeros)
    for copy in clear(0, 0):
        copy.start()

    def body(i, carry):
        slot, zslot = lax.rem(i, depth), lax.rem(i, 2)

        @pl.when(i + depth - 1 < half)
        def _():
            for copy in fetch(i + depth - 1, lax.rem(i + depth - 1, depth)):
                copy.start()

        @pl.when(i + 1 < half)
        def _():
            for copy in clear(i + 1, 1 - zslot):
                copy.start()

        for copy in clear(i, zslot):
            copy.wait()
        for copy in fetch(i, slot):
            copy.wait()
        rows = pl.ds(pl.multiple_of(i * TILE, TILE), TILE)
        for t in range(max(lt.shape[1], ht.shape[1])):
            jobs = []
            if t < lt.shape[1]:
                jobs += [(dl0, lc[i, t], lslots, 0), (dl1, lc[i + half, t], lslots, 1)]
            if t < ht.shape[1]:
                jobs += [(dh0, hc[i, t], hslots, 0), (dh1, hc[i + half, t], hslots, 1)]
            sums = [d[c, rows, :] + s[slot, p, t] for d, c, s, p in jobs]
            for (d, c, _, _), total in zip(jobs, sums):
                d[c, rows, :] = total
        return carry

    lax.fori_loop(0, half, body, 0)


def densify(local_cols, halo_cols, local_tiles, halo_tiles, halo_blocks):
    nblocks, local_count = local_cols.shape
    halo_count = halo_cols.shape[1]
    half = nblocks // 2 * TILE
    depth = 3
    slabs = (nblocks, nblocks, halo_blocks, halo_blocks)
    return pl.pallas_call(
        densify_kernel,
        out_shape=[VMEM((n, half, TILE), jnp.bfloat16) for n in slabs],
        in_specs=[sspec(), sspec()] + [pl.BlockSpec(memory_space=pltpu.HBM)] * 2,
        out_specs=[vspec()] * 4,
        scratch_shapes=[
            VMEM((depth, 2, local_count, TILE, TILE), jnp.bfloat16),
            VMEM((depth, 2, halo_count, TILE, TILE), jnp.bfloat16),
            VMEM((max(slabs), TILE, TILE), jnp.bfloat16),
            pltpu.SemaphoreType.DMA((depth, 4)),
            pltpu.SemaphoreType.DMA((2, 4)),
        ],
        compiler_params=params(12 * 1024 * 1024),
        cost_estimate=cost(16_000_000, nblocks * (local_count + halo_count) * TILE * TILE * 2),
    )(local_cols, halo_cols, in_hbm(local_tiles), in_hbm(halo_tiles))


def local_sums_kernel(d0_ref, d1_ref, x_ref, out_ref):
    half, step = d0_ref.shape[1], 512
    for p, dense_ref in enumerate((d0_ref, d1_ref)):
        for j in range(0, half, step):
            left = jnp.concatenate(
                [dense_ref[c, j : j + step, :] for c in range(dense_ref.shape[0])], axis=1
            )
            out_ref[p * half + j : p * half + j + step, :] = nn_dot(left, x_ref[...])


def local_sums(d0, d1, features):
    rows, width = features.shape
    return pl.pallas_call(
        local_sums_kernel,
        out_shape=VMEM((rows, width), jnp.float32),
        in_specs=[vspec()] * 3,
        out_specs=vspec(),
        compiler_params=params(),
        cost_estimate=cost(2 * rows * rows * width, 1_500_000),
    )(pinned(d0), pinned(d1), features)


def middle_kernel(rounds, *refs):
    got, refs = refs[:rounds], refs[rounds:]
    d0, d1, sum_ref, x_ref, ct_ref, deg_ref, ws_ref, wn_ref, bias_ref = refs[:9]
    out_ref, gp_ref, st_ref, mine_ref, give_ref, both, halo = refs[9:]
    core = lax.axis_index("dom") & 1
    half, step = d0.shape[1], 512
    boundary = got[0].shape[1]
    for r in range(rounds):
        halo[r * boundary : (r + 1) * boundary, :] = got[r][...].T
    for p, dense_ref in enumerate((d0, d1)):
        for j in range(0, half, step):
            left = jnp.concatenate(
                [dense_ref[c, j : j + step, :] for c in range(dense_ref.shape[0])], axis=1
            )
            start = p * half + j
            total = nn_dot(left, halo[...]) + sum_ref[start : start + step, :]
            for i in range(start // TILE, (start + step) // TILE):
                rows = slice(i * TILE, (i + 1) * TILE)
                line = deg_ref[i : i + 1, :].astype(jnp.float32)
                column = jnp.broadcast_to(line, (TILE, TILE)).T
                agg = total[i * TILE - start : (i + 1) * TILE - start, :] / column
                agg = agg.astype(jnp.bfloat16)
                both[rows, :TILE] = x_ref[rows, :]
                both[rows, TILE:] = agg
                preact = nn_dot(x_ref[rows, :], ws_ref[...]) + nn_dot(agg, wn_ref[...])
                preact = preact + bias_ref[...]
                sig = jax.nn.sigmoid(preact)
                out_ref[rows, :] = (preact * sig).astype(jnp.bfloat16)
                grad = ct_ref[rows, :].astype(jnp.float32) * sig * (1.0 + preact * (1.0 - sig))
                grad = grad.astype(jnp.bfloat16)
                gp_ref[rows, :] = grad
                st_ref[:, rows] = (nt_dot(wn_ref[...], grad) / line).astype(jnp.bfloat16)
    parts = lax.dot_general(
        both[...], gp_ref[...], (((0,), (0,)), ((), ())), preferred_element_type=jnp.float32
    )
    mine_ref[...] = jnp.where(core == 0, parts[:TILE], parts[TILE:])
    give_ref[...] = jnp.where(core == 0, parts[TILE:], parts[:TILE])


def middle(received, d0, d1, summed, features, cotangent, degree, w_self, w_neigh, bias):
    rows, width = features.shape
    rounds, boundary = len(received), received[0].shape[1]
    half = jax.ShapeDtypeStruct((rows, width), jnp.bfloat16)
    part = VMEM((width, width), jnp.float32)
    return pl.pallas_call(
        functools.partial(middle_kernel, rounds),
        out_shape=[
            half,
            VMEM((rows, width), jnp.bfloat16),
            VMEM((width, rows), jnp.bfloat16),
            part,
            part,
        ],
        in_specs=[vspec()] * (rounds + 9),
        out_specs=[vspec()] * 5,
        scratch_shapes=[
            VMEM((rows, 2 * width), jnp.bfloat16),
            VMEM((rounds * boundary, width), jnp.bfloat16),
        ],
        compiler_params=params(),
        cost_estimate=cost(2 * rows * rounds * boundary * width, 5_000_000, rows * width),
    )(
        *received,
        pinned(d0),
        pinned(d1),
        pinned(summed),
        features,
        cotangent,
        degree,
        w_self,
        w_neigh,
        bias,
    )


def beside(d0_ref, d1_ref, slab):
    return jnp.concatenate(
        [jnp.concatenate([d[slab], d[slab + 1]], axis=1) for d in (d0_ref, d1_ref)], axis=0
    )


def back_kernel(first, n, st_ref, d0_ref, d1_ref, before_ref, out_ref):
    for c in range(0, n, 2):
        product = nn_dot(st_ref[...], beside(d0_ref, d1_ref, first + c))
        out_ref[:, c * TILE : (c + 2) * TILE] = product.astype(jnp.bfloat16)


def back(first, n, scaled_t, d0, d1, before):
    width, rows = scaled_t.shape
    return pl.pallas_call(
        functools.partial(back_kernel, first, n),
        out_shape=jax.ShapeDtypeStruct((width, n * TILE), jnp.bfloat16),
        in_specs=[vspec()] * 3 + [pl.BlockSpec(memory_space=pl.ANY)],
        out_specs=vspec(),
        compiler_params=params(),
        cost_estimate=cost(2 * rows * n * TILE * width, 500_000),
    )(pinned(scaled_t), pinned(d0), pinned(d1), before)


def own_kernel(st_ref, d0_ref, d1_ref, gp_ref, ws_ref, before_ref, out_ref):
    for c in range(0, d0_ref.shape[0], 2):
        rows = slice(c * TILE, (c + 2) * TILE)
        product = nn_dot(st_ref[...], beside(d0_ref, d1_ref, c))
        out_ref[:, rows] = product + nt_dot(ws_ref[...], gp_ref[rows, :])


def own(scaled_t, d0, d1, grad_pre, w_self, before):
    width, rows = scaled_t.shape
    return pl.pallas_call(
        own_kernel,
        out_shape=VMEM((width, rows), jnp.float32),
        in_specs=[vspec()] * 5 + [pl.BlockSpec(memory_space=pl.ANY)],
        out_specs=vspec(),
        compiler_params=params(),
        cost_estimate=cost(2 * rows * rows * width, 1_500_000),
    )(pinned(scaled_t), pinned(d0), pinned(d1), pinned(grad_pre), w_self, before)


def place_kernel(count, last, acc_ref, *refs):
    returned, tables, out_ref = refs[:count], refs[count : 2 * count], refs[-1]
    step = 2 * TILE
    for j in range(0, acc_ref.shape[1], step):
        total = acc_ref[:, j : j + step]
        for got_ref, table_ref in zip(returned, tables):
            total = total + nt_dot(got_ref[...], table_ref[j : j + step, :])
        if last:
            out_ref[j : j + step, :] = total.T
        else:
            out_ref[:, j : j + step] = total


def place_rows(last, acc, returned, tables):
    width, rows = acc.shape
    count, boundary = len(returned), tables[0].shape[1]
    if last:
        out = jax.ShapeDtypeStruct((rows, width), jnp.float32)
    else:
        out = VMEM((width, rows), jnp.float32)
    return pl.pallas_call(
        functools.partial(place_kernel, count, last),
        out_shape=out,
        in_specs=[vspec()] * (1 + 2 * count),
        out_specs=vspec(),
        compiler_params=params(),
        cost_estimate=cost(2 * rows * count * boundary * width, 2_000_000),
    )(pinned(acc), *returned, *[pinned(t) for t in tables])


def add_kernel(left_ref, right_ref, out_ref):
    out_ref[...] = left_ref[...] + right_ref[...]


def added(left, right):
    return pl.pallas_call(
        add_kernel,
        out_shape=VMEM(left.shape, jnp.float32),
        in_specs=[vspec()] * 2,
        out_specs=vspec(),
        compiler_params=params(1024 * 1024),
        cost_estimate=cost(left.size, 3 * left.size * 4),
    )(pinned(left), right)


def halves_kernel(scale, total_ref, other_ref, self_ref, neigh_ref):
    core = lax.axis_index("dom") & 1
    total, other = total_ref[...], other_ref[...]
    self_ref[...] = jnp.where(core == 0, total, other) * scale
    neigh_ref[...] = jnp.where(core == 0, other, total) * scale


def halves(scale, total, other):
    out = jax.ShapeDtypeStruct(total.shape, jnp.float32)
    return pl.pallas_call(
        functools.partial(halves_kernel, scale),
        out_shape=[out, out],
        in_specs=[vspec()] * 2,
        out_specs=[vspec()] * 2,
        compiler_params=params(1024 * 1024),
        cost_estimate=cost(2 * total.size, 4 * total.size * 4),
    )(pinned(total), other)


def swapped(shard, mask):
    return lax.ppermute(shard, "dom", [(i, i ^ mask) for i in range(lax.axis_size("dom"))])


def summed_everywhere(mine, give, scale):
    total = added(mine, swapped(give, 1))
    mask = 2
    while mask < lax.axis_size("dom"):
        total = added(total, swapped(total, mask))
        mask *= 2
    return halves(scale, total, swapped(total, 1))


def local(
    node_features,
    w_self,
    w_neigh,
    output_bias,
    local_tiles,
    halo_tiles,
    local_cols,
    halo_cols,
    send_rows,
    degree,
    cotangent,
):
    row_count, width = node_features.shape
    nblocks = local_tiles.shape[0]
    round_count, boundary = send_rows.shape
    per = boundary // TILE
    picked, tables = pick_rows(send_rows, node_features)
    received = [swapped(rows, 1 << r) for r, rows in enumerate(picked)]
    dl0, dl1, dh0, dh1 = densify(
        local_cols, halo_cols, local_tiles, halo_tiles, round_count * per
    )
    summed = local_sums(dl0, dl1, node_features)
    output, grad_pre, scaled_t, mine, give = middle(
        received,
        dh0,
        dh1,
        summed,
        node_features,
        cotangent,
        degree.reshape(nblocks, TILE),
        w_self,
        w_neigh,
        output_bias.reshape(1, width),
    )
    returned = {}
    before = scaled_t
    for r in (2, 4, 1, 3, 0):
        before = back(r * per, per, scaled_t, dh0, dh1, before)
        returned[r] = swapped(before, 1 << r)
    grad_scale = 1.0 / math.sqrt(row_count * lax.axis_size("dom"))
    grad_self, grad_neigh = summed_everywhere(mine, give, grad_scale)
    grads_t = own(scaled_t, dl0, dl1, grad_pre, w_self, before)
    for rounds in ((0, 3), (1, 4, 2)):
        grads_t = place_rows(
            2 in rounds, grads_t, [returned[r] for r in rounds], [tables[r] for r in rounds]
        )
    return (output, grads_t, grad_self, grad_neigh)


def solution(mesh):
    in_specs = (
        P("dom", None),
        P(),
        P(),
        P(),
        P("dom", None, None, None),
        P("dom", None, None, None),
        P("dom", None),
        P("dom", None),
        P("dom", None),
        P("dom"),
        P("dom", None),
    )
    out_specs = (P("dom", None), P("dom", None), P(), P())
    return jax.shard_map(local, mesh=mesh, in_specs=in_specs, out_specs=out_specs, check_vma=False)
```

```python
import functools
import math

import jax
import jax.numpy as jnp
from jax import lax
from jax.experimental import pallas as pl
from jax.experimental.pallas import tpu as pltpu
from jax.sharding import PartitionSpec as P

TILE = 128
VMEM = pltpu.VMEM
LIMIT = 8 * 1024 * 1024


def vspec():
    return pl.BlockSpec(memory_space=VMEM)


def sspec():
    return pl.BlockSpec(memory_space=pltpu.SMEM)


def params(limit=LIMIT):
    return pltpu.CompilerParams(vmem_limit_bytes=limit)


def in_hbm(array):
    return pltpu.with_memory_space_constraint(array, pltpu.HBM)


def cost(flops, size, transcendentals=0):
    return pl.CostEstimate(flops=flops, bytes_accessed=size, transcendentals=transcendentals)


def pinned(array):
    return pltpu.with_memory_space_constraint(array, VMEM)


def nt_dot(left, right):
    return lax.dot_general(
        left, right, (((1,), (1,)), ((), ())), preferred_element_type=jnp.float32
    )


def nn_dot(left, right):
    return jnp.dot(left, right, preferred_element_type=jnp.float32)


def pick_kernel(rows_hbm, x_hbm, *refs):
    outs, (rows_ref, x_ref, xt_ref, rows_sem, x_sem) = refs[:-5], refs[-5:]
    rounds = len(outs)
    rows_copy = pltpu.make_async_copy(rows_hbm, rows_ref, rows_sem)
    x_copy = pltpu.make_async_copy(x_hbm, x_ref, x_sem)
    rows_copy.start()
    x_copy.start()
    rows_copy.wait()
    count, step = x_ref.shape[0], 2 * TILE
    numbers = lax.broadcasted_iota(jnp.int32, (count, step), 0)
    for r in range(rounds):
        for k in range(0, rows_ref.shape[1], step):
            listed = rows_ref[r : r + 1, k : k + step]
            table = jnp.where(numbers == listed, 1.0, 0.0).astype(jnp.bfloat16)
            if r == 0 and k == 0:
                x_copy.wait()
                for i in range(0, count, TILE):
                    xt_ref[:, i : i + TILE] = x_ref[i : i + TILE, :].T
            outs[r][:, k : k + step] = nn_dot(xt_ref[...], table).astype(jnp.bfloat16)


def pick_rows(send_rows, features):
    rows, width = features.shape
    rounds, boundary = send_rows.shape
    outs = [jax.ShapeDtypeStruct((width, boundary), jnp.bfloat16) for _ in range(rounds)]
    return pl.pallas_call(
        pick_kernel,
        out_shape=outs,
        in_specs=[pl.BlockSpec(memory_space=pltpu.HBM)] * 2,
        out_specs=[vspec()] * len(outs),
        scratch_shapes=[
            VMEM(send_rows.shape, jnp.int32),
            VMEM(features.shape, jnp.bfloat16),
            VMEM((width, rows), jnp.bfloat16),
            pltpu.SemaphoreType.DMA,
            pltpu.SemaphoreType.DMA,
        ],
        compiler_params=params(),
        cost_estimate=cost(2 * rows * boundary * rounds * width, 1_000_000),
    )(in_hbm(send_rows), in_hbm(features))


def densify_kernel(lc, hc, lt, ht, dl0, dl1, dh0, dh1, lslots, hslots, zeros, sems, zsems):
    half = lt.shape[0] // 2
    depth = lslots.shape[0]
    dense = (dl0, dl1, dh0, dh1)

    def fetch(i, slot):
        return [
            pltpu.make_async_copy(
                src.at[i + p * half], dst.at[slot, p], sems.at[slot, 2 * q + p]
            )
            for q, (src, dst) in enumerate(((lt, lslots), (ht, hslots)))
            for p in range(2)
        ]

    def clear(i, slot):
        rows = pl.ds(pl.multiple_of(i * TILE, TILE), TILE)
        return [
            pltpu.make_async_copy(
                zeros.at[pl.ds(0, d.shape[0])], d.at[:, rows, :], zsems.at[slot, k]
            )
            for k, d in enumerate(dense)
        ]

    for d in range(depth - 1):
        for copy in fetch(d, d):
            copy.start()
    zeros[...] = jnp.zeros_like(zeros)
    for copy in clear(0, 0):
        copy.start()

    def body(i, carry):
        slot, zslot = lax.rem(i, depth), lax.rem(i, 2)

        @pl.when(i + depth - 1 < half)
        def _():
            for copy in fetch(i + depth - 1, lax.rem(i + depth - 1, depth)):
                copy.start()

        @pl.when(i + 1 < half)
        def _():
            for copy in clear(i + 1, 1 - zslot):
                copy.start()

        for copy in clear(i, zslot):
            copy.wait()
        for copy in fetch(i, slot):
            copy.wait()
        rows = pl.ds(pl.multiple_of(i * TILE, TILE), TILE)
        for t in range(max(lt.shape[1], ht.shape[1])):
            jobs = []
            if t < lt.shape[1]:
                jobs += [(dl0, lc[i, t], lslots, 0), (dl1, lc[i + half, t], lslots, 1)]
            if t < ht.shape[1]:
                jobs += [(dh0, hc[i, t], hslots, 0), (dh1, hc[i + half, t], hslots, 1)]
            sums = [d[c, rows, :] + s[slot, p, t] for d, c, s, p in jobs]
            for (d, c, _, _), total in zip(jobs, sums):
                d[c, rows, :] = total
        return carry

    lax.fori_loop(0, half, body, 0)


def densify(local_cols, halo_cols, local_tiles, halo_tiles, halo_blocks):
    nblocks, local_count = local_cols.shape
    halo_count = halo_cols.shape[1]
    half = nblocks // 2 * TILE
    depth = 3
    slabs = (nblocks, nblocks, halo_blocks, halo_blocks)
    return pl.pallas_call(
        densify_kernel,
        out_shape=[VMEM((n, half, TILE), jnp.bfloat16) for n in slabs],
        in_specs=[sspec(), sspec()] + [pl.BlockSpec(memory_space=pltpu.HBM)] * 2,
        out_specs=[vspec()] * 4,
        scratch_shapes=[
            VMEM((depth, 2, local_count, TILE, TILE), jnp.bfloat16),
            VMEM((depth, 2, halo_count, TILE, TILE), jnp.bfloat16),
            VMEM((max(slabs), TILE, TILE), jnp.bfloat16),
            pltpu.SemaphoreType.DMA((depth, 4)),
            pltpu.SemaphoreType.DMA((2, 4)),
        ],
        compiler_params=params(12 * 1024 * 1024),
        cost_estimate=cost(16_000_000, nblocks * (local_count + halo_count) * TILE * TILE * 2),
    )(local_cols, halo_cols, in_hbm(local_tiles), in_hbm(halo_tiles))


def local_sums_kernel(d0_ref, d1_ref, x_ref, out_ref):
    half, step = d0_ref.shape[1], 512
    for p, dense_ref in enumerate((d0_ref, d1_ref)):
        for j in range(0, half, step):
            left = jnp.concatenate(
                [dense_ref[c, j : j + step, :] for c in range(dense_ref.shape[0])], axis=1
            )
            out_ref[p * half + j : p * half + j + step, :] = nn_dot(left, x_ref[...])


def local_sums(d0, d1, features):
    rows, width = features.shape
    return pl.pallas_call(
        local_sums_kernel,
        out_shape=VMEM((rows, width), jnp.float32),
        in_specs=[vspec()] * 3,
        out_specs=vspec(),
        compiler_params=params(),
        cost_estimate=cost(2 * rows * rows * width, 1_500_000),
    )(pinned(d0), pinned(d1), features)


def middle_kernel(rounds, *refs):
    got, refs = refs[:rounds], refs[rounds:]
    d0, d1, sum_ref, x_ref, ct_ref, deg_ref, ws_ref, wn_ref, bias_ref = refs[:9]
    out_ref, gp_ref, st_ref, mine_ref, give_ref, both, halo, sums = refs[9:]
    core = lax.axis_index("dom") & 1
    half, step = d0.shape[1], 512
    boundary = got[0].shape[1]
    per = boundary // TILE
    for r in range(rounds):
        halo[r * boundary : (r + 1) * boundary, :] = got[r][...].T
    for p, dense_ref in enumerate((d0, d1)):
        for j in range(0, half, step):
            start = p * half + j
            total = sum_ref[start : start + step, :]
            for r in range(rounds):
                left = jnp.concatenate(
                    [dense_ref[c, j : j + step, :] for c in range(r * per, (r + 1) * per)], axis=1
                )
                total = total + nn_dot(left, halo[r * boundary : (r + 1) * boundary, :])
            sums[start : start + step, :] = total
    for start in range(0, 2 * half, step):
        total = sums[start : start + step, :]
        for i in range(start // TILE, (start + step) // TILE):
            rows = slice(i * TILE, (i + 1) * TILE)
            line = deg_ref[i : i + 1, :].astype(jnp.float32)
            column = jnp.broadcast_to(line, (TILE, TILE)).T
            agg = total[i * TILE - start : (i + 1) * TILE - start, :] / column
            agg = agg.astype(jnp.bfloat16)
            both[rows, :TILE] = x_ref[rows, :]
            both[rows, TILE:] = agg
            preact = nn_dot(x_ref[rows, :], ws_ref[...]) + nn_dot(agg, wn_ref[...])
            preact = preact + bias_ref[...]
            sig = jax.nn.sigmoid(preact)
            out_ref[rows, :] = (preact * sig).astype(jnp.bfloat16)
            grad = ct_ref[rows, :].astype(jnp.float32) * sig * (1.0 + preact * (1.0 - sig))
            grad = grad.astype(jnp.bfloat16)
            gp_ref[rows, :] = grad
            st_ref[:, rows] = (nt_dot(wn_ref[...], grad) / line).astype(jnp.bfloat16)
    parts = lax.dot_general(
        both[...], gp_ref[...], (((0,), (0,)), ((), ())), preferred_element_type=jnp.float32
    )
    mine_ref[...] = jnp.where(core == 0, parts[:TILE], parts[TILE:])
    give_ref[...] = jnp.where(core == 0, parts[TILE:], parts[:TILE])


def middle(received, d0, d1, summed, features, cotangent, degree, w_self, w_neigh, bias):
    rows, width = features.shape
    rounds, boundary = len(received), received[0].shape[1]
    half = jax.ShapeDtypeStruct((rows, width), jnp.bfloat16)
    part = VMEM((width, width), jnp.float32)
    return pl.pallas_call(
        functools.partial(middle_kernel, rounds),
        out_shape=[
            half,
            VMEM((rows, width), jnp.bfloat16),
            VMEM((width, rows), jnp.bfloat16),
            part,
            part,
        ],
        in_specs=[vspec()] * (rounds + 9),
        out_specs=[vspec()] * 5,
        scratch_shapes=[
            VMEM((rows, 2 * width), jnp.bfloat16),
            VMEM((rounds * boundary, width), jnp.bfloat16),
            VMEM((rows, width), jnp.float32),
        ],
        compiler_params=params(),
        cost_estimate=cost(2 * rows * rounds * boundary * width, 5_000_000, rows * width),
    )(
        *received,
        pinned(d0),
        pinned(d1),
        pinned(summed),
        features,
        cotangent,
        degree,
        w_self,
        w_neigh,
        bias,
    )


def beside(d0_ref, d1_ref, slab):
    return jnp.concatenate(
        [jnp.concatenate([d[slab], d[slab + 1]], axis=1) for d in (d0_ref, d1_ref)], axis=0
    )


def back_kernel(first, n, st_ref, d0_ref, d1_ref, before_ref, out_ref):
    for c in range(0, n, 2):
        product = nn_dot(st_ref[...], beside(d0_ref, d1_ref, first + c))
        out_ref[:, c * TILE : (c + 2) * TILE] = product.astype(jnp.bfloat16)


def back(first, n, scaled_t, d0, d1, before):
    width, rows = scaled_t.shape
    return pl.pallas_call(
        functools.partial(back_kernel, first, n),
        out_shape=jax.ShapeDtypeStruct((width, n * TILE), jnp.bfloat16),
        in_specs=[vspec()] * 3 + [pl.BlockSpec(memory_space=pl.ANY)],
        out_specs=vspec(),
        compiler_params=params(),
        cost_estimate=cost(1, 1),
    )(pinned(scaled_t), pinned(d0), pinned(d1), before)


def own_kernel(st_ref, d0_ref, d1_ref, gp_ref, ws_ref, before_ref, out_ref):
    for c in range(0, d0_ref.shape[0], 2):
        rows = slice(c * TILE, (c + 2) * TILE)
        product = nn_dot(st_ref[...], beside(d0_ref, d1_ref, c))
        out_ref[:, rows] = product + nt_dot(ws_ref[...], gp_ref[rows, :])


def own(scaled_t, d0, d1, grad_pre, w_self, before):
    width, rows = scaled_t.shape
    return pl.pallas_call(
        own_kernel,
        out_shape=VMEM((width, rows), jnp.float32),
        in_specs=[vspec()] * 5 + [pl.BlockSpec(memory_space=pl.ANY)],
        out_specs=vspec(),
        compiler_params=params(),
        cost_estimate=cost(1, 1),
    )(pinned(scaled_t), pinned(d0), pinned(d1), pinned(grad_pre), w_self, before)


def place_kernel(rounds, last, rows_ref, acc_ref, before_ref, *refs):
    returned, (out_ref, listed) = refs[: len(rounds)], refs[len(rounds) :]
    step, boundary = 2 * TILE, rows_ref.shape[1]
    for place, r in enumerate(rounds):
        for k in range(0, boundary, TILE):
            line = rows_ref[r : r + 1, k : k + TILE].astype(jnp.float32)
            listed[place, k : k + TILE, :] = jnp.broadcast_to(line, (TILE, TILE)).T
    numbers = lax.broadcasted_iota(jnp.int32, (boundary, TILE), 1).astype(jnp.float32)
    for j in range(0, acc_ref.shape[1], step):
        total = acc_ref[:, j : j + step]
        for place, got_ref in enumerate(returned):
            table = jnp.concatenate(
                [
                    jnp.where(listed[place] == numbers + float(n), 1.0, 0.0).astype(jnp.bfloat16)
                    for n in range(j, j + step, TILE)
                ],
                axis=1,
            )
            total = total + nn_dot(got_ref[...], table)
        if last:
            out_ref[j : j + step, :] = total.T
        else:
            out_ref[:, j : j + step] = total


def place_rows(rounds, last, send_rows, acc, returned, before):
    width, rows = acc.shape
    count, boundary = len(rounds), send_rows.shape[1]
    if last:
        out = jax.ShapeDtypeStruct((rows, width), jnp.float32)
    else:
        out = VMEM((width, rows), jnp.float32)
    return pl.pallas_call(
        functools.partial(place_kernel, rounds, last),
        out_shape=out,
        in_specs=[vspec()] * 2 + [pl.BlockSpec(memory_space=pl.ANY)] + [vspec()] * count,
        out_specs=vspec(),
        scratch_shapes=[VMEM((count, boundary, TILE), jnp.float32)],
        compiler_params=params(),
        cost_estimate=cost(1, 1),
    )(send_rows, pinned(acc), before, *returned)


def add_kernel(left_ref, right_ref, before_ref, out_ref):
    out_ref[...] = left_ref[...] + right_ref[...]


def added(left, right, before):
    return pl.pallas_call(
        add_kernel,
        out_shape=VMEM(left.shape, jnp.float32),
        in_specs=[vspec()] * 2 + [pl.BlockSpec(memory_space=pl.ANY)],
        out_specs=vspec(),
        compiler_params=params(1024 * 1024),
        cost_estimate=cost(1, 1),
    )(pinned(left), right, before)


def halves_kernel(scale, total_ref, other_ref, self_ref, neigh_ref):
    core = lax.axis_index("dom") & 1
    total, other = total_ref[...], other_ref[...]
    self_ref[...] = jnp.where(core == 0, total, other) * scale
    neigh_ref[...] = jnp.where(core == 0, other, total) * scale


def halves(scale, total, other):
    out = jax.ShapeDtypeStruct(total.shape, jnp.float32)
    return pl.pallas_call(
        functools.partial(halves_kernel, scale),
        out_shape=[out, out],
        in_specs=[vspec()] * 2,
        out_specs=[vspec()] * 2,
        compiler_params=params(1024 * 1024),
        cost_estimate=cost(2 * total.size, 4 * total.size * 4),
    )(pinned(total), other)


def swapped(shard, mask):
    return lax.ppermute(shard, "dom", [(i, i ^ mask) for i in range(lax.axis_size("dom"))])


def local(
    node_features,
    w_self,
    w_neigh,
    output_bias,
    local_tiles,
    halo_tiles,
    local_cols,
    halo_cols,
    send_rows,
    degree,
    cotangent,
):
    row_count, width = node_features.shape
    nblocks = local_tiles.shape[0]
    round_count, boundary = send_rows.shape
    per = boundary // TILE
    picked = pick_rows(send_rows, node_features)
    received = [swapped(rows, 1 << r) for r, rows in enumerate(picked)]
    dl0, dl1, dh0, dh1 = densify(
        local_cols, halo_cols, local_tiles, halo_tiles, round_count * per
    )
    summed = local_sums(dl0, dl1, node_features)
    output, grad_pre, scaled_t, mine, give = middle(
        received,
        dh0,
        dh1,
        summed,
        node_features,
        cotangent,
        degree.reshape(nblocks, TILE),
        w_self,
        w_neigh,
        output_bias.reshape(1, width),
    )
    returned = {}

    def send_back(r, before):
        grads = back(r * per, per, scaled_t, dh0, dh1, before)
        returned[r] = swapped(grads, 1 << r)
        return grads

    def place(rounds, acc, before):
        got = [returned[r] for r in rounds]
        return place_rows(rounds, 2 in rounds, send_rows, acc, got, before)

    other = swapped(give, 1)
    last = send_back(2, scaled_t)
    total = added(mine, other, last)
    other = swapped(total, 32)
    last = send_back(4, total)
    last = send_back(1, last)
    total = added(total, other, last)
    other = swapped(total, 64)
    last = send_back(3, total)
    last = send_back(0, last)
    total = added(total, other, last)
    other = swapped(total, 8)
    grads_t = own(scaled_t, dl0, dl1, grad_pre, w_self, total)
    total = added(total, other, grads_t)
    other = swapped(total, 16)
    grads_t = place((0, 3), grads_t, total)
    total = added(total, other, grads_t)
    other = swapped(total, 2)
    grads_t = place((1,), grads_t, total)
    total = added(total, other, grads_t)
    other = swapped(total, 4)
    grads_t = place((4,), grads_t, total)
    total = added(total, other, grads_t)
    other = swapped(total, 1)
    grads_t = place((2,), grads_t, total)
    grad_scale = 1.0 / math.sqrt(row_count * lax.axis_size("dom"))
    grad_self, grad_neigh = halves(grad_scale, total, other)
    return (output, grads_t, grad_self, grad_neigh)


def solution(mesh):
    in_specs = (
        P("dom", None),
        P(),
        P(),
        P(),
        P("dom", None, None, None),
        P("dom", None, None, None),
        P("dom", None),
        P("dom", None),
        P("dom", None),
        P("dom"),
        P("dom", None),
    )
    out_specs = (P("dom", None), P("dom", None), P(), P())
    return jax.shard_map(local, mesh=mesh, in_specs=in_specs, out_specs=out_specs, check_vma=False)
```

```python
import functools
import math

import jax
import jax.numpy as jnp
from jax import lax
from jax.experimental import pallas as pl
from jax.experimental.pallas import tpu as pltpu
from jax.sharding import PartitionSpec as P

TILE = 128
VMEM = pltpu.VMEM
LIMIT = 8 * 1024 * 1024


def vspec():
    return pl.BlockSpec(memory_space=VMEM)


def sspec():
    return pl.BlockSpec(memory_space=pltpu.SMEM)


def params(limit=LIMIT):
    return pltpu.CompilerParams(vmem_limit_bytes=limit)


def in_hbm(array):
    return pltpu.with_memory_space_constraint(array, pltpu.HBM)


def cost(flops, size, transcendentals=0):
    return pl.CostEstimate(flops=flops, bytes_accessed=size, transcendentals=transcendentals)


def pinned(array):
    return pltpu.with_memory_space_constraint(array, VMEM)


def nt_dot(left, right):
    return lax.dot_general(
        left, right, (((1,), (1,)), ((), ())), preferred_element_type=jnp.float32
    )


def nn_dot(left, right):
    return jnp.dot(left, right, preferred_element_type=jnp.float32)


def pick_kernel(rows_hbm, x_hbm, *refs):
    outs, (rows_ref, x_ref, xt_ref, rows_sem, x_sem) = refs[:-5], refs[-5:]
    rounds = len(outs)
    rows_copy = pltpu.make_async_copy(rows_hbm, rows_ref, rows_sem)
    x_copy = pltpu.make_async_copy(x_hbm, x_ref, x_sem)
    rows_copy.start()
    x_copy.start()
    rows_copy.wait()
    count, step = x_ref.shape[0], 2 * TILE
    numbers = lax.broadcasted_iota(jnp.int32, (count, step), 0)
    for r in range(rounds):
        for k in range(0, rows_ref.shape[1], step):
            listed = rows_ref[r : r + 1, k : k + step]
            table = jnp.where(numbers == listed, 1.0, 0.0).astype(jnp.bfloat16)
            if r == 0 and k == 0:
                x_copy.wait()
                for i in range(0, count, TILE):
                    xt_ref[:, i : i + TILE] = x_ref[i : i + TILE, :].T
            outs[r][:, k : k + step] = nn_dot(xt_ref[...], table).astype(jnp.bfloat16)


def pick_rows(send_rows, features):
    rows, width = features.shape
    rounds, boundary = send_rows.shape
    outs = [jax.ShapeDtypeStruct((width, boundary), jnp.bfloat16) for _ in range(rounds)]
    return pl.pallas_call(
        pick_kernel,
        out_shape=outs,
        in_specs=[pl.BlockSpec(memory_space=pltpu.HBM)] * 2,
        out_specs=[vspec()] * len(outs),
        scratch_shapes=[
            VMEM(send_rows.shape, jnp.int32),
            VMEM(features.shape, jnp.bfloat16),
            VMEM((width, rows), jnp.bfloat16),
            pltpu.SemaphoreType.DMA,
            pltpu.SemaphoreType.DMA,
        ],
        compiler_params=params(),
        cost_estimate=cost(2 * rows * boundary * rounds * width, 1_000_000),
    )(in_hbm(send_rows), in_hbm(features))


def densify_kernel(
    lc_hbm, hc_hbm, lt, ht, dl0, dl1, dh0, dh1, lslots, hslots, zeros, lc, hc, sems, zsems, csems
):
    half = lt.shape[0] // 2
    depth = lslots.shape[0]
    dense = (dl0, dl1, dh0, dh1)

    def fetch(i, slot):
        return [
            pltpu.make_async_copy(
                src.at[i + p * half], dst.at[slot, p], sems.at[slot, 2 * q + p]
            )
            for q, (src, dst) in enumerate(((lt, lslots), (ht, hslots)))
            for p in range(2)
        ]

    def clear(i, slot):
        rows = pl.ds(pl.multiple_of(i * TILE, TILE), TILE)
        return [
            pltpu.make_async_copy(
                zeros.at[pl.ds(0, d.shape[0])], d.at[:, rows, :], zsems.at[slot, k]
            )
            for k, d in enumerate(dense)
        ]

    for d in range(depth - 1):
        for copy in fetch(d, d):
            copy.start()
    columns = [
        pltpu.make_async_copy(lc_hbm, lc, csems.at[0]),
        pltpu.make_async_copy(hc_hbm, hc, csems.at[1]),
    ]
    for copy in columns:
        copy.start()
    zeros[...] = jnp.zeros_like(zeros)
    for copy in clear(0, 0):
        copy.start()
    for copy in columns:
        copy.wait()

    def body(i, carry):
        slot, zslot = lax.rem(i, depth), lax.rem(i, 2)

        @pl.when(i + depth - 1 < half)
        def _():
            for copy in fetch(i + depth - 1, lax.rem(i + depth - 1, depth)):
                copy.start()

        @pl.when(i + 1 < half)
        def _():
            for copy in clear(i + 1, 1 - zslot):
                copy.start()

        for copy in clear(i, zslot):
            copy.wait()
        for copy in fetch(i, slot):
            copy.wait()
        rows = pl.ds(pl.multiple_of(i * TILE, TILE), TILE)
        for t in range(max(lt.shape[1], ht.shape[1])):
            jobs = []
            if t < lt.shape[1]:
                jobs += [(dl0, lc[i, t], lslots, 0), (dl1, lc[i + half, t], lslots, 1)]
            if t < ht.shape[1]:
                jobs += [(dh0, hc[i, t], hslots, 0), (dh1, hc[i + half, t], hslots, 1)]
            sums = [d[c, rows, :] + s[slot, p, t] for d, c, s, p in jobs]
            for (d, c, _, _), total in zip(jobs, sums):
                d[c, rows, :] = total
        return carry

    lax.fori_loop(0, half, body, 0)


def densify(local_cols, halo_cols, local_tiles, halo_tiles, halo_blocks):
    nblocks, local_count = local_cols.shape
    halo_count = halo_cols.shape[1]
    half = nblocks // 2 * TILE
    depth = 3
    slabs = (nblocks, nblocks, halo_blocks, halo_blocks)
    return pl.pallas_call(
        densify_kernel,
        out_shape=[VMEM((n, half, TILE), jnp.bfloat16) for n in slabs],
        in_specs=[pl.BlockSpec(memory_space=pltpu.HBM)] * 4,
        out_specs=[vspec()] * 4,
        scratch_shapes=[
            VMEM((depth, 2, local_count, TILE, TILE), jnp.bfloat16),
            VMEM((depth, 2, halo_count, TILE, TILE), jnp.bfloat16),
            VMEM((max(slabs), TILE, TILE), jnp.bfloat16),
            pltpu.SMEM(local_cols.shape, jnp.int32),
            pltpu.SMEM(halo_cols.shape, jnp.int32),
            pltpu.SemaphoreType.DMA((depth, 4)),
            pltpu.SemaphoreType.DMA((2, 4)),
            pltpu.SemaphoreType.DMA((2,)),
        ],
        compiler_params=params(12 * 1024 * 1024),
        cost_estimate=cost(16_000_000, nblocks * (local_count + halo_count) * TILE * TILE * 2),
    )(in_hbm(local_cols), in_hbm(halo_cols), in_hbm(local_tiles), in_hbm(halo_tiles))


def local_sums_kernel(d0_ref, d1_ref, x_ref, out_ref):
    half, step = d0_ref.shape[1], 512
    for p, dense_ref in enumerate((d0_ref, d1_ref)):
        for j in range(0, half, step):
            left = jnp.concatenate(
                [dense_ref[c, j : j + step, :] for c in range(dense_ref.shape[0])], axis=1
            )
            out_ref[p * half + j : p * half + j + step, :] = nn_dot(left, x_ref[...])


def local_sums(d0, d1, features):
    rows, width = features.shape
    return pl.pallas_call(
        local_sums_kernel,
        out_shape=VMEM((rows, width), jnp.float32),
        in_specs=[vspec()] * 3,
        out_specs=vspec(),
        compiler_params=params(),
        cost_estimate=cost(2 * rows * rows * width, 1_500_000),
    )(pinned(d0), pinned(d1), features)


def middle_kernel(rounds, *refs):
    got, refs = refs[:rounds], refs[rounds:]
    d0, d1, sum_ref, x_ref, ct_ref, deg_ref, ws_ref, wn_ref, bias_ref = refs[:9]
    out_ref, gp_ref, st_ref, mine_ref, give_ref, both, halo, sums = refs[9:]
    core = lax.axis_index("dom") & 1
    half, step = d0.shape[1], 512
    boundary = got[0].shape[1]
    per = boundary // TILE
    for r in range(rounds):
        halo[r * boundary : (r + 1) * boundary, :] = got[r][...].T
    for p, dense_ref in enumerate((d0, d1)):
        for j in range(0, half, step):
            start = p * half + j
            total = sum_ref[start : start + step, :]
            for r in range(rounds):
                left = jnp.concatenate(
                    [dense_ref[c, j : j + step, :] for c in range(r * per, (r + 1) * per)], axis=1
                )
                total = total + nn_dot(left, halo[r * boundary : (r + 1) * boundary, :])
            sums[start : start + step, :] = total
    for start in range(0, 2 * half, step):
        total = sums[start : start + step, :]
        for i in range(start // TILE, (start + step) // TILE):
            rows = slice(i * TILE, (i + 1) * TILE)
            line = deg_ref[i : i + 1, :].astype(jnp.float32)
            column = jnp.broadcast_to(line, (TILE, TILE)).T
            agg = total[i * TILE - start : (i + 1) * TILE - start, :] / column
            agg = agg.astype(jnp.bfloat16)
            both[rows, :TILE] = x_ref[rows, :]
            both[rows, TILE:] = agg
            preact = nn_dot(x_ref[rows, :], ws_ref[...]) + nn_dot(agg, wn_ref[...])
            preact = preact + bias_ref[...]
            sig = jax.nn.sigmoid(preact)
            out_ref[rows, :] = (preact * sig).astype(jnp.bfloat16)
            grad = ct_ref[rows, :].astype(jnp.float32) * sig * (1.0 + preact * (1.0 - sig))
            grad = grad.astype(jnp.bfloat16)
            gp_ref[rows, :] = grad
            st_ref[:, rows] = (nt_dot(wn_ref[...], grad) / line).astype(jnp.bfloat16)
    parts = lax.dot_general(
        both[...], gp_ref[...], (((0,), (0,)), ((), ())), preferred_element_type=jnp.float32
    )
    mine_ref[...] = jnp.where(core == 0, parts[:TILE], parts[TILE:])
    give_ref[...] = jnp.where(core == 0, parts[TILE:], parts[:TILE])


def middle(received, d0, d1, summed, features, cotangent, degree, w_self, w_neigh, bias):
    rows, width = features.shape
    rounds, boundary = len(received), received[0].shape[1]
    half = jax.ShapeDtypeStruct((rows, width), jnp.bfloat16)
    part = VMEM((width, width), jnp.float32)
    return pl.pallas_call(
        functools.partial(middle_kernel, rounds),
        out_shape=[
            half,
            VMEM((rows, width), jnp.bfloat16),
            VMEM((width, rows), jnp.bfloat16),
            part,
            part,
        ],
        in_specs=[vspec()] * (rounds + 9),
        out_specs=[vspec()] * 5,
        scratch_shapes=[
            VMEM((rows, 2 * width), jnp.bfloat16),
            VMEM((rounds * boundary, width), jnp.bfloat16),
            VMEM((rows, width), jnp.float32),
        ],
        compiler_params=params(),
        cost_estimate=cost(2 * rows * rounds * boundary * width, 5_000_000, rows * width),
    )(
        *received,
        pinned(d0),
        pinned(d1),
        pinned(summed),
        features,
        cotangent,
        degree,
        w_self,
        w_neigh,
        bias,
    )


def beside(d0_ref, d1_ref, slab):
    return jnp.concatenate(
        [jnp.concatenate([d[slab], d[slab + 1]], axis=1) for d in (d0_ref, d1_ref)], axis=0
    )


def back_kernel(first, n, st_ref, d0_ref, d1_ref, before_ref, out_ref):
    for c in range(0, n, 2):
        product = nn_dot(st_ref[...], beside(d0_ref, d1_ref, first + c))
        out_ref[:, c * TILE : (c + 2) * TILE] = product.astype(jnp.bfloat16)


def back(first, n, scaled_t, d0, d1, before):
    width, rows = scaled_t.shape
    return pl.pallas_call(
        functools.partial(back_kernel, first, n),
        out_shape=jax.ShapeDtypeStruct((width, n * TILE), jnp.bfloat16),
        in_specs=[vspec()] * 3 + [pl.BlockSpec(memory_space=pl.ANY)],
        out_specs=vspec(),
        compiler_params=params(),
        cost_estimate=cost(1, 1),
    )(pinned(scaled_t), pinned(d0), pinned(d1), before)


def own_kernel(st_ref, d0_ref, d1_ref, gp_ref, ws_ref, before_ref, out_ref):
    for c in range(0, d0_ref.shape[0], 2):
        rows = slice(c * TILE, (c + 2) * TILE)
        product = nn_dot(st_ref[...], beside(d0_ref, d1_ref, c))
        out_ref[:, rows] = product + nt_dot(ws_ref[...], gp_ref[rows, :])


def own(scaled_t, d0, d1, grad_pre, w_self, before):
    width, rows = scaled_t.shape
    return pl.pallas_call(
        own_kernel,
        out_shape=VMEM((width, rows), jnp.float32),
        in_specs=[vspec()] * 5 + [pl.BlockSpec(memory_space=pl.ANY)],
        out_specs=vspec(),
        compiler_params=params(),
        cost_estimate=cost(1, 1),
    )(pinned(scaled_t), pinned(d0), pinned(d1), pinned(grad_pre), w_self, before)


def place_kernel(rounds, last, rows_ref, acc_ref, before_ref, *refs):
    returned, (out_ref, token_ref, listed) = refs[: len(rounds)], refs[len(rounds) :]
    token_ref[...] = jnp.zeros_like(token_ref)
    step, boundary = 2 * TILE, rows_ref.shape[1]
    for place, r in enumerate(rounds):
        for k in range(0, boundary, TILE):
            line = rows_ref[r : r + 1, k : k + TILE].astype(jnp.float32)
            listed[place, k : k + TILE, :] = jnp.broadcast_to(line, (TILE, TILE)).T
    numbers = lax.broadcasted_iota(jnp.int32, (boundary, TILE), 1).astype(jnp.float32)
    for j in range(0, acc_ref.shape[1], step):
        total = acc_ref[:, j : j + step]
        for place, got_ref in enumerate(returned):
            table = jnp.concatenate(
                [
                    jnp.where(listed[place] == numbers + float(n), 1.0, 0.0).astype(jnp.bfloat16)
                    for n in range(j, j + step, TILE)
                ],
                axis=1,
            )
            total = total + nn_dot(got_ref[...], table)
        if last:
            out_ref[j : j + step, :] = total.T
        else:
            out_ref[:, j : j + step] = total


def place_rows(rounds, last, send_rows, acc, returned, before):
    width, rows = acc.shape
    count, boundary = len(rounds), send_rows.shape[1]
    if last:
        out = jax.ShapeDtypeStruct((rows, width), jnp.float32)
    else:
        out = VMEM((width, rows), jnp.float32)
    return pl.pallas_call(
        functools.partial(place_kernel, rounds, last),
        out_shape=[out, VMEM((8, TILE), jnp.float32)],
        in_specs=[vspec()] * 2 + [pl.BlockSpec(memory_space=pl.ANY)] + [vspec()] * count,
        out_specs=[vspec()] * 2,
        scratch_shapes=[VMEM((count, boundary, TILE), jnp.float32)],
        compiler_params=params(),
        cost_estimate=cost(1, 1),
    )(send_rows, pinned(acc), before, *returned)


def add_kernel(left_ref, right_ref, before_ref, out_ref):
    out_ref[...] = left_ref[...] + right_ref[...]


def added(left, right, before):
    return pl.pallas_call(
        add_kernel,
        out_shape=VMEM(left.shape, jnp.float32),
        in_specs=[vspec()] * 2 + [pl.BlockSpec(memory_space=pl.ANY)],
        out_specs=vspec(),
        compiler_params=params(1024 * 1024),
        cost_estimate=cost(1, 1),
    )(pinned(left), right, before)


def halves_kernel(scale, total_ref, other_ref, self_ref, neigh_ref):
    core = lax.axis_index("dom") & 1
    total, other = total_ref[...], other_ref[...]
    self_ref[...] = jnp.where(core == 0, total, other) * scale
    neigh_ref[...] = jnp.where(core == 0, other, total) * scale


def halves(scale, total, other):
    out = jax.ShapeDtypeStruct(total.shape, jnp.float32)
    return pl.pallas_call(
        functools.partial(halves_kernel, scale),
        out_shape=[out, out],
        in_specs=[vspec()] * 2,
        out_specs=[vspec()] * 2,
        compiler_params=params(1024 * 1024),
        cost_estimate=cost(2 * total.size, 4 * total.size * 4),
    )(pinned(total), other)


def swapped(shard, mask):
    return lax.ppermute(shard, "dom", [(i, i ^ mask) for i in range(lax.axis_size("dom"))])


def local(
    node_features,
    w_self,
    w_neigh,
    output_bias,
    local_tiles,
    halo_tiles,
    local_cols,
    halo_cols,
    send_rows,
    degree,
    cotangent,
):
    row_count, width = node_features.shape
    nblocks = local_tiles.shape[0]
    round_count, boundary = send_rows.shape
    per = boundary // TILE
    picked = pick_rows(send_rows, node_features)
    received = [swapped(rows, 1 << r) for r, rows in enumerate(picked)]
    dl0, dl1, dh0, dh1 = densify(
        local_cols, halo_cols, local_tiles, halo_tiles, round_count * per
    )
    summed = local_sums(dl0, dl1, node_features)
    output, grad_pre, scaled_t, mine, give = middle(
        received,
        dh0,
        dh1,
        summed,
        node_features,
        cotangent,
        degree.reshape(nblocks, TILE),
        w_self,
        w_neigh,
        output_bias.reshape(1, width),
    )
    returned = {}

    def send_back(r, before):
        grads = back(r * per, per, scaled_t, dh0, dh1, before)
        returned[r] = swapped(grads, 1 << r)
        return grads

    def place(rounds, acc, before):
        got = [returned[r] for r in rounds]
        return place_rows(rounds, 0 in rounds, send_rows, acc, got, before)

    other = swapped(give, 1)
    last = send_back(2, scaled_t)
    last = send_back(4, last)
    total = added(mine, other, last)
    other = swapped(total, 32)
    last = send_back(1, total)
    last = send_back(3, last)
    last = send_back(0, last)
    total = added(total, other, last)
    other = swapped(total, 64)
    grads_t = own(scaled_t, dl0, dl1, grad_pre, w_self, total)
    total = added(total, other, grads_t)
    other = swapped(total, 8)
    grads_t, last = place((2, 4), grads_t, total)
    total = added(total, other, last)
    other = swapped(total, 16)
    grads_t, last = place((3, 1), grads_t, total)
    total = added(total, other, last)
    other = swapped(total, 2)
    grads, last = place((0,), grads_t, total)
    total = added(total, other, last)
    other = swapped(total, 4)
    total = added(total, other, total)
    other = swapped(total, 1)
    grad_scale = 1.0 / math.sqrt(row_count * lax.axis_size("dom"))
    grad_self, grad_neigh = halves(grad_scale, total, other)
    return (output, grads, grad_self, grad_neigh)


def solution(mesh):
    in_specs = (
        P("dom", None),
        P(),
        P(),
        P(),
        P("dom", None, None, None),
        P("dom", None, None, None),
        P("dom", None),
        P("dom", None),
        P("dom", None),
        P("dom"),
        P("dom", None),
    )
    out_specs = (P("dom", None), P("dom", None), P(), P())
    return jax.shard_map(local, mesh=mesh, in_specs=in_specs, out_specs=out_specs, check_vma=False)
```

```python
import functools
import math

import jax
import jax.numpy as jnp
from jax import lax
from jax.experimental import pallas as pl
from jax.experimental.pallas import tpu as pltpu
from jax.sharding import PartitionSpec as P

TILE = 128
VMEM = pltpu.VMEM
LIMIT = 8 * 1024 * 1024


def vspec():
    return pl.BlockSpec(memory_space=VMEM)


def sspec():
    return pl.BlockSpec(memory_space=pltpu.SMEM)


def params(limit=LIMIT):
    return pltpu.CompilerParams(vmem_limit_bytes=limit)


def in_hbm(array):
    return pltpu.with_memory_space_constraint(array, pltpu.HBM)


def cost(flops, size, transcendentals=0):
    return pl.CostEstimate(flops=flops, bytes_accessed=size, transcendentals=transcendentals)


def pinned(array):
    return pltpu.with_memory_space_constraint(array, VMEM)


def nt_dot(left, right):
    return lax.dot_general(
        left, right, (((1,), (1,)), ((), ())), preferred_element_type=jnp.float32
    )


def nn_dot(left, right):
    return jnp.dot(left, right, preferred_element_type=jnp.float32)


def pick_kernel(rows_hbm, x_hbm, *refs):
    outs, (rows_ref, x_ref, xt_ref, rows_sem, x_sem) = refs[:-5], refs[-5:]
    rounds = len(outs)
    rows_copy = pltpu.make_async_copy(rows_hbm, rows_ref, rows_sem)
    x_copy = pltpu.make_async_copy(x_hbm, x_ref, x_sem)
    rows_copy.start()
    x_copy.start()
    rows_copy.wait()
    count, step = x_ref.shape[0], 2 * TILE
    numbers = lax.broadcasted_iota(jnp.int32, (count, step), 0)
    for r in range(rounds):
        for k in range(0, rows_ref.shape[1], step):
            listed = rows_ref[r : r + 1, k : k + step]
            table = jnp.where(numbers == listed, 1.0, 0.0).astype(jnp.bfloat16)
            if r == 0 and k == 0:
                x_copy.wait()
                for i in range(0, count, TILE):
                    xt_ref[:, i : i + TILE] = x_ref[i : i + TILE, :].T
            outs[r][:, k : k + step] = nn_dot(xt_ref[...], table).astype(jnp.bfloat16)


def pick_rows(send_rows, features):
    rows, width = features.shape
    rounds, boundary = send_rows.shape
    outs = [jax.ShapeDtypeStruct((width, boundary), jnp.bfloat16) for _ in range(rounds)]
    return pl.pallas_call(
        pick_kernel,
        out_shape=outs,
        in_specs=[pl.BlockSpec(memory_space=pltpu.HBM)] * 2,
        out_specs=[vspec()] * len(outs),
        scratch_shapes=[
            VMEM(send_rows.shape, jnp.int32),
            VMEM(features.shape, jnp.bfloat16),
            VMEM((width, rows), jnp.bfloat16),
            pltpu.SemaphoreType.DMA,
            pltpu.SemaphoreType.DMA,
        ],
        compiler_params=params(),
        cost_estimate=cost(2 * rows * boundary * rounds * width, 1_000_000),
    )(in_hbm(send_rows), in_hbm(features))


def densify_kernel(
    lc_hbm, hc_hbm, lt, ht, dl0, dl1, dh0, dh1, lslots, hslots, zeros, lc, hc, sems, zsems, csems
):
    half = lt.shape[0] // 2
    depth = lslots.shape[0]
    dense = (dl0, dl1, dh0, dh1)

    def fetch(i, slot):
        return [
            pltpu.make_async_copy(
                src.at[i + p * half], dst.at[slot, p], sems.at[slot, 2 * q + p]
            )
            for q, (src, dst) in enumerate(((lt, lslots), (ht, hslots)))
            for p in range(2)
        ]

    def clear(i, slot):
        rows = pl.ds(pl.multiple_of(i * TILE, TILE), TILE)
        return [
            pltpu.make_async_copy(
                zeros.at[pl.ds(0, d.shape[0])], d.at[:, rows, :], zsems.at[slot, k]
            )
            for k, d in enumerate(dense)
        ]

    for d in range(depth - 1):
        for copy in fetch(d, d):
            copy.start()
    columns = [
        pltpu.make_async_copy(lc_hbm, lc, csems.at[0]),
        pltpu.make_async_copy(hc_hbm, hc, csems.at[1]),
    ]
    for copy in columns:
        copy.start()
    zeros[...] = jnp.zeros_like(zeros)
    for copy in clear(0, 0):
        copy.start()
    for copy in columns:
        copy.wait()

    def body(i, carry):
        slot, zslot = lax.rem(i, depth), lax.rem(i, 2)

        @pl.when(i + depth - 1 < half)
        def _():
            for copy in fetch(i + depth - 1, lax.rem(i + depth - 1, depth)):
                copy.start()

        @pl.when(i + 1 < half)
        def _():
            for copy in clear(i + 1, 1 - zslot):
                copy.start()

        for copy in clear(i, zslot):
            copy.wait()
        for copy in fetch(i, slot):
            copy.wait()
        rows = pl.ds(pl.multiple_of(i * TILE, TILE), TILE)
        for t in range(max(lt.shape[1], ht.shape[1])):
            jobs = []
            if t < lt.shape[1]:
                jobs += [(dl0, lc[i, t], lslots, 0), (dl1, lc[i + half, t], lslots, 1)]
            if t < ht.shape[1]:
                jobs += [(dh0, hc[i, t], hslots, 0), (dh1, hc[i + half, t], hslots, 1)]
            sums = [d[c, rows, :] + s[slot, p, t] for d, c, s, p in jobs]
            for (d, c, _, _), total in zip(jobs, sums):
                d[c, rows, :] = total
        return carry

    lax.fori_loop(0, half, body, 0)


def densify(local_cols, halo_cols, local_tiles, halo_tiles, halo_blocks):
    nblocks, local_count = local_cols.shape
    halo_count = halo_cols.shape[1]
    half = nblocks // 2 * TILE
    depth = 3
    slabs = (nblocks, nblocks, halo_blocks, halo_blocks)
    return pl.pallas_call(
        densify_kernel,
        out_shape=[VMEM((n, half, TILE), jnp.bfloat16) for n in slabs],
        in_specs=[pl.BlockSpec(memory_space=pltpu.HBM)] * 4,
        out_specs=[vspec()] * 4,
        scratch_shapes=[
            VMEM((depth, 2, local_count, TILE, TILE), jnp.bfloat16),
            VMEM((depth, 2, halo_count, TILE, TILE), jnp.bfloat16),
            VMEM((max(slabs), TILE, TILE), jnp.bfloat16),
            pltpu.SMEM(local_cols.shape, jnp.int32),
            pltpu.SMEM(halo_cols.shape, jnp.int32),
            pltpu.SemaphoreType.DMA((depth, 4)),
            pltpu.SemaphoreType.DMA((2, 4)),
            pltpu.SemaphoreType.DMA((2,)),
        ],
        compiler_params=params(12 * 1024 * 1024),
        cost_estimate=cost(16_000_000, nblocks * (local_count + halo_count) * TILE * TILE * 2),
    )(in_hbm(local_cols), in_hbm(halo_cols), in_hbm(local_tiles), in_hbm(halo_tiles))


def local_sums_kernel(d0_ref, d1_ref, x_ref, out_ref):
    half, step = d0_ref.shape[1], 512
    for p, dense_ref in enumerate((d0_ref, d1_ref)):
        for j in range(0, half, step):
            left = jnp.concatenate(
                [dense_ref[c, j : j + step, :] for c in range(dense_ref.shape[0])], axis=1
            )
            out_ref[p * half + j : p * half + j + step, :] = nn_dot(left, x_ref[...])


def local_sums(d0, d1, features):
    rows, width = features.shape
    return pl.pallas_call(
        local_sums_kernel,
        out_shape=VMEM((rows, width), jnp.float32),
        in_specs=[vspec()] * 3,
        out_specs=vspec(),
        compiler_params=params(),
        cost_estimate=cost(2 * rows * rows * width, 1_500_000),
    )(pinned(d0), pinned(d1), features)


def middle_kernel(rounds, *refs):
    got, refs = refs[:rounds], refs[rounds:]
    d0, d1, sum_ref, x_ref, ct_ref, deg_ref, ws_ref, wn_ref, bias_ref = refs[:9]
    out_ref, gp_ref, st_ref, mine_ref, give_ref, both, halo, sums = refs[9:]
    core = lax.axis_index("dom") & 1
    half, step = d0.shape[1], 512
    boundary = got[0].shape[1]
    per = boundary // TILE
    for r in range(rounds):
        halo[r * boundary : (r + 1) * boundary, :] = got[r][...].T
    for p, dense_ref in enumerate((d0, d1)):
        for j in range(0, half, step):
            start = p * half + j
            total = sum_ref[start : start + step, :]
            for r in range(rounds):
                left = jnp.concatenate(
                    [dense_ref[c, j : j + step, :] for c in range(r * per, (r + 1) * per)], axis=1
                )
                total = total + nn_dot(left, halo[r * boundary : (r + 1) * boundary, :])
            sums[start : start + step, :] = total
    for start in range(0, 2 * half, step):
        total = sums[start : start + step, :]
        for i in range(start // TILE, (start + step) // TILE):
            rows = slice(i * TILE, (i + 1) * TILE)
            line = deg_ref[i : i + 1, :].astype(jnp.float32)
            column = jnp.broadcast_to(line, (TILE, TILE)).T
            agg = total[i * TILE - start : (i + 1) * TILE - start, :] / column
            agg = agg.astype(jnp.bfloat16)
            both[rows, :TILE] = x_ref[rows, :]
            both[rows, TILE:] = agg
            preact = nn_dot(x_ref[rows, :], ws_ref[...]) + nn_dot(agg, wn_ref[...])
            preact = preact + bias_ref[...]
            sig = jax.nn.sigmoid(preact)
            out_ref[rows, :] = (preact * sig).astype(jnp.bfloat16)
            grad = ct_ref[rows, :].astype(jnp.float32) * sig * (1.0 + preact * (1.0 - sig))
            grad = grad.astype(jnp.bfloat16)
            gp_ref[rows, :] = grad
            st_ref[:, rows] = (nt_dot(wn_ref[...], grad) / line).astype(jnp.bfloat16)
    parts = lax.dot_general(
        both[...], gp_ref[...], (((0,), (0,)), ((), ())), preferred_element_type=jnp.float32
    )
    mine_ref[...] = jnp.where(core == 0, parts[:TILE], parts[TILE:])
    give_ref[...] = jnp.where(core == 0, parts[TILE:], parts[:TILE])


def middle(received, d0, d1, summed, features, cotangent, degree, w_self, w_neigh, bias):
    rows, width = features.shape
    rounds, boundary = len(received), received[0].shape[1]
    half = jax.ShapeDtypeStruct((rows, width), jnp.bfloat16)
    part = VMEM((width, width), jnp.float32)
    return pl.pallas_call(
        functools.partial(middle_kernel, rounds),
        out_shape=[
            half,
            VMEM((rows, width), jnp.bfloat16),
            VMEM((width, rows), jnp.bfloat16),
            part,
            part,
        ],
        in_specs=[vspec()] * (rounds + 9),
        out_specs=[vspec()] * 5,
        scratch_shapes=[
            VMEM((rows, 2 * width), jnp.bfloat16),
            VMEM((rounds * boundary, width), jnp.bfloat16),
            VMEM((rows, width), jnp.float32),
        ],
        compiler_params=params(),
        cost_estimate=cost(2 * rows * rounds * boundary * width, 5_000_000, rows * width),
    )(
        *received,
        pinned(d0),
        pinned(d1),
        pinned(summed),
        features,
        cotangent,
        degree,
        w_self,
        w_neigh,
        bias,
    )


def beside(d0_ref, d1_ref, slab):
    return jnp.concatenate(
        [jnp.concatenate([d[slab], d[slab + 1]], axis=1) for d in (d0_ref, d1_ref)], axis=0
    )


def back_kernel(first, n, st_ref, d0_ref, d1_ref, before_ref, out_ref):
    for c in range(0, n, 2):
        product = nn_dot(st_ref[...], beside(d0_ref, d1_ref, first + c))
        out_ref[:, c * TILE : (c + 2) * TILE] = product.astype(jnp.bfloat16)


def back(first, n, scaled_t, d0, d1, before):
    width, rows = scaled_t.shape
    return pl.pallas_call(
        functools.partial(back_kernel, first, n),
        out_shape=jax.ShapeDtypeStruct((width, n * TILE), jnp.bfloat16),
        in_specs=[vspec()] * 3 + [pl.BlockSpec(memory_space=pl.ANY)],
        out_specs=vspec(),
        compiler_params=params(),
        cost_estimate=cost(1, 1),
    )(pinned(scaled_t), pinned(d0), pinned(d1), before)


def own_kernel(st_ref, d0_ref, d1_ref, gp_ref, ws_ref, before_ref, out_ref):
    for c in range(0, d0_ref.shape[0], 2):
        rows = slice(c * TILE, (c + 2) * TILE)
        product = nn_dot(st_ref[...], beside(d0_ref, d1_ref, c))
        out_ref[:, rows] = product + nt_dot(ws_ref[...], gp_ref[rows, :])


def own(scaled_t, d0, d1, grad_pre, w_self, before):
    width, rows = scaled_t.shape
    return pl.pallas_call(
        own_kernel,
        out_shape=VMEM((width, rows), jnp.float32),
        in_specs=[vspec()] * 5 + [pl.BlockSpec(memory_space=pl.ANY)],
        out_specs=vspec(),
        compiler_params=params(),
        cost_estimate=cost(1, 1),
    )(pinned(scaled_t), pinned(d0), pinned(d1), pinned(grad_pre), w_self, before)


def place_kernel(rounds, last, rows_ref, acc_ref, before_ref, *refs):
    returned, (out_ref, token_ref, listed) = refs[: len(rounds)], refs[len(rounds) :]
    token_ref[...] = jnp.zeros_like(token_ref)
    step, boundary = 2 * TILE, rows_ref.shape[1]
    for place, r in enumerate(rounds):
        for k in range(0, boundary, TILE):
            line = rows_ref[r : r + 1, k : k + TILE].astype(jnp.float32)
            listed[place, k : k + TILE, :] = jnp.broadcast_to(line, (TILE, TILE)).T
    numbers = lax.broadcasted_iota(jnp.int32, (boundary, TILE), 1).astype(jnp.float32)
    for j in range(0, acc_ref.shape[1], step):
        total = acc_ref[:, j : j + step]
        for place, got_ref in enumerate(returned):
            table = jnp.concatenate(
                [
                    jnp.where(listed[place] == numbers + float(n), 1.0, 0.0).astype(jnp.bfloat16)
                    for n in range(j, j + step, TILE)
                ],
                axis=1,
            )
            total = total + nn_dot(got_ref[...], table)
        if last:
            out_ref[j : j + step, :] = total.T
        else:
            out_ref[:, j : j + step] = total


def place_rows(rounds, last, send_rows, acc, returned, before):
    width, rows = acc.shape
    count, boundary = len(rounds), send_rows.shape[1]
    if last:
        out = jax.ShapeDtypeStruct((rows, width), jnp.float32)
    else:
        out = VMEM((width, rows), jnp.float32)
    return pl.pallas_call(
        functools.partial(place_kernel, rounds, last),
        out_shape=[out, VMEM((8, TILE), jnp.float32)],
        in_specs=[vspec()] * 2 + [pl.BlockSpec(memory_space=pl.ANY)] + [vspec()] * count,
        out_specs=[vspec()] * 2,
        scratch_shapes=[VMEM((count, boundary, TILE), jnp.float32)],
        compiler_params=params(),
        cost_estimate=cost(1, 1),
    )(send_rows, pinned(acc), before, *returned)


def add_kernel(left_ref, right_ref, before_ref, out_ref):
    out_ref[...] = left_ref[...] + right_ref[...]


def added(left, right, before):
    return pl.pallas_call(
        add_kernel,
        out_shape=VMEM(left.shape, jnp.float32),
        in_specs=[vspec()] * 2 + [pl.BlockSpec(memory_space=pl.ANY)],
        out_specs=vspec(),
        compiler_params=params(1024 * 1024),
        cost_estimate=cost(1, 1),
    )(pinned(left), right, before)


def halves_kernel(scale, total_ref, other_ref, self_ref, neigh_ref):
    core = lax.axis_index("dom") & 1
    total, other = total_ref[...], other_ref[...]
    self_ref[...] = jnp.where(core == 0, total, other) * scale
    neigh_ref[...] = jnp.where(core == 0, other, total) * scale


def halves(scale, total, other):
    out = jax.ShapeDtypeStruct(total.shape, jnp.float32)
    return pl.pallas_call(
        functools.partial(halves_kernel, scale),
        out_shape=[out, out],
        in_specs=[vspec()] * 2,
        out_specs=[vspec()] * 2,
        compiler_params=params(1024 * 1024),
        cost_estimate=cost(2 * total.size, 4 * total.size * 4),
    )(pinned(total), other)


def swapped(shard, mask):
    return lax.ppermute(shard, "dom", [(i, i ^ mask) for i in range(lax.axis_size("dom"))])


def local(
    node_features,
    w_self,
    w_neigh,
    output_bias,
    local_tiles,
    halo_tiles,
    local_cols,
    halo_cols,
    send_rows,
    degree,
    cotangent,
):
    row_count, width = node_features.shape
    nblocks = local_tiles.shape[0]
    round_count, boundary = send_rows.shape
    per = boundary // TILE
    picked = pick_rows(send_rows, node_features)
    received = [swapped(rows, 1 << r) for r, rows in enumerate(picked)]
    dl0, dl1, dh0, dh1 = densify(
        local_cols, halo_cols, local_tiles, halo_tiles, round_count * per
    )
    summed = local_sums(dl0, dl1, node_features)
    output, grad_pre, scaled_t, mine, give = middle(
        received,
        dh0,
        dh1,
        summed,
        node_features,
        cotangent,
        degree.reshape(nblocks, TILE),
        w_self,
        w_neigh,
        output_bias.reshape(1, width),
    )
    returned = {}

    def send_back(r, before):
        grads = back(r * per, per, scaled_t, dh0, dh1, before)
        returned[r] = swapped(grads, 1 << r)
        return grads

    def place(rounds, acc, before):
        got = [returned[r] for r in rounds]
        return place_rows(rounds, 0 in rounds, send_rows, acc, got, before)

    other = swapped(give, 1)
    last = send_back(2, scaled_t)
    last = send_back(4, last)
    total = added(mine, other, last)
    other = swapped(total, 32)
    last = send_back(1, total)
    last = send_back(3, last)
    last = send_back(0, last)
    total = added(total, other, last)
    other = swapped(total, 96)
    grads_t = own(scaled_t, dl0, dl1, grad_pre, w_self, total)
    total = added(total, other, grads_t)
    other = swapped(total, 8)
    grads_t, last = place((2, 4), grads_t, total)
    total = added(total, other, last)
    other = swapped(total, 24)
    grads_t, last = place((3, 1), grads_t, total)
    total = added(total, other, last)
    other = swapped(total, 2)
    grads, last = place((0,), grads_t, total)
    total = added(total, other, last)
    other = swapped(total, 6)
    total = added(total, other, total)
    other = swapped(total, 1)
    grad_scale = 1.0 / math.sqrt(row_count * lax.axis_size("dom"))
    grad_self, grad_neigh = halves(grad_scale, total, other)
    return (output, grads, grad_self, grad_neigh)


def solution(mesh):
    in_specs = (
        P("dom", None),
        P(),
        P(),
        P(),
        P("dom", None, None, None),
        P("dom", None, None, None),
        P("dom", None),
        P("dom", None),
        P("dom", None),
        P("dom"),
        P("dom", None),
    )
    out_specs = (P("dom", None), P("dom", None), P(), P())
    return jax.shard_map(local, mesh=mesh, in_specs=in_specs, out_specs=out_specs, check_vma=False)
```

```python
import functools
import math

import jax
import jax.numpy as jnp
from jax import lax
from jax.experimental import pallas as pl
from jax.experimental.pallas import tpu as pltpu
from jax.sharding import PartitionSpec as P

TILE = 128
VMEM = pltpu.VMEM
LIMIT = 8 * 1024 * 1024


def vspec():
    return pl.BlockSpec(memory_space=VMEM)


def sspec():
    return pl.BlockSpec(memory_space=pltpu.SMEM)


def params(limit=LIMIT):
    return pltpu.CompilerParams(vmem_limit_bytes=limit)


def in_hbm(array):
    return pltpu.with_memory_space_constraint(array, pltpu.HBM)


def cost(flops, size, transcendentals=0):
    return pl.CostEstimate(flops=flops, bytes_accessed=size, transcendentals=transcendentals)


def pinned(array):
    return pltpu.with_memory_space_constraint(array, VMEM)


def nt_dot(left, right):
    return lax.dot_general(
        left, right, (((1,), (1,)), ((), ())), preferred_element_type=jnp.float32
    )


def nn_dot(left, right):
    return jnp.dot(left, right, preferred_element_type=jnp.float32)


def pick_kernel(rows_hbm, x_hbm, *refs):
    outs, (rows_ref, x_ref, xt_ref, rows_sem, x_sem) = refs[:-5], refs[-5:]
    rounds = len(outs)
    rows_copy = pltpu.make_async_copy(rows_hbm, rows_ref, rows_sem)
    x_copy = pltpu.make_async_copy(x_hbm, x_ref, x_sem)
    rows_copy.start()
    x_copy.start()
    rows_copy.wait()
    count, step = x_ref.shape[0], 2 * TILE
    numbers = lax.broadcasted_iota(jnp.int32, (count, step), 0)
    for r in range(rounds):
        for k in range(0, rows_ref.shape[1], step):
            listed = rows_ref[r : r + 1, k : k + step]
            table = jnp.where(numbers == listed, 1.0, 0.0).astype(jnp.bfloat16)
            if r == 0 and k == 0:
                x_copy.wait()
                for i in range(0, count, TILE):
                    xt_ref[:, i : i + TILE] = x_ref[i : i + TILE, :].T
            outs[r][:, k : k + step] = nn_dot(xt_ref[...], table).astype(jnp.bfloat16)


def pick_rows(send_rows, features):
    rows, width = features.shape
    rounds, boundary = send_rows.shape
    outs = [jax.ShapeDtypeStruct((width, boundary), jnp.bfloat16) for _ in range(rounds)]
    return pl.pallas_call(
        pick_kernel,
        out_shape=outs,
        in_specs=[pl.BlockSpec(memory_space=pltpu.HBM)] * 2,
        out_specs=[vspec()] * len(outs),
        scratch_shapes=[
            VMEM(send_rows.shape, jnp.int32),
            VMEM(features.shape, jnp.bfloat16),
            VMEM((width, rows), jnp.bfloat16),
            pltpu.SemaphoreType.DMA,
            pltpu.SemaphoreType.DMA,
        ],
        compiler_params=params(),
        cost_estimate=cost(2 * rows * boundary * rounds * width, 1_000_000),
    )(in_hbm(send_rows), in_hbm(features))


def densify_kernel(
    lc_hbm, hc_hbm, lt, ht, dl0, dl1, dh0, dh1, lslots, hslots, zeros, lc, hc, sems, zsems, csems
):
    half = lt.shape[0] // 2
    depth = lslots.shape[0]
    dense = (dl0, dl1, dh0, dh1)

    def fetch(i, slot):
        return [
            pltpu.make_async_copy(
                src.at[i + p * half], dst.at[slot, p], sems.at[slot, 2 * q + p]
            )
            for q, (src, dst) in enumerate(((lt, lslots), (ht, hslots)))
            for p in range(2)
        ]

    def clear(i, slot):
        rows = pl.ds(pl.multiple_of(i * TILE, TILE), TILE)
        return [
            pltpu.make_async_copy(
                zeros.at[pl.ds(0, d.shape[0])], d.at[:, rows, :], zsems.at[slot, k]
            )
            for k, d in enumerate(dense)
        ]

    for d in range(depth - 1):
        for copy in fetch(d, d):
            copy.start()
    columns = [
        pltpu.make_async_copy(lc_hbm, lc, csems.at[0]),
        pltpu.make_async_copy(hc_hbm, hc, csems.at[1]),
    ]
    for copy in columns:
        copy.start()
    zeros[...] = jnp.zeros_like(zeros)
    for copy in clear(0, 0):
        copy.start()
    for copy in columns:
        copy.wait()

    def body(i, carry):
        slot, zslot = lax.rem(i, depth), lax.rem(i, 2)

        @pl.when(i + depth - 1 < half)
        def _():
            for copy in fetch(i + depth - 1, lax.rem(i + depth - 1, depth)):
                copy.start()

        @pl.when(i + 1 < half)
        def _():
            for copy in clear(i + 1, 1 - zslot):
                copy.start()

        for copy in clear(i, zslot):
            copy.wait()
        for copy in fetch(i, slot):
            copy.wait()
        rows = pl.ds(pl.multiple_of(i * TILE, TILE), TILE)
        for t in range(max(lt.shape[1], ht.shape[1])):
            jobs = []
            if t < lt.shape[1]:
                jobs += [(dl0, lc[i, t], lslots, 0), (dl1, lc[i + half, t], lslots, 1)]
            if t < ht.shape[1]:
                jobs += [(dh0, hc[i, t], hslots, 0), (dh1, hc[i + half, t], hslots, 1)]
            sums = [d[c, rows, :] + s[slot, p, t] for d, c, s, p in jobs]
            for (d, c, _, _), total in zip(jobs, sums):
                d[c, rows, :] = total
        return carry

    lax.fori_loop(0, half, body, 0)


def densify(local_cols, halo_cols, local_tiles, halo_tiles, halo_blocks):
    nblocks, local_count = local_cols.shape
    halo_count = halo_cols.shape[1]
    half = nblocks // 2 * TILE
    depth = 3
    slabs = (nblocks, nblocks, halo_blocks, halo_blocks)
    return pl.pallas_call(
        densify_kernel,
        out_shape=[VMEM((n, half, TILE), jnp.bfloat16) for n in slabs],
        in_specs=[pl.BlockSpec(memory_space=pltpu.HBM)] * 4,
        out_specs=[vspec()] * 4,
        scratch_shapes=[
            VMEM((depth, 2, local_count, TILE, TILE), jnp.bfloat16),
            VMEM((depth, 2, halo_count, TILE, TILE), jnp.bfloat16),
            VMEM((max(slabs), TILE, TILE), jnp.bfloat16),
            pltpu.SMEM(local_cols.shape, jnp.int32),
            pltpu.SMEM(halo_cols.shape, jnp.int32),
            pltpu.SemaphoreType.DMA((depth, 4)),
            pltpu.SemaphoreType.DMA((2, 4)),
            pltpu.SemaphoreType.DMA((2,)),
        ],
        compiler_params=params(12 * 1024 * 1024),
        cost_estimate=cost(16_000_000, nblocks * (local_count + halo_count) * TILE * TILE * 2),
    )(in_hbm(local_cols), in_hbm(halo_cols), in_hbm(local_tiles), in_hbm(halo_tiles))


def local_sums_kernel(d0_ref, d1_ref, x_ref, out_ref):
    half, step = d0_ref.shape[1], 512
    for p, dense_ref in enumerate((d0_ref, d1_ref)):
        for j in range(0, half, step):
            left = jnp.concatenate(
                [dense_ref[c, j : j + step, :] for c in range(dense_ref.shape[0])], axis=1
            )
            out_ref[p * half + j : p * half + j + step, :] = nn_dot(left, x_ref[...])


def local_sums(d0, d1, features):
    rows, width = features.shape
    return pl.pallas_call(
        local_sums_kernel,
        out_shape=VMEM((rows, width), jnp.float32),
        in_specs=[vspec()] * 3,
        out_specs=vspec(),
        compiler_params=params(),
        cost_estimate=cost(2 * rows * rows * width, 1_500_000),
    )(pinned(d0), pinned(d1), features)


def middle_kernel(rounds, *refs):
    got, refs = refs[:rounds], refs[rounds:]
    d0, d1, sum_ref, x_ref, ct_ref, deg_ref, ws_ref, wn_ref, bias_ref = refs[:9]
    out_ref, gp_ref, st_ref, mine_ref, give_ref, both, halo, sums = refs[9:]
    core = lax.axis_index("dom") & 1
    half, step = d0.shape[1], 512
    boundary = got[0].shape[1]
    per = boundary // TILE
    for r in range(rounds):
        halo[r * boundary : (r + 1) * boundary, :] = got[r][...].T
    for p, dense_ref in enumerate((d0, d1)):
        for j in range(0, half, step):
            start = p * half + j
            total = sum_ref[start : start + step, :]
            for r in range(rounds):
                left = jnp.concatenate(
                    [dense_ref[c, j : j + step, :] for c in range(r * per, (r + 1) * per)], axis=1
                )
                total = total + nn_dot(left, halo[r * boundary : (r + 1) * boundary, :])
            sums[start : start + step, :] = total
    for start in range(0, 2 * half, step):
        total = sums[start : start + step, :]
        for i in range(start // TILE, (start + step) // TILE):
            rows = slice(i * TILE, (i + 1) * TILE)
            line = deg_ref[i : i + 1, :].astype(jnp.float32)
            column = jnp.broadcast_to(line, (TILE, TILE)).T
            agg = total[i * TILE - start : (i + 1) * TILE - start, :] / column
            agg = agg.astype(jnp.bfloat16)
            both[rows, :TILE] = x_ref[rows, :]
            both[rows, TILE:] = agg
            preact = nn_dot(x_ref[rows, :], ws_ref[...]) + nn_dot(agg, wn_ref[...])
            preact = preact + bias_ref[...]
            sig = jax.nn.sigmoid(preact)
            out_ref[rows, :] = (preact * sig).astype(jnp.bfloat16)
            grad = ct_ref[rows, :].astype(jnp.float32) * sig * (1.0 + preact * (1.0 - sig))
            grad = grad.astype(jnp.bfloat16)
            gp_ref[rows, :] = grad
            st_ref[:, rows] = (nt_dot(wn_ref[...], grad) / line).astype(jnp.bfloat16)
    parts = lax.dot_general(
        both[...], gp_ref[...], (((0,), (0,)), ((), ())), preferred_element_type=jnp.float32
    )
    mine_ref[...] = jnp.where(core == 0, parts[:TILE], parts[TILE:])
    give_ref[...] = jnp.where(core == 0, parts[TILE:], parts[:TILE])


def middle(received, d0, d1, summed, features, cotangent, degree, w_self, w_neigh, bias):
    rows, width = features.shape
    rounds, boundary = len(received), received[0].shape[1]
    half = jax.ShapeDtypeStruct((rows, width), jnp.bfloat16)
    part = VMEM((width, width), jnp.float32)
    return pl.pallas_call(
        functools.partial(middle_kernel, rounds),
        out_shape=[
            half,
            VMEM((rows, width), jnp.bfloat16),
            VMEM((width, rows), jnp.bfloat16),
            part,
            part,
        ],
        in_specs=[vspec()] * (rounds + 9),
        out_specs=[vspec()] * 5,
        scratch_shapes=[
            VMEM((rows, 2 * width), jnp.bfloat16),
            VMEM((rounds * boundary, width), jnp.bfloat16),
            VMEM((rows, width), jnp.float32),
        ],
        compiler_params=params(),
        cost_estimate=cost(2 * rows * rounds * boundary * width, 5_000_000, rows * width),
    )(
        *received,
        pinned(d0),
        pinned(d1),
        pinned(summed),
        features,
        cotangent,
        degree,
        w_self,
        w_neigh,
        bias,
    )


def beside(d0_ref, d1_ref, slab):
    return jnp.concatenate(
        [jnp.concatenate([d[slab], d[slab + 1]], axis=1) for d in (d0_ref, d1_ref)], axis=0
    )


def back_kernel(first, n, st_ref, d0_ref, d1_ref, before_ref, out_ref):
    for c in range(0, n, 2):
        product = nn_dot(st_ref[...], beside(d0_ref, d1_ref, first + c))
        out_ref[:, c * TILE : (c + 2) * TILE] = product.astype(jnp.bfloat16)


def back(first, n, scaled_t, d0, d1, before):
    width, rows = scaled_t.shape
    return pl.pallas_call(
        functools.partial(back_kernel, first, n),
        out_shape=jax.ShapeDtypeStruct((width, n * TILE), jnp.bfloat16),
        in_specs=[vspec()] * 3 + [pl.BlockSpec(memory_space=pl.ANY)],
        out_specs=vspec(),
        compiler_params=params(),
        cost_estimate=cost(1, 1),
    )(pinned(scaled_t), pinned(d0), pinned(d1), before)


def own_kernel(st_ref, d0_ref, d1_ref, gp_ref, ws_ref, before_ref, out_ref):
    for c in range(0, d0_ref.shape[0], 2):
        rows = slice(c * TILE, (c + 2) * TILE)
        product = nn_dot(st_ref[...], beside(d0_ref, d1_ref, c))
        out_ref[:, rows] = product + nt_dot(ws_ref[...], gp_ref[rows, :])


def own(scaled_t, d0, d1, grad_pre, w_self, before):
    width, rows = scaled_t.shape
    return pl.pallas_call(
        own_kernel,
        out_shape=VMEM((width, rows), jnp.float32),
        in_specs=[vspec()] * 5 + [pl.BlockSpec(memory_space=pl.ANY)],
        out_specs=vspec(),
        compiler_params=params(),
        cost_estimate=cost(1, 1),
    )(pinned(scaled_t), pinned(d0), pinned(d1), pinned(grad_pre), w_self, before)


def place_kernel(rounds, last, rows_ref, acc_ref, before_ref, *refs):
    returned, (out_ref, token_ref, listed) = refs[: len(rounds)], refs[len(rounds) :]
    token_ref[...] = jnp.zeros_like(token_ref)
    step, boundary = 2 * TILE, rows_ref.shape[1]
    for place, r in enumerate(rounds):
        for k in range(0, boundary, TILE):
            line = rows_ref[r : r + 1, k : k + TILE].astype(jnp.float32)
            listed[place, k : k + TILE, :] = jnp.broadcast_to(line, (TILE, TILE)).T
    numbers = lax.broadcasted_iota(jnp.int32, (boundary, TILE), 1).astype(jnp.float32)
    for j in range(0, acc_ref.shape[1], step):
        total = acc_ref[:, j : j + step]
        for place, got_ref in enumerate(returned):
            table = jnp.concatenate(
                [
                    jnp.where(listed[place] == numbers + float(n), 1.0, 0.0).astype(jnp.bfloat16)
                    for n in range(j, j + step, TILE)
                ],
                axis=1,
            )
            total = total + nn_dot(got_ref[...], table)
        if last:
            out_ref[j : j + step, :] = total.T
        else:
            out_ref[:, j : j + step] = total


def place_rows(rounds, last, send_rows, acc, returned, before):
    width, rows = acc.shape
    count, boundary = len(rounds), send_rows.shape[1]
    if last:
        out = jax.ShapeDtypeStruct((rows, width), jnp.float32)
    else:
        out = VMEM((width, rows), jnp.float32)
    return pl.pallas_call(
        functools.partial(place_kernel, rounds, last),
        out_shape=[out, VMEM((8, TILE), jnp.float32)],
        in_specs=[vspec()] * 2 + [pl.BlockSpec(memory_space=pl.ANY)] + [vspec()] * count,
        out_specs=[vspec()] * 2,
        scratch_shapes=[VMEM((count, boundary, TILE), jnp.float32)],
        compiler_params=params(),
        cost_estimate=cost(1, 1),
    )(send_rows, pinned(acc), before, *returned)


def add_kernel(left_ref, right_ref, before_ref, out_ref):
    out_ref[...] = left_ref[...] + right_ref[...]


def added(left, right, before):
    return pl.pallas_call(
        add_kernel,
        out_shape=VMEM(left.shape, jnp.float32),
        in_specs=[vspec()] * 2 + [pl.BlockSpec(memory_space=pl.ANY)],
        out_specs=vspec(),
        compiler_params=params(1024 * 1024),
        cost_estimate=cost(1, 1),
    )(pinned(left), right, before)


def halves_kernel(scale, total_ref, other_ref, self_ref, neigh_ref):
    core = lax.axis_index("dom") & 1
    total, other = total_ref[...], other_ref[...]
    self_ref[...] = jnp.where(core == 0, total, other) * scale
    neigh_ref[...] = jnp.where(core == 0, other, total) * scale


def halves(scale, total, other):
    out = jax.ShapeDtypeStruct(total.shape, jnp.float32)
    return pl.pallas_call(
        functools.partial(halves_kernel, scale),
        out_shape=[out, out],
        in_specs=[vspec()] * 2,
        out_specs=[vspec()] * 2,
        compiler_params=params(1024 * 1024),
        cost_estimate=cost(2 * total.size, 4 * total.size * 4),
    )(pinned(total), other)


def swapped(shard, mask):
    return lax.ppermute(shard, "dom", [(i, i ^ mask) for i in range(lax.axis_size("dom"))])


def local(
    node_features,
    w_self,
    w_neigh,
    output_bias,
    local_tiles,
    halo_tiles,
    local_cols,
    halo_cols,
    send_rows,
    degree,
    cotangent,
):
    row_count, width = node_features.shape
    nblocks = local_tiles.shape[0]
    round_count, boundary = send_rows.shape
    per = boundary // TILE
    picked = pick_rows(send_rows, node_features)
    received = [swapped(rows, 1 << r) for r, rows in enumerate(picked)]
    dl0, dl1, dh0, dh1 = densify(
        local_cols, halo_cols, local_tiles, halo_tiles, round_count * per
    )
    summed = local_sums(dl0, dl1, node_features)
    output, grad_pre, scaled_t, mine, give = middle(
        received,
        dh0,
        dh1,
        summed,
        node_features,
        cotangent,
        degree.reshape(nblocks, TILE),
        w_self,
        w_neigh,
        output_bias.reshape(1, width),
    )
    returned = {}

    def send_back(r, before):
        grads = back(r * per, per, scaled_t, dh0, dh1, before)
        returned[r] = swapped(grads, 1 << r)
        return grads

    def place(rounds, acc, before):
        got = [returned[r] for r in rounds]
        return place_rows(rounds, 0 in rounds, send_rows, acc, got, before)

    other = swapped(give, 1)
    last = send_back(2, scaled_t)
    total = added(mine, other, last)
    other = swapped(total, 32)
    last = send_back(4, total)
    total = added(total, other, last)
    other = swapped(total, 96)
    last = send_back(1, total)
    last = send_back(3, last)
    total = added(total, other, last)
    other = swapped(total, 8)
    last = send_back(0, total)
    grads_t = own(scaled_t, dl0, dl1, grad_pre, w_self, last)
    total = added(total, other, grads_t)
    other = swapped(total, 24)
    grads_t, last = place((2, 4), grads_t, total)
    total = added(total, other, last)
    other = swapped(total, 2)
    grads_t, last = place((3, 1), grads_t, total)
    total = added(total, other, last)
    other = swapped(total, 6)
    grads, last = place((0,), grads_t, total)
    total = added(total, other, last)
    other = swapped(total, 1)
    grad_scale = 1.0 / math.sqrt(row_count * lax.axis_size("dom"))
    grad_self, grad_neigh = halves(grad_scale, total, other)
    return (output, grads, grad_self, grad_neigh)


def solution(mesh):
    in_specs = (
        P("dom", None),
        P(),
        P(),
        P(),
        P("dom", None, None, None),
        P("dom", None, None, None),
        P("dom", None),
        P("dom", None),
        P("dom", None),
        P("dom"),
        P("dom", None),
    )
    out_specs = (P("dom", None), P("dom", None), P(), P())
    return jax.shard_map(local, mesh=mesh, in_specs=in_specs, out_specs=out_specs, check_vma=False)
```

```python
import functools
import math

import jax
import jax.numpy as jnp
from jax import lax
from jax.experimental import pallas as pl
from jax.experimental.pallas import tpu as pltpu
from jax.sharding import PartitionSpec as P

TILE = 128
VMEM = pltpu.VMEM
LIMIT = 8 * 1024 * 1024


def vspec():
    return pl.BlockSpec(memory_space=VMEM)


def sspec():
    return pl.BlockSpec(memory_space=pltpu.SMEM)


def params(limit=LIMIT):
    return pltpu.CompilerParams(vmem_limit_bytes=limit)


def in_hbm(array):
    return pltpu.with_memory_space_constraint(array, pltpu.HBM)


def cost(flops, size, transcendentals=0):
    return pl.CostEstimate(flops=flops, bytes_accessed=size, transcendentals=transcendentals)


def pinned(array):
    return pltpu.with_memory_space_constraint(array, VMEM)


def nt_dot(left, right):
    return lax.dot_general(
        left, right, (((1,), (1,)), ((), ())), preferred_element_type=jnp.float32
    )


def nn_dot(left, right):
    return jnp.dot(left, right, preferred_element_type=jnp.float32)


def pick_kernel(rows_hbm, x_hbm, *refs):
    outs, (rows_ref, x_ref, xt_ref, rows_sem, x_sem) = refs[:-5], refs[-5:]
    rounds = len(outs)
    rows_copy = pltpu.make_async_copy(rows_hbm, rows_ref, rows_sem)
    x_copy = pltpu.make_async_copy(x_hbm, x_ref, x_sem)
    rows_copy.start()
    x_copy.start()
    rows_copy.wait()
    count, step = x_ref.shape[0], 2 * TILE
    numbers = lax.broadcasted_iota(jnp.int32, (count, step), 0)
    for r in range(rounds):
        for k in range(0, rows_ref.shape[1], step):
            listed = rows_ref[r : r + 1, k : k + step]
            table = jnp.where(numbers == listed, 1.0, 0.0).astype(jnp.bfloat16)
            if r == 0 and k == 0:
                x_copy.wait()
                for i in range(0, count, TILE):
                    xt_ref[:, i : i + TILE] = x_ref[i : i + TILE, :].T
            outs[r][:, k : k + step] = nn_dot(xt_ref[...], table).astype(jnp.bfloat16)


def pick_rows(send_rows, features):
    rows, width = features.shape
    rounds, boundary = send_rows.shape
    outs = [jax.ShapeDtypeStruct((width, boundary), jnp.bfloat16) for _ in range(rounds)]
    return pl.pallas_call(
        pick_kernel,
        out_shape=outs,
        in_specs=[pl.BlockSpec(memory_space=pltpu.HBM)] * 2,
        out_specs=[vspec()] * len(outs),
        scratch_shapes=[
            VMEM(send_rows.shape, jnp.int32),
            VMEM(features.shape, jnp.bfloat16),
            VMEM((width, rows), jnp.bfloat16),
            pltpu.SemaphoreType.DMA,
            pltpu.SemaphoreType.DMA,
        ],
        compiler_params=params(),
        cost_estimate=cost(2 * rows * boundary * rounds * width, 1_000_000),
    )(in_hbm(send_rows), in_hbm(features))


def densify_kernel(
    lc_hbm, hc_hbm, lt, ht, dl0, dl1, dh0, dh1, lslots, hslots, zeros, lc, hc, sems, zsems, csems
):
    half = lt.shape[0] // 2
    depth = lslots.shape[0]
    dense = (dl0, dl1, dh0, dh1)

    def fetch(i, slot):
        return [
            pltpu.make_async_copy(
                src.at[i + p * half], dst.at[slot, p], sems.at[slot, 2 * q + p]
            )
            for q, (src, dst) in enumerate(((lt, lslots), (ht, hslots)))
            for p in range(2)
        ]

    def clear(i, slot):
        rows = pl.ds(pl.multiple_of(i * TILE, TILE), TILE)
        return [
            pltpu.make_async_copy(
                zeros.at[pl.ds(0, d.shape[0])], d.at[:, rows, :], zsems.at[slot, k]
            )
            for k, d in enumerate(dense)
        ]

    for d in range(depth - 1):
        for copy in fetch(d, d):
            copy.start()
    columns = [
        pltpu.make_async_copy(lc_hbm, lc, csems.at[0]),
        pltpu.make_async_copy(hc_hbm, hc, csems.at[1]),
    ]
    for copy in columns:
        copy.start()
    zeros[...] = jnp.zeros_like(zeros)
    for copy in clear(0, 0):
        copy.start()
    for copy in columns:
        copy.wait()

    def body(i, carry):
        slot, zslot = lax.rem(i, depth), lax.rem(i, 2)

        @pl.when(i + depth - 1 < half)
        def _():
            for copy in fetch(i + depth - 1, lax.rem(i + depth - 1, depth)):
                copy.start()

        @pl.when(i + 1 < half)
        def _():
            for copy in clear(i + 1, 1 - zslot):
                copy.start()

        for copy in clear(i, zslot):
            copy.wait()
        for copy in fetch(i, slot):
            copy.wait()
        rows = pl.ds(pl.multiple_of(i * TILE, TILE), TILE)
        for t in range(max(lt.shape[1], ht.shape[1])):
            jobs = []
            if t < lt.shape[1]:
                jobs += [(dl0, lc[i, t], lslots, 0), (dl1, lc[i + half, t], lslots, 1)]
            if t < ht.shape[1]:
                jobs += [(dh0, hc[i, t], hslots, 0), (dh1, hc[i + half, t], hslots, 1)]
            sums = [d[c, rows, :] + s[slot, p, t] for d, c, s, p in jobs]
            for (d, c, _, _), total in zip(jobs, sums):
                d[c, rows, :] = total
        return carry

    lax.fori_loop(0, half, body, 0)


def densify(local_cols, halo_cols, local_tiles, halo_tiles, halo_blocks):
    nblocks, local_count = local_cols.shape
    halo_count = halo_cols.shape[1]
    half = nblocks // 2 * TILE
    depth = 3
    slabs = (nblocks, nblocks, halo_blocks, halo_blocks)
    return pl.pallas_call(
        densify_kernel,
        out_shape=[VMEM((n, half, TILE), jnp.bfloat16) for n in slabs],
        in_specs=[pl.BlockSpec(memory_space=pltpu.HBM)] * 4,
        out_specs=[vspec()] * 4,
        scratch_shapes=[
            VMEM((depth, 2, local_count, TILE, TILE), jnp.bfloat16),
            VMEM((depth, 2, halo_count, TILE, TILE), jnp.bfloat16),
            VMEM((max(slabs), TILE, TILE), jnp.bfloat16),
            pltpu.SMEM(local_cols.shape, jnp.int32),
            pltpu.SMEM(halo_cols.shape, jnp.int32),
            pltpu.SemaphoreType.DMA((depth, 4)),
            pltpu.SemaphoreType.DMA((2, 4)),
            pltpu.SemaphoreType.DMA((2,)),
        ],
        compiler_params=params(12 * 1024 * 1024),
        cost_estimate=cost(16_000_000, nblocks * (local_count + halo_count) * TILE * TILE * 2),
    )(in_hbm(local_cols), in_hbm(halo_cols), in_hbm(local_tiles), in_hbm(halo_tiles))


def local_sums_kernel(d0_ref, d1_ref, x_ref, out_ref):
    half, step = d0_ref.shape[1], 512
    for p, dense_ref in enumerate((d0_ref, d1_ref)):
        for j in range(0, half, step):
            left = jnp.concatenate(
                [dense_ref[c, j : j + step, :] for c in range(dense_ref.shape[0])], axis=1
            )
            out_ref[p * half + j : p * half + j + step, :] = nn_dot(left, x_ref[...])


def local_sums(d0, d1, features):
    rows, width = features.shape
    return pl.pallas_call(
        local_sums_kernel,
        out_shape=VMEM((rows, width), jnp.float32),
        in_specs=[vspec()] * 3,
        out_specs=vspec(),
        compiler_params=params(),
        cost_estimate=cost(2 * rows * rows * width, 1_500_000),
    )(pinned(d0), pinned(d1), features)


def middle_kernel(rounds, *refs):
    got, refs = refs[:rounds], refs[rounds:]
    d0, d1, sum_ref, x_ref, ct_ref, deg_ref, ws_ref, wn_ref, bias_ref = refs[:9]
    out_ref, gp_ref, st_ref, parts_ref, both, halo, sums = refs[9:]
    half, step = d0.shape[1], 512
    boundary = got[0].shape[1]
    per = boundary // TILE
    for r in range(rounds):
        halo[r * boundary : (r + 1) * boundary, :] = got[r][...].T
    for p, dense_ref in enumerate((d0, d1)):
        for j in range(0, half, step):
            start = p * half + j
            total = sum_ref[start : start + step, :]
            for r in range(rounds):
                left = jnp.concatenate(
                    [dense_ref[c, j : j + step, :] for c in range(r * per, (r + 1) * per)], axis=1
                )
                total = total + nn_dot(left, halo[r * boundary : (r + 1) * boundary, :])
            sums[start : start + step, :] = total
    for start in range(0, 2 * half, step):
        total = sums[start : start + step, :]
        for i in range(start // TILE, (start + step) // TILE):
            rows = slice(i * TILE, (i + 1) * TILE)
            line = deg_ref[i : i + 1, :].astype(jnp.float32)
            column = jnp.broadcast_to(line, (TILE, TILE)).T
            agg = total[i * TILE - start : (i + 1) * TILE - start, :] / column
            agg = agg.astype(jnp.bfloat16)
            both[rows, :TILE] = x_ref[rows, :]
            both[rows, TILE:] = agg
            preact = nn_dot(x_ref[rows, :], ws_ref[...]) + nn_dot(agg, wn_ref[...])
            preact = preact + bias_ref[...]
            sig = jax.nn.sigmoid(preact)
            out_ref[rows, :] = (preact * sig).astype(jnp.bfloat16)
            grad = ct_ref[rows, :].astype(jnp.float32) * sig * (1.0 + preact * (1.0 - sig))
            grad = grad.astype(jnp.bfloat16)
            gp_ref[rows, :] = grad
            st_ref[:, rows] = (nt_dot(wn_ref[...], grad) / line).astype(jnp.bfloat16)
    parts_ref[...] = lax.dot_general(
        both[...], gp_ref[...], (((0,), (0,)), ((), ())), preferred_element_type=jnp.float32
    )


def middle(received, d0, d1, summed, features, cotangent, degree, w_self, w_neigh, bias):
    rows, width = features.shape
    rounds, boundary = len(received), received[0].shape[1]
    half = jax.ShapeDtypeStruct((rows, width), jnp.bfloat16)
    return pl.pallas_call(
        functools.partial(middle_kernel, rounds),
        out_shape=[
            half,
            VMEM((rows, width), jnp.bfloat16),
            VMEM((width, rows), jnp.bfloat16),
            VMEM((2 * width, width), jnp.float32),
        ],
        in_specs=[vspec()] * (rounds + 9),
        out_specs=[vspec()] * 4,
        scratch_shapes=[
            VMEM((rows, 2 * width), jnp.bfloat16),
            VMEM((rounds * boundary, width), jnp.bfloat16),
            VMEM((rows, width), jnp.float32),
        ],
        compiler_params=params(),
        cost_estimate=cost(2 * rows * rounds * boundary * width, 5_000_000, rows * width),
    )(
        *received,
        pinned(d0),
        pinned(d1),
        pinned(summed),
        features,
        cotangent,
        degree,
        w_self,
        w_neigh,
        bias,
    )


def beside(d0_ref, d1_ref, slab):
    return jnp.concatenate(
        [jnp.concatenate([d[slab], d[slab + 1]], axis=1) for d in (d0_ref, d1_ref)], axis=0
    )


def back_kernel(first, n, st_ref, d0_ref, d1_ref, before_ref, out_ref):
    for c in range(0, n, 2):
        product = nn_dot(st_ref[...], beside(d0_ref, d1_ref, first + c))
        out_ref[:, c * TILE : (c + 2) * TILE] = product.astype(jnp.bfloat16)


def back(first, n, scaled_t, d0, d1, before):
    width, rows = scaled_t.shape
    return pl.pallas_call(
        functools.partial(back_kernel, first, n),
        out_shape=jax.ShapeDtypeStruct((width, n * TILE), jnp.bfloat16),
        in_specs=[vspec()] * 3 + [pl.BlockSpec(memory_space=pl.ANY)],
        out_specs=vspec(),
        compiler_params=params(),
        cost_estimate=cost(1, 1),
    )(pinned(scaled_t), pinned(d0), pinned(d1), before)


def own_kernel(st_ref, d0_ref, d1_ref, gp_ref, ws_ref, before_ref, out_ref):
    for c in range(0, d0_ref.shape[0], 2):
        rows = slice(c * TILE, (c + 2) * TILE)
        product = nn_dot(st_ref[...], beside(d0_ref, d1_ref, c))
        out_ref[:, rows] = product + nt_dot(ws_ref[...], gp_ref[rows, :])


def own(scaled_t, d0, d1, grad_pre, w_self, before):
    width, rows = scaled_t.shape
    return pl.pallas_call(
        own_kernel,
        out_shape=VMEM((width, rows), jnp.float32),
        in_specs=[vspec()] * 5 + [pl.BlockSpec(memory_space=pl.ANY)],
        out_specs=vspec(),
        compiler_params=params(),
        cost_estimate=cost(1, 1),
    )(pinned(scaled_t), pinned(d0), pinned(d1), pinned(grad_pre), w_self, before)


def place_kernel(rounds, last, rows_ref, acc_ref, before_ref, *refs):
    returned, (out_ref, token_ref, listed) = refs[: len(rounds)], refs[len(rounds) :]
    token_ref[...] = jnp.zeros_like(token_ref)
    step, boundary = 2 * TILE, rows_ref.shape[1]
    for place, r in enumerate(rounds):
        for k in range(0, boundary, TILE):
            line = rows_ref[r : r + 1, k : k + TILE].astype(jnp.float32)
            listed[place, k : k + TILE, :] = jnp.broadcast_to(line, (TILE, TILE)).T
    numbers = lax.broadcasted_iota(jnp.int32, (boundary, TILE), 1).astype(jnp.float32)
    for j in range(0, acc_ref.shape[1], step):
        total = acc_ref[:, j : j + step]
        for place, got_ref in enumerate(returned):
            table = jnp.concatenate(
                [
                    jnp.where(listed[place] == numbers + float(n), 1.0, 0.0).astype(jnp.bfloat16)
                    for n in range(j, j + step, TILE)
                ],
                axis=1,
            )
            total = total + nn_dot(got_ref[...], table)
        if last:
            out_ref[j : j + step, :] = total.T
        else:
            out_ref[:, j : j + step] = total


def place_rows(rounds, last, send_rows, acc, returned, before):
    width, rows = acc.shape
    count, boundary = len(rounds), send_rows.shape[1]
    if last:
        out = jax.ShapeDtypeStruct((rows, width), jnp.float32)
    else:
        out = VMEM((width, rows), jnp.float32)
    return pl.pallas_call(
        functools.partial(place_kernel, rounds, last),
        out_shape=[out, VMEM((8, TILE), jnp.float32)],
        in_specs=[vspec()] * 2 + [pl.BlockSpec(memory_space=pl.ANY)] + [vspec()] * count,
        out_specs=[vspec()] * 2,
        scratch_shapes=[VMEM((count, boundary, TILE), jnp.float32)],
        compiler_params=params(),
        cost_estimate=cost(1, 1),
    )(send_rows, pinned(acc), before, *returned)


def add_kernel(left_ref, right_ref, before_ref, out_ref):
    out_ref[...] = left_ref[...] + right_ref[...]


def added(left, right, before):
    return pl.pallas_call(
        add_kernel,
        out_shape=VMEM(left.shape, jnp.float32),
        in_specs=[vspec()] * 2 + [pl.BlockSpec(memory_space=pl.ANY)],
        out_specs=vspec(),
        compiler_params=params(1024 * 1024),
        cost_estimate=cost(1, 1),
    )(pinned(left), right, before)


def split_kernel(scale, total_ref, other_ref, self_ref, neigh_ref):
    core = lax.axis_index("dom") & 1
    width = self_ref.shape[0]
    total = jnp.where(core == 1, total_ref[...], other_ref[...]) * scale
    self_ref[...] = total[:width]
    neigh_ref[...] = total[width:]


def split(scale, total, other):
    rows, width = total.shape
    out = jax.ShapeDtypeStruct((rows // 2, width), jnp.float32)
    return pl.pallas_call(
        functools.partial(split_kernel, scale),
        out_shape=[out, out],
        in_specs=[vspec()] * 2,
        out_specs=[vspec()] * 2,
        compiler_params=params(1024 * 1024),
        cost_estimate=cost(1, 1),
    )(pinned(total), other)


def swapped(shard, mask):
    return lax.ppermute(shard, "dom", [(i, i ^ mask) for i in range(lax.axis_size("dom"))])


def swapped_from(core, shard, mask):
    senders = range(core, lax.axis_size("dom"), 2)
    return lax.ppermute(shard, "dom", [(i, i ^ mask) for i in senders])


def local(
    node_features,
    w_self,
    w_neigh,
    output_bias,
    local_tiles,
    halo_tiles,
    local_cols,
    halo_cols,
    send_rows,
    degree,
    cotangent,
):
    row_count, width = node_features.shape
    nblocks = local_tiles.shape[0]
    round_count, boundary = send_rows.shape
    per = boundary // TILE
    picked = pick_rows(send_rows, node_features)
    received = [swapped(rows, 1 << r) for r, rows in enumerate(picked)]
    dl0, dl1, dh0, dh1 = densify(
        local_cols, halo_cols, local_tiles, halo_tiles, round_count * per
    )
    summed = local_sums(dl0, dl1, node_features)
    output, grad_pre, scaled_t, parts = middle(
        received,
        dh0,
        dh1,
        summed,
        node_features,
        cotangent,
        degree.reshape(nblocks, TILE),
        w_self,
        w_neigh,
        output_bias.reshape(1, width),
    )
    returned = {}

    def send_back(r, before):
        grads = back(r * per, per, scaled_t, dh0, dh1, before)
        returned[r] = swapped(grads, 1 << r)
        return grads

    def place(rounds, acc, before):
        got = [returned[r] for r in rounds]
        return place_rows(rounds, 0 in rounds, send_rows, acc, got, before)

    other = swapped_from(0, parts, 1)
    last = send_back(2, scaled_t)
    total = added(parts, other, last)
    other = swapped_from(1, total, 32)
    last = send_back(4, total)
    total = added(total, other, last)
    other = swapped_from(1, total, 96)
    last = send_back(1, total)
    last = send_back(3, last)
    total = added(total, other, last)
    other = swapped_from(1, total, 8)
    last = send_back(0, total)
    grads_t = own(scaled_t, dl0, dl1, grad_pre, w_self, last)
    total = added(total, other, grads_t)
    other = swapped_from(1, total, 24)
    grads_t, last = place((2, 4), grads_t, total)
    total = added(total, other, last)
    other = swapped_from(1, total, 2)
    grads_t, last = place((3, 1), grads_t, total)
    total = added(total, other, last)
    other = swapped_from(1, total, 6)
    grads, last = place((0,), grads_t, total)
    total = added(total, other, last)
    other = swapped_from(1, total, 1)
    grad_scale = 1.0 / math.sqrt(row_count * lax.axis_size("dom"))
    grad_self, grad_neigh = split(grad_scale, total, other)
    return (output, grads, grad_self, grad_neigh)


def solution(mesh):
    in_specs = (
        P("dom", None),
        P(),
        P(),
        P(),
        P("dom", None, None, None),
        P("dom", None, None, None),
        P("dom", None),
        P("dom", None),
        P("dom", None),
        P("dom"),
        P("dom", None),
    )
    out_specs = (P("dom", None), P("dom", None), P(), P())
    return jax.shard_map(local, mesh=mesh, in_specs=in_specs, out_specs=out_specs, check_vma=False)
```

```python
import functools
import math

import jax
import jax.numpy as jnp
from jax import lax
from jax.experimental import pallas as pl
from jax.experimental.pallas import tpu as pltpu
from jax.sharding import PartitionSpec as P

TILE = 128
VMEM = pltpu.VMEM
LIMIT = 8 * 1024 * 1024


def vspec():
    return pl.BlockSpec(memory_space=VMEM)


def sspec():
    return pl.BlockSpec(memory_space=pltpu.SMEM)


def params(limit=LIMIT):
    return pltpu.CompilerParams(vmem_limit_bytes=limit)


def in_hbm(array):
    return pltpu.with_memory_space_constraint(array, pltpu.HBM)


def cost(flops, size, transcendentals=0):
    return pl.CostEstimate(flops=flops, bytes_accessed=size, transcendentals=transcendentals)


def pinned(array):
    return pltpu.with_memory_space_constraint(array, VMEM)


def nt_dot(left, right):
    return lax.dot_general(
        left, right, (((1,), (1,)), ((), ())), preferred_element_type=jnp.float32
    )


def nn_dot(left, right):
    return jnp.dot(left, right, preferred_element_type=jnp.float32)


def pick_kernel(rows_hbm, x_hbm, tiles_hbm, *refs):
    outs, (tiles_ref, rows_ref, x_ref, xt_ref, rows_sem, x_sem, tiles_sem) = refs[:-7], refs[-7:]
    rounds = len(outs)
    tiles_copy = pltpu.make_async_copy(tiles_hbm, tiles_ref, tiles_sem)
    rows_copy = pltpu.make_async_copy(rows_hbm, rows_ref, rows_sem)
    x_copy = pltpu.make_async_copy(x_hbm, x_ref, x_sem)
    rows_copy.start()
    x_copy.start()
    tiles_copy.start()
    rows_copy.wait()
    count, step = x_ref.shape[0], 2 * TILE
    numbers = lax.broadcasted_iota(jnp.int32, (count, step), 0)
    for r in range(rounds):
        for k in range(0, rows_ref.shape[1], step):
            listed = rows_ref[r : r + 1, k : k + step]
            table = jnp.where(numbers == listed, 1.0, 0.0).astype(jnp.bfloat16)
            if r == 0 and k == 0:
                x_copy.wait()
                for i in range(0, count, TILE):
                    xt_ref[:, i : i + TILE] = x_ref[i : i + TILE, :].T
            outs[r][:, k : k + step] = nn_dot(xt_ref[...], table).astype(jnp.bfloat16)
    tiles_copy.wait()


def pick_rows(send_rows, features, tiles):
    rows, width = features.shape
    rounds, boundary = send_rows.shape
    outs = [jax.ShapeDtypeStruct((width, boundary), jnp.bfloat16) for _ in range(rounds)]
    outs.append(VMEM(tiles.shape, tiles.dtype))
    return pl.pallas_call(
        pick_kernel,
        out_shape=outs,
        in_specs=[pl.BlockSpec(memory_space=pltpu.HBM)] * 3,
        out_specs=[vspec()] * len(outs),
        scratch_shapes=[
            VMEM(send_rows.shape, jnp.int32),
            VMEM(features.shape, jnp.bfloat16),
            VMEM((width, rows), jnp.bfloat16),
            pltpu.SemaphoreType.DMA,
            pltpu.SemaphoreType.DMA,
            pltpu.SemaphoreType.DMA,
        ],
        compiler_params=params(),
        cost_estimate=cost(2 * rows * boundary * rounds * width, 1_000_000),
    )(in_hbm(send_rows), in_hbm(features), in_hbm(tiles))


def densify_kernel(
    lc_hbm, hc_hbm, lt, ht, dl0, dl1, dh0, dh1, hslots, zeros, lc, hc, sems, zsems, csems
):
    half = lt.shape[0] // 2
    depth = hslots.shape[0]
    dense = (dl0, dl1, dh0, dh1)

    def fetch(i, slot):
        return [
            pltpu.make_async_copy(ht.at[i + p * half], hslots.at[slot, p], sems.at[slot, p])
            for p in range(2)
        ]

    def clear(i, slot):
        rows = pl.ds(pl.multiple_of(i * TILE, TILE), TILE)
        return [
            pltpu.make_async_copy(
                zeros.at[pl.ds(0, d.shape[0])], d.at[:, rows, :], zsems.at[slot, k]
            )
            for k, d in enumerate(dense)
        ]

    for d in range(depth - 1):
        for copy in fetch(d, d):
            copy.start()
    columns = [
        pltpu.make_async_copy(lc_hbm, lc, csems.at[0]),
        pltpu.make_async_copy(hc_hbm, hc, csems.at[1]),
    ]
    for copy in columns:
        copy.start()
    zeros[...] = jnp.zeros_like(zeros)
    for copy in clear(0, 0):
        copy.start()
    for copy in columns:
        copy.wait()

    def body(i, carry):
        slot, zslot = lax.rem(i, depth), lax.rem(i, 2)

        @pl.when(i + depth - 1 < half)
        def _():
            for copy in fetch(i + depth - 1, lax.rem(i + depth - 1, depth)):
                copy.start()

        @pl.when(i + 1 < half)
        def _():
            for copy in clear(i + 1, 1 - zslot):
                copy.start()

        for copy in clear(i, zslot):
            copy.wait()
        for copy in fetch(i, slot):
            copy.wait()
        rows = pl.ds(pl.multiple_of(i * TILE, TILE), TILE)
        for t in range(max(lt.shape[1], ht.shape[1])):
            jobs = []
            if t < lt.shape[1]:
                jobs += [(dl0, lc[i, t], lt[i, t]), (dl1, lc[i + half, t], lt[i + half, t])]
            if t < ht.shape[1]:
                jobs += [
                    (dh0, hc[i, t], hslots[slot, 0, t]),
                    (dh1, hc[i + half, t], hslots[slot, 1, t]),
                ]
            sums = [d[c, rows, :] + tile for d, c, tile in jobs]
            for (d, c, _), total in zip(jobs, sums):
                d[c, rows, :] = total
        return carry

    lax.fori_loop(0, half, body, 0)


def densify(local_cols, halo_cols, local_tiles, halo_tiles, halo_blocks):
    nblocks, local_count = local_cols.shape
    halo_count = halo_cols.shape[1]
    half = nblocks // 2 * TILE
    depth = 3
    slabs = (nblocks, nblocks, halo_blocks, halo_blocks)
    return pl.pallas_call(
        densify_kernel,
        out_shape=[VMEM((n, half, TILE), jnp.bfloat16) for n in slabs],
        in_specs=[pl.BlockSpec(memory_space=pltpu.HBM)] * 2
        + [vspec(), pl.BlockSpec(memory_space=pltpu.HBM)],
        out_specs=[vspec()] * 4,
        scratch_shapes=[
            VMEM((depth, 2, halo_count, TILE, TILE), jnp.bfloat16),
            VMEM((max(slabs), TILE, TILE), jnp.bfloat16),
            pltpu.SMEM(local_cols.shape, jnp.int32),
            pltpu.SMEM(halo_cols.shape, jnp.int32),
            pltpu.SemaphoreType.DMA((depth, 2)),
            pltpu.SemaphoreType.DMA((2, 4)),
            pltpu.SemaphoreType.DMA((2,)),
        ],
        compiler_params=params(8 * 1024 * 1024),
        cost_estimate=cost(16_000_000, nblocks * (local_count + halo_count) * TILE * TILE * 2),
    )(in_hbm(local_cols), in_hbm(halo_cols), pinned(local_tiles), in_hbm(halo_tiles))


def local_sums_kernel(d0_ref, d1_ref, x_ref, out_ref):
    half, step = d0_ref.shape[1], 512
    for p, dense_ref in enumerate((d0_ref, d1_ref)):
        for j in range(0, half, step):
            left = jnp.concatenate(
                [dense_ref[c, j : j + step, :] for c in range(dense_ref.shape[0])], axis=1
            )
            out_ref[p * half + j : p * half + j + step, :] = nn_dot(left, x_ref[...])


def local_sums(d0, d1, features):
    rows, width = features.shape
    return pl.pallas_call(
        local_sums_kernel,
        out_shape=VMEM((rows, width), jnp.float32),
        in_specs=[vspec()] * 3,
        out_specs=vspec(),
        compiler_params=params(),
        cost_estimate=cost(2 * rows * rows * width, 1_500_000),
    )(pinned(d0), pinned(d1), features)


def middle_kernel(rounds, *refs):
    got, refs = refs[:rounds], refs[rounds:]
    d0, d1, sum_ref, x_ref, ct_ref, deg_ref, ws_ref, wn_ref, bias_ref = refs[:9]
    out_ref, gp_ref, st_ref, mine_ref, give_ref, both, halo, sums = refs[9:]
    core = lax.axis_index("dom") & 1
    half, step = d0.shape[1], 512
    boundary = got[0].shape[1]
    per = boundary // TILE
    for r in range(rounds):
        halo[r * boundary : (r + 1) * boundary, :] = got[r][...].T
    for p, dense_ref in enumerate((d0, d1)):
        for j in range(0, half, step):
            start = p * half + j
            total = sum_ref[start : start + step, :]
            for r in range(rounds):
                left = jnp.concatenate(
                    [dense_ref[c, j : j + step, :] for c in range(r * per, (r + 1) * per)], axis=1
                )
                total = total + nn_dot(left, halo[r * boundary : (r + 1) * boundary, :])
            sums[start : start + step, :] = total
    for start in range(0, 2 * half, step):
        total = sums[start : start + step, :]
        for i in range(start // TILE, (start + step) // TILE):
            rows = slice(i * TILE, (i + 1) * TILE)
            line = deg_ref[i : i + 1, :].astype(jnp.float32)
            column = jnp.broadcast_to(line, (TILE, TILE)).T
            agg = total[i * TILE - start : (i + 1) * TILE - start, :] / column
            agg = agg.astype(jnp.bfloat16)
            both[rows, :TILE] = x_ref[rows, :]
            both[rows, TILE:] = agg
            preact = nn_dot(x_ref[rows, :], ws_ref[...]) + nn_dot(agg, wn_ref[...])
            preact = preact + bias_ref[...]
            sig = jax.nn.sigmoid(preact)
            out_ref[rows, :] = (preact * sig).astype(jnp.bfloat16)
            grad = ct_ref[rows, :].astype(jnp.float32) * sig * (1.0 + preact * (1.0 - sig))
            grad = grad.astype(jnp.bfloat16)
            gp_ref[rows, :] = grad
            st_ref[:, rows] = (nt_dot(wn_ref[...], grad) / line).astype(jnp.bfloat16)
    parts = lax.dot_general(
        both[...], gp_ref[...], (((0,), (0,)), ((), ())), preferred_element_type=jnp.float32
    )
    mine_ref[...] = jnp.where(core == 0, parts[:TILE], parts[TILE:])
    give_ref[...] = jnp.where(core == 0, parts[TILE:], parts[:TILE])


def middle(received, d0, d1, summed, features, cotangent, degree, w_self, w_neigh, bias):
    rows, width = features.shape
    rounds, boundary = len(received), received[0].shape[1]
    half = jax.ShapeDtypeStruct((rows, width), jnp.bfloat16)
    part = VMEM((width, width), jnp.float32)
    return pl.pallas_call(
        functools.partial(middle_kernel, rounds),
        out_shape=[
            half,
            VMEM((rows, width), jnp.bfloat16),
            VMEM((width, rows), jnp.bfloat16),
            part,
            part,
        ],
        in_specs=[vspec()] * (rounds + 9),
        out_specs=[vspec()] * 5,
        scratch_shapes=[
            VMEM((rows, 2 * width), jnp.bfloat16),
            VMEM((rounds * boundary, width), jnp.bfloat16),
            VMEM((rows, width), jnp.float32),
        ],
        compiler_params=params(),
        cost_estimate=cost(2 * rows * rounds * boundary * width, 5_000_000, rows * width),
    )(
        *received,
        pinned(d0),
        pinned(d1),
        pinned(summed),
        features,
        cotangent,
        degree,
        w_self,
        w_neigh,
        bias,
    )


def beside(d0_ref, d1_ref, slab):
    return jnp.concatenate(
        [jnp.concatenate([d[slab], d[slab + 1]], axis=1) for d in (d0_ref, d1_ref)], axis=0
    )


def back_kernel(first, n, st_ref, d0_ref, d1_ref, before_ref, out_ref):
    for c in range(0, n, 2):
        product = nn_dot(st_ref[...], beside(d0_ref, d1_ref, first + c))
        out_ref[:, c * TILE : (c + 2) * TILE] = product.astype(jnp.bfloat16)


def back(first, n, scaled_t, d0, d1, before):
    width, rows = scaled_t.shape
    return pl.pallas_call(
        functools.partial(back_kernel, first, n),
        out_shape=jax.ShapeDtypeStruct((width, n * TILE), jnp.bfloat16),
        in_specs=[vspec()] * 3 + [pl.BlockSpec(memory_space=pl.ANY)],
        out_specs=vspec(),
        compiler_params=params(),
        cost_estimate=cost(1, 1),
    )(pinned(scaled_t), pinned(d0), pinned(d1), before)


def own_kernel(st_ref, d0_ref, d1_ref, gp_ref, ws_ref, before_ref, out_ref):
    for c in range(0, d0_ref.shape[0], 2):
        rows = slice(c * TILE, (c + 2) * TILE)
        product = nn_dot(st_ref[...], beside(d0_ref, d1_ref, c))
        out_ref[:, rows] = product + nt_dot(ws_ref[...], gp_ref[rows, :])


def own(scaled_t, d0, d1, grad_pre, w_self, before):
    width, rows = scaled_t.shape
    return pl.pallas_call(
        own_kernel,
        out_shape=VMEM((width, rows), jnp.float32),
        in_specs=[vspec()] * 5 + [pl.BlockSpec(memory_space=pl.ANY)],
        out_specs=vspec(),
        compiler_params=params(),
        cost_estimate=cost(1, 1),
    )(pinned(scaled_t), pinned(d0), pinned(d1), pinned(grad_pre), w_self, before)


def place_kernel(rounds, last, rows_ref, acc_ref, before_ref, *refs):
    returned, (out_ref, token_ref, listed, *rest) = refs[: len(rounds)], refs[len(rounds) :]
    token_ref[...] = jnp.zeros_like(token_ref)
    step, boundary = 2 * TILE, rows_ref.shape[1]
    for place, r in enumerate(rounds):
        for k in range(0, boundary, TILE):
            line = rows_ref[r : r + 1, k : k + TILE].astype(jnp.float32)
            listed[place, k : k + TILE, :] = jnp.broadcast_to(line, (TILE, TILE)).T
    numbers = lax.broadcasted_iota(jnp.int32, (boundary, TILE), 1).astype(jnp.float32)
    copies = []
    for j in range(0, acc_ref.shape[1], step):
        total = acc_ref[:, j : j + step]
        for place, got_ref in enumerate(returned):
            table = jnp.concatenate(
                [
                    jnp.where(listed[place] == numbers + float(n), 1.0, 0.0).astype(jnp.bfloat16)
                    for n in range(j, j + step, TILE)
                ],
                axis=1,
            )
            total = total + nn_dot(got_ref[...], table)
        if last:
            ready, sems = rest
            ready[j : j + step, :] = total.T
            rows = pl.ds(j, step)
            copies.append(
                pltpu.make_async_copy(ready.at[rows], out_ref.at[rows], sems.at[j // step])
            )
            copies[-1].start()
        else:
            out_ref[:, j : j + step] = total
    for copy in copies:
        copy.wait()


def place_rows(rounds, last, send_rows, acc, returned, before):
    width, rows = acc.shape
    count, boundary = len(rounds), send_rows.shape[1]
    scratch = [VMEM((count, boundary, TILE), jnp.float32)]
    if last:
        out = jax.ShapeDtypeStruct((rows, width), jnp.float32)
        scratch += [VMEM((rows, width), jnp.float32)]
        scratch += [pltpu.SemaphoreType.DMA((rows // (2 * TILE),))]
    else:
        out = VMEM((width, rows), jnp.float32)
    return pl.pallas_call(
        functools.partial(place_kernel, rounds, last),
        out_shape=[out, VMEM((8, TILE), jnp.float32)],
        in_specs=[vspec()] * 2 + [pl.BlockSpec(memory_space=pl.ANY)] + [vspec()] * count,
        out_specs=[pl.BlockSpec(memory_space=pltpu.HBM) if last else vspec(), vspec()],
        scratch_shapes=scratch,
        compiler_params=params(),
        cost_estimate=cost(1, 1),
    )(send_rows, pinned(acc), before, *returned)


def add_kernel(left_ref, right_ref, before_ref, out_ref):
    out_ref[...] = left_ref[...] + right_ref[...]


def added(left, right, before):
    return pl.pallas_call(
        add_kernel,
        out_shape=VMEM(left.shape, jnp.float32),
        in_specs=[vspec()] * 2 + [pl.BlockSpec(memory_space=pl.ANY)],
        out_specs=vspec(),
        compiler_params=params(1024 * 1024),
        cost_estimate=cost(1, 1),
    )(pinned(left), right, before)


def halves_kernel(scale, total_ref, other_ref, self_ref, neigh_ref):
    core = lax.axis_index("dom") & 1
    total, other = total_ref[...], other_ref[...]
    self_ref[...] = jnp.where(core == 0, total, other) * scale
    neigh_ref[...] = jnp.where(core == 0, other, total) * scale


def halves(scale, total, other):
    out = jax.ShapeDtypeStruct(total.shape, jnp.float32)
    return pl.pallas_call(
        functools.partial(halves_kernel, scale),
        out_shape=[out, out],
        in_specs=[vspec()] * 2,
        out_specs=[vspec()] * 2,
        compiler_params=params(1024 * 1024),
        cost_estimate=cost(2 * total.size, 4 * total.size * 4),
    )(pinned(total), other)


def swapped(shard, mask):
    return lax.ppermute(shard, "dom", [(i, i ^ mask) for i in range(lax.axis_size("dom"))])


def local(
    node_features,
    w_self,
    w_neigh,
    output_bias,
    local_tiles,
    halo_tiles,
    local_cols,
    halo_cols,
    send_rows,
    degree,
    cotangent,
):
    row_count, width = node_features.shape
    nblocks = local_tiles.shape[0]
    round_count, boundary = send_rows.shape
    per = boundary // TILE
    *picked, near_tiles = pick_rows(send_rows, node_features, local_tiles)
    received = [swapped(rows, 1 << r) for r, rows in enumerate(picked)]
    dl0, dl1, dh0, dh1 = densify(
        local_cols, halo_cols, near_tiles, halo_tiles, round_count * per
    )
    summed = local_sums(dl0, dl1, node_features)
    output, grad_pre, scaled_t, mine, give = middle(
        received,
        dh0,
        dh1,
        summed,
        node_features,
        cotangent,
        degree.reshape(nblocks, TILE),
        w_self,
        w_neigh,
        output_bias.reshape(1, width),
    )
    returned = {}

    def send_back(r, before):
        grads = back(r * per, per, scaled_t, dh0, dh1, before)
        returned[r] = swapped(grads, 1 << r)
        return grads

    def place(rounds, acc, before):
        got = [returned[r] for r in rounds]
        return place_rows(rounds, 0 in rounds, send_rows, acc, got, before)

    other = swapped(give, 1)
    last = send_back(2, scaled_t)
    total = added(mine, other, last)
    other = swapped(total, 32)
    last = send_back(4, total)
    last = send_back(1, last)
    total = added(total, other, last)
    other = swapped(total, 96)
    last = send_back(3, total)
    last = send_back(0, last)
    total = added(total, other, last)
    other = swapped(total, 8)
    grads_t = own(scaled_t, dl0, dl1, grad_pre, w_self, total)
    total = added(total, other, grads_t)
    other = swapped(total, 24)
    grads_t, last = place((2,), grads_t, total)
    total = added(total, other, last)
    other = swapped(total, 2)
    grads_t, last = place((4, 3), grads_t, total)
    total = added(total, other, last)
    other = swapped(total, 6)
    grads_t, last = place((1,), grads_t, total)
    total = added(total, other, last)
    other = swapped(total, 1)
    grads, last = place((0,), grads_t, total)
    grad_scale = 1.0 / math.sqrt(row_count * lax.axis_size("dom"))
    grad_self, grad_neigh = halves(grad_scale, total, other)
    return (output, grads, grad_self, grad_neigh)


def solution(mesh):
    in_specs = (
        P("dom", None),
        P(),
        P(),
        P(),
        P("dom", None, None, None),
        P("dom", None, None, None),
        P("dom", None),
        P("dom", None),
        P("dom", None),
        P("dom"),
        P("dom", None),
    )
    out_specs = (P("dom", None), P("dom", None), P(), P())
    return jax.shard_map(local, mesh=mesh, in_specs=in_specs, out_specs=out_specs, check_vma=False)
```

```python
import functools
import math

import jax
import jax.numpy as jnp
from jax import lax
from jax.experimental import pallas as pl
from jax.experimental.pallas import tpu as pltpu
from jax.sharding import PartitionSpec as P

TILE = 128
VMEM = pltpu.VMEM
LIMIT = 8 * 1024 * 1024


def vspec():
    return pl.BlockSpec(memory_space=VMEM)


def sspec():
    return pl.BlockSpec(memory_space=pltpu.SMEM)


def params(limit=LIMIT):
    return pltpu.CompilerParams(vmem_limit_bytes=limit)


def in_hbm(array):
    return pltpu.with_memory_space_constraint(array, pltpu.HBM)


def cost(flops, size, transcendentals=0):
    return pl.CostEstimate(flops=flops, bytes_accessed=size, transcendentals=transcendentals)


def pinned(array):
    return pltpu.with_memory_space_constraint(array, VMEM)


def nt_dot(left, right):
    return lax.dot_general(
        left, right, (((1,), (1,)), ((), ())), preferred_element_type=jnp.float32
    )


def nn_dot(left, right):
    return jnp.dot(left, right, preferred_element_type=jnp.float32)


def pick_kernel(rows_hbm, x_hbm, *refs):
    outs, (rows_ref, x_ref, xt_ref, rows_sem, x_sem) = refs[:-5], refs[-5:]
    rounds = len(outs)
    rows_copy = pltpu.make_async_copy(rows_hbm, rows_ref, rows_sem)
    x_copy = pltpu.make_async_copy(x_hbm, x_ref, x_sem)
    rows_copy.start()
    x_copy.start()
    rows_copy.wait()
    count, step = x_ref.shape[0], 2 * TILE
    numbers = lax.broadcasted_iota(jnp.int32, (count, step), 0)
    for r in range(rounds):
        for k in range(0, rows_ref.shape[1], step):
            listed = rows_ref[r : r + 1, k : k + step]
            table = jnp.where(numbers == listed, 1.0, 0.0).astype(jnp.bfloat16)
            if r == 0 and k == 0:
                x_copy.wait()
                for i in range(0, count, TILE):
                    xt_ref[:, i : i + TILE] = x_ref[i : i + TILE, :].T
            outs[r][:, k : k + step] = nn_dot(xt_ref[...], table).astype(jnp.bfloat16)


def pick_rows(send_rows, features):
    rows, width = features.shape
    rounds, boundary = send_rows.shape
    outs = [jax.ShapeDtypeStruct((width, boundary), jnp.bfloat16) for _ in range(rounds)]
    return pl.pallas_call(
        pick_kernel,
        out_shape=outs,
        in_specs=[pl.BlockSpec(memory_space=pltpu.HBM)] * 2,
        out_specs=[vspec()] * len(outs),
        scratch_shapes=[
            VMEM(send_rows.shape, jnp.int32),
            VMEM(features.shape, jnp.bfloat16),
            VMEM((width, rows), jnp.bfloat16),
            pltpu.SemaphoreType.DMA,
            pltpu.SemaphoreType.DMA,
        ],
        compiler_params=params(),
        cost_estimate=cost(2 * rows * boundary * rounds * width, 1_000_000),
    )(in_hbm(send_rows), in_hbm(features))


def densify_kernel(
    lc_hbm, hc_hbm, lt, ht, dl0, dl1, dh0, dh1, lslots, hslots, zeros, lc, hc, sems, zsems, csems
):
    half = lt.shape[0] // 2
    depth = lslots.shape[0]
    dense = (dl0, dl1, dh0, dh1)

    def fetch(i, slot):
        return [
            pltpu.make_async_copy(
                src.at[i + p * half], dst.at[slot, p], sems.at[slot, 2 * q + p]
            )
            for q, (src, dst) in enumerate(((lt, lslots), (ht, hslots)))
            for p in range(2)
        ]

    def clear(i, slot):
        rows = pl.ds(pl.multiple_of(i * TILE, TILE), TILE)
        return [
            pltpu.make_async_copy(
                zeros.at[pl.ds(0, d.shape[0])], d.at[:, rows, :], zsems.at[slot, k]
            )
            for k, d in enumerate(dense)
        ]

    for d in range(depth - 1):
        for copy in fetch(d, d):
            copy.start()
    columns = [
        pltpu.make_async_copy(lc_hbm, lc, csems.at[0]),
        pltpu.make_async_copy(hc_hbm, hc, csems.at[1]),
    ]
    for copy in columns:
        copy.start()
    zeros[...] = jnp.zeros_like(zeros)
    for copy in clear(0, 0):
        copy.start()
    for copy in columns:
        copy.wait()

    def body(i, carry):
        slot, zslot = lax.rem(i, depth), lax.rem(i, 2)

        @pl.when(i + depth - 1 < half)
        def _():
            for copy in fetch(i + depth - 1, lax.rem(i + depth - 1, depth)):
                copy.start()

        @pl.when(i + 1 < half)
        def _():
            for copy in clear(i + 1, 1 - zslot):
                copy.start()

        for copy in clear(i, zslot):
            copy.wait()
        for copy in fetch(i, slot):
            copy.wait()
        rows = pl.ds(pl.multiple_of(i * TILE, TILE), TILE)
        for t in range(max(lt.shape[1], ht.shape[1])):
            jobs = []
            if t < lt.shape[1]:
                jobs += [(dl0, lc[i, t], lslots, 0), (dl1, lc[i + half, t], lslots, 1)]
            if t < ht.shape[1]:
                jobs += [(dh0, hc[i, t], hslots, 0), (dh1, hc[i + half, t], hslots, 1)]
            sums = [d[c, rows, :] + s[slot, p, t] for d, c, s, p in jobs]
            for (d, c, _, _), total in zip(jobs, sums):
                d[c, rows, :] = total
        return carry

    lax.fori_loop(0, half, body, 0)


def densify(local_cols, halo_cols, local_tiles, halo_tiles, halo_blocks):
    nblocks, local_count = local_cols.shape
    halo_count = halo_cols.shape[1]
    half = nblocks // 2 * TILE
    depth = 3
    slabs = (nblocks, nblocks, halo_blocks, halo_blocks)
    return pl.pallas_call(
        densify_kernel,
        out_shape=[VMEM((n, half, TILE), jnp.bfloat16) for n in slabs],
        in_specs=[pl.BlockSpec(memory_space=pltpu.HBM)] * 4,
        out_specs=[vspec()] * 4,
        scratch_shapes=[
            VMEM((depth, 2, local_count, TILE, TILE), jnp.bfloat16),
            VMEM((depth, 2, halo_count, TILE, TILE), jnp.bfloat16),
            VMEM((max(slabs), TILE, TILE), jnp.bfloat16),
            pltpu.SMEM(local_cols.shape, jnp.int32),
            pltpu.SMEM(halo_cols.shape, jnp.int32),
            pltpu.SemaphoreType.DMA((depth, 4)),
            pltpu.SemaphoreType.DMA((2, 4)),
            pltpu.SemaphoreType.DMA((2,)),
        ],
        compiler_params=params(12 * 1024 * 1024),
        cost_estimate=cost(16_000_000, nblocks * (local_count + halo_count) * TILE * TILE * 2),
    )(in_hbm(local_cols), in_hbm(halo_cols), in_hbm(local_tiles), in_hbm(halo_tiles))


def local_sums_kernel(d0_ref, d1_ref, x_ref, out_ref):
    half, step = d0_ref.shape[1], 512
    for p, dense_ref in enumerate((d0_ref, d1_ref)):
        for j in range(0, half, step):
            left = jnp.concatenate(
                [dense_ref[c, j : j + step, :] for c in range(dense_ref.shape[0])], axis=1
            )
            out_ref[p * half + j : p * half + j + step, :] = nn_dot(left, x_ref[...])


def local_sums(d0, d1, features):
    rows, width = features.shape
    return pl.pallas_call(
        local_sums_kernel,
        out_shape=VMEM((rows, width), jnp.float32),
        in_specs=[vspec()] * 3,
        out_specs=vspec(),
        compiler_params=params(),
        cost_estimate=cost(2 * rows * rows * width, 1_500_000),
    )(pinned(d0), pinned(d1), features)


def middle_kernel(rounds, *refs):
    got, refs = refs[:rounds], refs[rounds:]
    d0, d1, sum_ref, x_ref, ct_ref, deg_ref, ws_ref, wn_ref, bias_ref = refs[:9]
    out_ref, gp_ref, st_ref, mine_ref, give_ref, both, halo, sums = refs[9:]
    core = lax.axis_index("dom") & 1
    half, step = d0.shape[1], 512
    boundary = got[0].shape[1]
    per = boundary // TILE
    for r in range(rounds):
        halo[r * boundary : (r + 1) * boundary, :] = got[r][...].T
    for p, dense_ref in enumerate((d0, d1)):
        for j in range(0, half, step):
            start = p * half + j
            total = sum_ref[start : start + step, :]
            for r in range(rounds):
                left = jnp.concatenate(
                    [dense_ref[c, j : j + step, :] for c in range(r * per, (r + 1) * per)], axis=1
                )
                total = total + nn_dot(left, halo[r * boundary : (r + 1) * boundary, :])
            sums[start : start + step, :] = total
    for start in range(0, 2 * half, step):
        total = sums[start : start + step, :]
        for i in range(start // TILE, (start + step) // TILE):
            rows = slice(i * TILE, (i + 1) * TILE)
            line = deg_ref[i : i + 1, :].astype(jnp.float32)
            column = jnp.broadcast_to(line, (TILE, TILE)).T
            agg = total[i * TILE - start : (i + 1) * TILE - start, :] / column
            agg = agg.astype(jnp.bfloat16)
            both[rows, :TILE] = x_ref[rows, :]
            both[rows, TILE:] = agg
            preact = nn_dot(x_ref[rows, :], ws_ref[...]) + nn_dot(agg, wn_ref[...])
            preact = preact + bias_ref[...]
            sig = jax.nn.sigmoid(preact)
            out_ref[rows, :] = (preact * sig).astype(jnp.bfloat16)
            grad = ct_ref[rows, :].astype(jnp.float32) * sig * (1.0 + preact * (1.0 - sig))
            grad = grad.astype(jnp.bfloat16)
            gp_ref[rows, :] = grad
            st_ref[:, rows] = (nt_dot(wn_ref[...], grad) / line).astype(jnp.bfloat16)
    parts = lax.dot_general(
        both[...], gp_ref[...], (((0,), (0,)), ((), ())), preferred_element_type=jnp.float32
    )
    mine_ref[...] = jnp.where(core == 0, parts[:TILE], parts[TILE:])
    give_ref[...] = jnp.where(core == 0, parts[TILE:], parts[:TILE])


def middle(received, d0, d1, summed, features, cotangent, degree, w_self, w_neigh, bias):
    rows, width = features.shape
    rounds, boundary = len(received), received[0].shape[1]
    half = jax.ShapeDtypeStruct((rows, width), jnp.bfloat16)
    part = VMEM((width, width), jnp.float32)
    return pl.pallas_call(
        functools.partial(middle_kernel, rounds),
        out_shape=[
            half,
            VMEM((rows, width), jnp.bfloat16),
            VMEM((width, rows), jnp.bfloat16),
            part,
            part,
        ],
        in_specs=[vspec()] * (rounds + 9),
        out_specs=[vspec()] * 5,
        scratch_shapes=[
            VMEM((rows, 2 * width), jnp.bfloat16),
            VMEM((rounds * boundary, width), jnp.bfloat16),
            VMEM((rows, width), jnp.float32),
        ],
        compiler_params=params(),
        cost_estimate=cost(2 * rows * rounds * boundary * width, 5_000_000, rows * width),
    )(
        *received,
        pinned(d0),
        pinned(d1),
        pinned(summed),
        features,
        cotangent,
        degree,
        w_self,
        w_neigh,
        bias,
    )


def beside(d0_ref, d1_ref, slab):
    return jnp.concatenate(
        [jnp.concatenate([d[slab], d[slab + 1]], axis=1) for d in (d0_ref, d1_ref)], axis=0
    )


def back_kernel(first, n, st_ref, d0_ref, d1_ref, before_ref, out_ref):
    for c in range(0, n, 2):
        product = nn_dot(st_ref[...], beside(d0_ref, d1_ref, first + c))
        out_ref[:, c * TILE : (c + 2) * TILE] = product.astype(jnp.bfloat16)


def back(first, n, scaled_t, d0, d1, before):
    width, rows = scaled_t.shape
    return pl.pallas_call(
        functools.partial(back_kernel, first, n),
        out_shape=jax.ShapeDtypeStruct((width, n * TILE), jnp.bfloat16),
        in_specs=[vspec()] * 3 + [pl.BlockSpec(memory_space=pl.ANY)],
        out_specs=vspec(),
        compiler_params=params(),
        cost_estimate=cost(1, 1),
    )(pinned(scaled_t), pinned(d0), pinned(d1), before)


def own_kernel(st_ref, d0_ref, d1_ref, gp_ref, ws_ref, before_ref, out_ref):
    for c in range(0, d0_ref.shape[0], 2):
        rows = slice(c * TILE, (c + 2) * TILE)
        product = nn_dot(st_ref[...], beside(d0_ref, d1_ref, c))
        out_ref[:, rows] = product + nt_dot(ws_ref[...], gp_ref[rows, :])


def own(scaled_t, d0, d1, grad_pre, w_self, before):
    width, rows = scaled_t.shape
    return pl.pallas_call(
        own_kernel,
        out_shape=VMEM((width, rows), jnp.float32),
        in_specs=[vspec()] * 5 + [pl.BlockSpec(memory_space=pl.ANY)],
        out_specs=vspec(),
        compiler_params=params(),
        cost_estimate=cost(1, 1),
    )(pinned(scaled_t), pinned(d0), pinned(d1), pinned(grad_pre), w_self, before)


def place_kernel(rounds, last, rows_ref, acc_ref, before_ref, *refs):
    returned, (out_ref, token_ref, listed) = refs[: len(rounds)], refs[len(rounds) :]
    token_ref[...] = jnp.zeros_like(token_ref)
    step, boundary = 2 * TILE, rows_ref.shape[1]
    for place, r in enumerate(rounds):
        for k in range(0, boundary, TILE):
            line = rows_ref[r : r + 1, k : k + TILE].astype(jnp.float32)
            listed[place, k : k + TILE, :] = jnp.broadcast_to(line, (TILE, TILE)).T
    numbers = lax.broadcasted_iota(jnp.int32, (boundary, TILE), 1).astype(jnp.float32)
    for j in range(0, acc_ref.shape[1], step):
        total = acc_ref[:, j : j + step]
        for place, got_ref in enumerate(returned):
            table = jnp.concatenate(
                [
                    jnp.where(listed[place] == numbers + float(n), 1.0, 0.0).astype(jnp.bfloat16)
                    for n in range(j, j + step, TILE)
                ],
                axis=1,
            )
            total = total + nn_dot(got_ref[...], table)
        if last:
            out_ref[j : j + step, :] = total.T
        else:
            out_ref[:, j : j + step] = total


def place_rows(rounds, last, send_rows, acc, returned, before):
    width, rows = acc.shape
    count, boundary = len(rounds), send_rows.shape[1]
    if last:
        out = jax.ShapeDtypeStruct((rows, width), jnp.float32)
    else:
        out = VMEM((width, rows), jnp.float32)
    return pl.pallas_call(
        functools.partial(place_kernel, rounds, last),
        out_shape=[out, VMEM((8, TILE), jnp.float32)],
        in_specs=[vspec()] * 2 + [pl.BlockSpec(memory_space=pl.ANY)] + [vspec()] * count,
        out_specs=[vspec()] * 2,
        scratch_shapes=[VMEM((count, boundary, TILE), jnp.float32)],
        compiler_params=params(),
        cost_estimate=cost(1, 1),
    )(send_rows, pinned(acc), before, *returned)


def add_kernel(left_ref, before_ref, *refs):
    others, out_ref = refs[:-1], refs[-1]
    total = left_ref[...] + others[0][...]
    if len(others) == 3:
        total = total + (others[1][...] + others[2][...])
    out_ref[...] = total


def added(left, others, before):
    return pl.pallas_call(
        add_kernel,
        out_shape=VMEM(left.shape, jnp.float32),
        in_specs=[vspec(), pl.BlockSpec(memory_space=pl.ANY)] + [vspec()] * len(others),
        out_specs=vspec(),
        compiler_params=params(1024 * 1024),
        cost_estimate=cost(1, 1),
    )(pinned(left), before, *others)


def halves_kernel(scale, total_ref, other_ref, before_ref, self_ref, neigh_ref):
    core = lax.axis_index("dom") & 1
    total, other = total_ref[...], other_ref[...]
    self_ref[...] = jnp.where(core == 0, total, other) * scale
    neigh_ref[...] = jnp.where(core == 0, other, total) * scale


def halves(scale, total, other, before):
    out = jax.ShapeDtypeStruct(total.shape, jnp.float32)
    return pl.pallas_call(
        functools.partial(halves_kernel, scale),
        out_shape=[out, out],
        in_specs=[vspec()] * 2 + [pl.BlockSpec(memory_space=pl.ANY)],
        out_specs=[vspec()] * 2,
        compiler_params=params(1024 * 1024),
        cost_estimate=cost(2 * total.size, 4 * total.size * 4),
    )(pinned(total), other, before)


def swapped(shard, mask):
    return lax.ppermute(shard, "dom", [(i, i ^ mask) for i in range(lax.axis_size("dom"))])


def local(
    node_features,
    w_self,
    w_neigh,
    output_bias,
    local_tiles,
    halo_tiles,
    local_cols,
    halo_cols,
    send_rows,
    degree,
    cotangent,
):
    row_count, width = node_features.shape
    nblocks = local_tiles.shape[0]
    round_count, boundary = send_rows.shape
    per = boundary // TILE
    picked = pick_rows(send_rows, node_features)
    received = [swapped(rows, 1 << r) for r, rows in enumerate(picked)]
    dl0, dl1, dh0, dh1 = densify(
        local_cols, halo_cols, local_tiles, halo_tiles, round_count * per
    )
    summed = local_sums(dl0, dl1, node_features)
    output, grad_pre, scaled_t, mine, give = middle(
        received,
        dh0,
        dh1,
        summed,
        node_features,
        cotangent,
        degree.reshape(nblocks, TILE),
        w_self,
        w_neigh,
        output_bias.reshape(1, width),
    )
    returned = {}

    def send_back(r, before):
        grads = back(r * per, per, scaled_t, dh0, dh1, before)
        returned[r] = swapped(grads, 1 << r)
        return grads

    def place(rounds, acc, before):
        got = [returned[r] for r in rounds]
        return place_rows(rounds, 0 in rounds, send_rows, acc, got, before)

    others = [swapped(give, 1)]
    last = send_back(2, scaled_t)
    total = added(mine, others, last)
    others = [swapped(total, mask) for mask in (32, 64, 96)]
    last = send_back(4, total)
    last = send_back(1, last)
    total = added(total, others, last)
    others = [swapped(total, 8)]
    last = send_back(3, total)
    total = added(total, others, last)
    others = [swapped(total, 24)]
    grads_t = own(scaled_t, dl0, dl1, grad_pre, w_self, total)
    last = send_back(0, grads_t)
    total = added(total, others, last)
    others = [swapped(total, mask) for mask in (2, 4, 6)]
    grads_t, last = place((2,), grads_t, total)
    grads_t, last = place((4,), grads_t, last)
    grads_t, last = place((3, 1), grads_t, last)
    total = added(total, others, last)
    other = swapped(total, 1)
    grads, last = place((0,), grads_t, total)
    grad_scale = 1.0 / math.sqrt(row_count * lax.axis_size("dom"))
    grad_self, grad_neigh = halves(grad_scale, total, other, last)
    return (output, grads, grad_self, grad_neigh)


def solution(mesh):
    in_specs = (
        P("dom", None),
        P(),
        P(),
        P(),
        P("dom", None, None, None),
        P("dom", None, None, None),
        P("dom", None),
        P("dom", None),
        P("dom", None),
        P("dom"),
        P("dom", None),
    )
    out_specs = (P("dom", None), P("dom", None), P(), P())
    return jax.shard_map(local, mesh=mesh, in_specs=in_specs, out_specs=out_specs, check_vma=False)
```

```python
import functools
import math

import jax
import jax.numpy as jnp
from jax import lax
from jax.experimental import pallas as pl
from jax.experimental.pallas import tpu as pltpu
from jax.sharding import PartitionSpec as P

TILE = 128
VMEM = pltpu.VMEM
LIMIT = 8 * 1024 * 1024


def vspec():
    return pl.BlockSpec(memory_space=VMEM)


def sspec():
    return pl.BlockSpec(memory_space=pltpu.SMEM)


def params(limit=LIMIT):
    return pltpu.CompilerParams(vmem_limit_bytes=limit)


def in_hbm(array):
    return pltpu.with_memory_space_constraint(array, pltpu.HBM)


def cost(flops, size, transcendentals=0):
    return pl.CostEstimate(flops=flops, bytes_accessed=size, transcendentals=transcendentals)


def pinned(array):
    return pltpu.with_memory_space_constraint(array, VMEM)


def nt_dot(left, right):
    return lax.dot_general(
        left, right, (((1,), (1,)), ((), ())), preferred_element_type=jnp.float32
    )


def nn_dot(left, right):
    return jnp.dot(left, right, preferred_element_type=jnp.float32)


def pick_kernel(rows_hbm, x_hbm, *refs):
    outs, (rows_ref, x_ref, xt_ref, rows_sem, x_sem) = refs[:-5], refs[-5:]
    rounds = len(outs)
    rows_copy = pltpu.make_async_copy(rows_hbm, rows_ref, rows_sem)
    x_copy = pltpu.make_async_copy(x_hbm, x_ref, x_sem)
    rows_copy.start()
    x_copy.start()
    rows_copy.wait()
    count, step = x_ref.shape[0], 2 * TILE
    numbers = lax.broadcasted_iota(jnp.int32, (count, step), 0)
    for r in range(rounds):
        for k in range(0, rows_ref.shape[1], step):
            listed = rows_ref[r : r + 1, k : k + step]
            table = jnp.where(numbers == listed, 1.0, 0.0).astype(jnp.bfloat16)
            if r == 0 and k == 0:
                x_copy.wait()
                for i in range(0, count, TILE):
                    xt_ref[:, i : i + TILE] = x_ref[i : i + TILE, :].T
            outs[r][:, k : k + step] = nn_dot(xt_ref[...], table).astype(jnp.bfloat16)


def pick_rows(send_rows, features):
    rows, width = features.shape
    rounds, boundary = send_rows.shape
    outs = [jax.ShapeDtypeStruct((width, boundary), jnp.bfloat16) for _ in range(rounds)]
    return pl.pallas_call(
        pick_kernel,
        out_shape=outs,
        in_specs=[pl.BlockSpec(memory_space=pltpu.HBM)] * 2,
        out_specs=[vspec()] * len(outs),
        scratch_shapes=[
            VMEM(send_rows.shape, jnp.int32),
            VMEM(features.shape, jnp.bfloat16),
            VMEM((width, rows), jnp.bfloat16),
            pltpu.SemaphoreType.DMA,
            pltpu.SemaphoreType.DMA,
        ],
        compiler_params=params(),
        cost_estimate=cost(2 * rows * boundary * rounds * width, 1_000_000),
    )(in_hbm(send_rows), in_hbm(features))


def densify_kernel(
    lc_hbm, hc_hbm, lt, ht, dl0, dl1, dh0, dh1, lslots, hslots, zeros, lc, hc, sems, zsems, csems
):
    half = lt.shape[0] // 2
    depth = lslots.shape[0]
    dense = (dl0, dl1, dh0, dh1)

    def fetch(i, slot):
        return [
            pltpu.make_async_copy(
                src.at[i + p * half], dst.at[slot, p], sems.at[slot, 2 * q + p]
            )
            for q, (src, dst) in enumerate(((lt, lslots), (ht, hslots)))
            for p in range(2)
        ]

    def clear(i, slot):
        rows = pl.ds(pl.multiple_of(i * TILE, TILE), TILE)
        return [
            pltpu.make_async_copy(
                zeros.at[pl.ds(0, d.shape[0])], d.at[:, rows, :], zsems.at[slot, k]
            )
            for k, d in enumerate(dense)
        ]

    for d in range(depth - 1):
        for copy in fetch(d, d):
            copy.start()
    columns = [
        pltpu.make_async_copy(lc_hbm, lc, csems.at[0]),
        pltpu.make_async_copy(hc_hbm, hc, csems.at[1]),
    ]
    for copy in columns:
        copy.start()
    zeros[...] = jnp.zeros_like(zeros)
    for copy in clear(0, 0):
        copy.start()
    for copy in columns:
        copy.wait()

    def body(i, carry):
        slot, zslot = lax.rem(i, depth), lax.rem(i, 2)

        @pl.when(i + depth - 1 < half)
        def _():
            for copy in fetch(i + depth - 1, lax.rem(i + depth - 1, depth)):
                copy.start()

        @pl.when(i + 1 < half)
        def _():
            for copy in clear(i + 1, 1 - zslot):
                copy.start()

        for copy in clear(i, zslot):
            copy.wait()
        for copy in fetch(i, slot):
            copy.wait()
        rows = pl.ds(pl.multiple_of(i * TILE, TILE), TILE)
        for t in range(max(lt.shape[1], ht.shape[1])):
            jobs = []
            if t < lt.shape[1]:
                jobs += [(dl0, lc[i, t], lslots, 0), (dl1, lc[i + half, t], lslots, 1)]
            if t < ht.shape[1]:
                jobs += [(dh0, hc[i, t], hslots, 0), (dh1, hc[i + half, t], hslots, 1)]
            sums = [d[c, rows, :] + s[slot, p, t] for d, c, s, p in jobs]
            for (d, c, _, _), total in zip(jobs, sums):
                d[c, rows, :] = total
        return carry

    lax.fori_loop(0, half, body, 0)


def densify(local_cols, halo_cols, local_tiles, halo_tiles, halo_blocks):
    nblocks, local_count = local_cols.shape
    halo_count = halo_cols.shape[1]
    half = nblocks // 2 * TILE
    depth = 3
    slabs = (nblocks, nblocks, halo_blocks, halo_blocks)
    return pl.pallas_call(
        densify_kernel,
        out_shape=[VMEM((n, half, TILE), jnp.bfloat16) for n in slabs],
        in_specs=[pl.BlockSpec(memory_space=pltpu.HBM)] * 4,
        out_specs=[vspec()] * 4,
        scratch_shapes=[
            VMEM((depth, 2, local_count, TILE, TILE), jnp.bfloat16),
            VMEM((depth, 2, halo_count, TILE, TILE), jnp.bfloat16),
            VMEM((max(slabs), TILE, TILE), jnp.bfloat16),
            pltpu.SMEM(local_cols.shape, jnp.int32),
            pltpu.SMEM(halo_cols.shape, jnp.int32),
            pltpu.SemaphoreType.DMA((depth, 4)),
            pltpu.SemaphoreType.DMA((2, 4)),
            pltpu.SemaphoreType.DMA((2,)),
        ],
        compiler_params=params(12 * 1024 * 1024),
        cost_estimate=cost(16_000_000, nblocks * (local_count + halo_count) * TILE * TILE * 2),
    )(in_hbm(local_cols), in_hbm(halo_cols), in_hbm(local_tiles), in_hbm(halo_tiles))


def local_sums_kernel(d0_ref, d1_ref, x_ref, out_ref):
    half, step = d0_ref.shape[1], 512
    for p, dense_ref in enumerate((d0_ref, d1_ref)):
        for j in range(0, half, step):
            left = jnp.concatenate(
                [dense_ref[c, j : j + step, :] for c in range(dense_ref.shape[0])], axis=1
            )
            out_ref[p * half + j : p * half + j + step, :] = nn_dot(left, x_ref[...])


def local_sums(d0, d1, features):
    rows, width = features.shape
    return pl.pallas_call(
        local_sums_kernel,
        out_shape=VMEM((rows, width), jnp.float32),
        in_specs=[vspec()] * 3,
        out_specs=vspec(),
        compiler_params=params(),
        cost_estimate=cost(2 * rows * rows * width, 1_500_000),
    )(pinned(d0), pinned(d1), features)


def middle_kernel(rounds, *refs):
    got, refs = refs[:rounds], refs[rounds:]
    d0, d1, sum_ref, x_ref, ct_ref, deg_ref, ws_ref, wn_ref, bias_ref = refs[:9]
    out_ref, gp_ref, st_ref, mine_ref, give_ref, both, halo, sums = refs[9:]
    core = lax.axis_index("dom") & 1
    half, step = d0.shape[1], 512
    boundary = got[0].shape[1]
    per = boundary // TILE
    for r in range(rounds):
        halo[r * boundary : (r + 1) * boundary, :] = got[r][...].T
    for p, dense_ref in enumerate((d0, d1)):
        for j in range(0, half, step):
            start = p * half + j
            total = sum_ref[start : start + step, :]
            for r in range(rounds):
                left = jnp.concatenate(
                    [dense_ref[c, j : j + step, :] for c in range(r * per, (r + 1) * per)], axis=1
                )
                total = total + nn_dot(left, halo[r * boundary : (r + 1) * boundary, :])
            sums[start : start + step, :] = total
    for start in range(0, 2 * half, step):
        total = sums[start : start + step, :]
        for i in range(start // TILE, (start + step) // TILE):
            rows = slice(i * TILE, (i + 1) * TILE)
            line = deg_ref[i : i + 1, :].astype(jnp.float32)
            column = jnp.broadcast_to(line, (TILE, TILE)).T
            agg = total[i * TILE - start : (i + 1) * TILE - start, :] / column
            agg = agg.astype(jnp.bfloat16)
            both[rows, :TILE] = x_ref[rows, :]
            both[rows, TILE:] = agg
            preact = nn_dot(x_ref[rows, :], ws_ref[...]) + nn_dot(agg, wn_ref[...])
            preact = preact + bias_ref[...]
            sig = jax.nn.sigmoid(preact)
            out_ref[rows, :] = (preact * sig).astype(jnp.bfloat16)
            grad = ct_ref[rows, :].astype(jnp.float32) * sig * (1.0 + preact * (1.0 - sig))
            grad = grad.astype(jnp.bfloat16)
            gp_ref[rows, :] = grad
            st_ref[:, rows] = (nt_dot(wn_ref[...], grad) / line).astype(jnp.bfloat16)
    parts = lax.dot_general(
        both[...], gp_ref[...], (((0,), (0,)), ((), ())), preferred_element_type=jnp.float32
    )
    mine_ref[...] = jnp.where(core == 0, parts[:TILE], parts[TILE:])
    give_ref[...] = jnp.where(core == 0, parts[TILE:], parts[:TILE])


def middle(received, d0, d1, summed, features, cotangent, degree, w_self, w_neigh, bias):
    rows, width = features.shape
    rounds, boundary = len(received), received[0].shape[1]
    half = jax.ShapeDtypeStruct((rows, width), jnp.bfloat16)
    part = VMEM((width, width), jnp.float32)
    return pl.pallas_call(
        functools.partial(middle_kernel, rounds),
        out_shape=[
            half,
            VMEM((rows, width), jnp.bfloat16),
            VMEM((width, rows), jnp.bfloat16),
            part,
            part,
        ],
        in_specs=[vspec()] * (rounds + 9),
        out_specs=[vspec()] * 5,
        scratch_shapes=[
            VMEM((rows, 2 * width), jnp.bfloat16),
            VMEM((rounds * boundary, width), jnp.bfloat16),
            VMEM((rows, width), jnp.float32),
        ],
        compiler_params=params(),
        cost_estimate=cost(2 * rows * rounds * boundary * width, 5_000_000, rows * width),
    )(
        *received,
        pinned(d0),
        pinned(d1),
        pinned(summed),
        features,
        cotangent,
        degree,
        w_self,
        w_neigh,
        bias,
    )


def beside(d0_ref, d1_ref, slab):
    return jnp.concatenate(
        [jnp.concatenate([d[slab], d[slab + 1]], axis=1) for d in (d0_ref, d1_ref)], axis=0
    )


def back_kernel(first, n, st_ref, d0_ref, d1_ref, before_ref, out_ref):
    for c in range(0, n, 2):
        product = nn_dot(st_ref[...], beside(d0_ref, d1_ref, first + c))
        out_ref[:, c * TILE : (c + 2) * TILE] = product.astype(jnp.bfloat16)


def back(first, n, scaled_t, d0, d1, before):
    width, rows = scaled_t.shape
    return pl.pallas_call(
        functools.partial(back_kernel, first, n),
        out_shape=jax.ShapeDtypeStruct((width, n * TILE), jnp.bfloat16),
        in_specs=[vspec()] * 3 + [pl.BlockSpec(memory_space=pl.ANY)],
        out_specs=vspec(),
        compiler_params=params(),
        cost_estimate=cost(1, 1),
    )(pinned(scaled_t), pinned(d0), pinned(d1), before)


def own_kernel(st_ref, d0_ref, d1_ref, gp_ref, ws_ref, before_ref, out_ref):
    for c in range(0, d0_ref.shape[0], 2):
        rows = slice(c * TILE, (c + 2) * TILE)
        product = nn_dot(st_ref[...], beside(d0_ref, d1_ref, c))
        out_ref[:, rows] = product + nt_dot(ws_ref[...], gp_ref[rows, :])


def own(scaled_t, d0, d1, grad_pre, w_self, before):
    width, rows = scaled_t.shape
    return pl.pallas_call(
        own_kernel,
        out_shape=VMEM((width, rows), jnp.float32),
        in_specs=[vspec()] * 5 + [pl.BlockSpec(memory_space=pl.ANY)],
        out_specs=vspec(),
        compiler_params=params(),
        cost_estimate=cost(1, 1),
    )(pinned(scaled_t), pinned(d0), pinned(d1), pinned(grad_pre), w_self, before)


def place_kernel(rounds, last, rows_ref, acc_ref, before_ref, *refs):
    returned, (out_ref, token_ref, listed) = refs[: len(rounds)], refs[len(rounds) :]
    token_ref[...] = jnp.zeros_like(token_ref)
    step, boundary = 2 * TILE, rows_ref.shape[1]
    for place, r in enumerate(rounds):
        for k in range(0, boundary, TILE):
            line = rows_ref[r : r + 1, k : k + TILE].astype(jnp.float32)
            listed[place, k : k + TILE, :] = jnp.broadcast_to(line, (TILE, TILE)).T
    numbers = lax.broadcasted_iota(jnp.int32, (boundary, TILE), 1).astype(jnp.float32)
    for j in range(0, acc_ref.shape[1], step):
        total = acc_ref[:, j : j + step]
        for place, got_ref in enumerate(returned):
            table = jnp.concatenate(
                [
                    jnp.where(listed[place] == numbers + float(n), 1.0, 0.0).astype(jnp.bfloat16)
                    for n in range(j, j + step, TILE)
                ],
                axis=1,
            )
            total = total + nn_dot(got_ref[...], table)
        if last:
            out_ref[j : j + step, :] = total.T
        else:
            out_ref[:, j : j + step] = total


def place_rows(rounds, last, send_rows, acc, returned, before):
    width, rows = acc.shape
    count, boundary = len(rounds), send_rows.shape[1]
    if last:
        out = jax.ShapeDtypeStruct((rows, width), jnp.float32)
    else:
        out = VMEM((width, rows), jnp.float32)
    return pl.pallas_call(
        functools.partial(place_kernel, rounds, last),
        out_shape=[out, VMEM((8, TILE), jnp.float32)],
        in_specs=[vspec()] * 2 + [pl.BlockSpec(memory_space=pl.ANY)] + [vspec()] * count,
        out_specs=[vspec()] * 2,
        scratch_shapes=[VMEM((count, boundary, TILE), jnp.float32)],
        compiler_params=params(),
        cost_estimate=cost(1, 1),
    )(send_rows, pinned(acc), before, *returned)


def add_kernel(left_ref, before_ref, *refs):
    others, out_ref = refs[:-1], refs[-1]
    total = left_ref[...] + others[0][...]
    if len(others) == 3:
        total = total + (others[1][...] + others[2][...])
    out_ref[...] = total


def added(left, others, before):
    return pl.pallas_call(
        add_kernel,
        out_shape=VMEM(left.shape, jnp.float32),
        in_specs=[vspec(), pl.BlockSpec(memory_space=pl.ANY)] + [vspec()] * len(others),
        out_specs=vspec(),
        compiler_params=params(1024 * 1024),
        cost_estimate=cost(1, 1),
    )(pinned(left), before, *others)


def halves_kernel(scale, total_ref, other_ref, before_ref, self_ref, neigh_ref):
    core = lax.axis_index("dom") & 1
    total, other = total_ref[...], other_ref[...]
    self_ref[...] = jnp.where(core == 0, total, other) * scale
    neigh_ref[...] = jnp.where(core == 0, other, total) * scale


def halves(scale, total, other, before):
    out = jax.ShapeDtypeStruct(total.shape, jnp.float32)
    return pl.pallas_call(
        functools.partial(halves_kernel, scale),
        out_shape=[out, out],
        in_specs=[vspec()] * 2 + [pl.BlockSpec(memory_space=pl.ANY)],
        out_specs=[vspec()] * 2,
        compiler_params=params(1024 * 1024),
        cost_estimate=cost(2 * total.size, 4 * total.size * 4),
    )(pinned(total), other, before)


def swapped(shard, mask):
    return lax.ppermute(shard, "dom", [(i, i ^ mask) for i in range(lax.axis_size("dom"))])


def local(
    node_features,
    w_self,
    w_neigh,
    output_bias,
    local_tiles,
    halo_tiles,
    local_cols,
    halo_cols,
    send_rows,
    degree,
    cotangent,
):
    row_count, width = node_features.shape
    nblocks = local_tiles.shape[0]
    round_count, boundary = send_rows.shape
    per = boundary // TILE
    picked = pick_rows(send_rows, node_features)
    received = [swapped(rows, 1 << r) for r, rows in enumerate(picked)]
    dl0, dl1, dh0, dh1 = densify(
        local_cols, halo_cols, local_tiles, halo_tiles, round_count * per
    )
    summed = local_sums(dl0, dl1, node_features)
    output, grad_pre, scaled_t, mine, give = middle(
        received,
        dh0,
        dh1,
        summed,
        node_features,
        cotangent,
        degree.reshape(nblocks, TILE),
        w_self,
        w_neigh,
        output_bias.reshape(1, width),
    )
    returned = {}

    def send_back(r, before):
        grads = back(r * per, per, scaled_t, dh0, dh1, before)
        returned[r] = swapped(grads, 1 << r)
        return grads

    def place(rounds, acc, before):
        got = [returned[r] for r in rounds]
        return place_rows(rounds, 0 in rounds, send_rows, acc, got, before)

    others = [swapped(give, 1)]
    last = send_back(2, scaled_t)
    last = send_back(4, last)
    total = added(mine, others, last)
    others = [swapped(total, mask) for mask in (32, 64, 96)]
    last = send_back(1, total)
    total = added(total, others, last)
    others = [swapped(total, mask) for mask in (8,)]
    last = send_back(3, total)
    total = added(total, others, last)
    others = [swapped(total, mask) for mask in (24,)]
    grads_t = own(scaled_t, dl0, dl1, grad_pre, w_self, total)
    last = send_back(0, grads_t)
    total = added(total, others, last)
    others = [swapped(total, mask) for mask in (2, 4, 6)]
    grads_t, last = place((2,), grads_t, total)
    grads_t, last = place((4,), grads_t, last)
    grads_t, last = place((3,1,), grads_t, last)
    total = added(total, others, last)
    other = swapped(total, 1)
    grads, last = place((0,), grads_t, total)
    grad_scale = 1.0 / math.sqrt(row_count * lax.axis_size("dom"))
    grad_self, grad_neigh = halves(grad_scale, total, other, last)
    return (output, grads, grad_self, grad_neigh)


def solution(mesh):
    in_specs = (
        P("dom", None),
        P(),
        P(),
        P(),
        P("dom", None, None, None),
        P("dom", None, None, None),
        P("dom", None),
        P("dom", None),
        P("dom", None),
        P("dom"),
        P("dom", None),
    )
    out_specs = (P("dom", None), P("dom", None), P(), P())
    return jax.shard_map(local, mesh=mesh, in_specs=in_specs, out_specs=out_specs, check_vma=False)
```

```python
import functools
import math

import jax
import jax.numpy as jnp
from jax import lax
from jax.experimental import pallas as pl
from jax.experimental.pallas import tpu as pltpu
from jax.sharding import PartitionSpec as P

TILE = 128
VMEM = pltpu.VMEM
LIMIT = 8 * 1024 * 1024


def vspec():
    return pl.BlockSpec(memory_space=VMEM)


def sspec():
    return pl.BlockSpec(memory_space=pltpu.SMEM)


def params(limit=LIMIT):
    return pltpu.CompilerParams(vmem_limit_bytes=limit)


def in_hbm(array):
    return pltpu.with_memory_space_constraint(array, pltpu.HBM)


def cost(flops, size, transcendentals=0):
    return pl.CostEstimate(flops=flops, bytes_accessed=size, transcendentals=transcendentals)


def pinned(array):
    return pltpu.with_memory_space_constraint(array, VMEM)


def nt_dot(left, right):
    return lax.dot_general(
        left, right, (((1,), (1,)), ((), ())), preferred_element_type=jnp.float32
    )


def nn_dot(left, right):
    return jnp.dot(left, right, preferred_element_type=jnp.float32)


def pick_kernel(rows_hbm, x_hbm, *refs):
    outs, (rows_ref, x_ref, xt_ref, rows_sem, x_sem) = refs[:-5], refs[-5:]
    rounds = len(outs)
    rows_copy = pltpu.make_async_copy(rows_hbm, rows_ref, rows_sem)
    x_copy = pltpu.make_async_copy(x_hbm, x_ref, x_sem)
    rows_copy.start()
    x_copy.start()
    rows_copy.wait()
    count, step = x_ref.shape[0], 2 * TILE
    numbers = lax.broadcasted_iota(jnp.int32, (count, step), 0)
    for r in range(rounds):
        for k in range(0, rows_ref.shape[1], step):
            listed = rows_ref[r : r + 1, k : k + step]
            table = jnp.where(numbers == listed, 1.0, 0.0).astype(jnp.bfloat16)
            if r == 0 and k == 0:
                x_copy.wait()
                for i in range(0, count, TILE):
                    xt_ref[:, i : i + TILE] = x_ref[i : i + TILE, :].T
            outs[r][:, k : k + step] = nn_dot(xt_ref[...], table).astype(jnp.bfloat16)


def pick_rows(send_rows, features):
    rows, width = features.shape
    rounds, boundary = send_rows.shape
    outs = [jax.ShapeDtypeStruct((width, boundary), jnp.bfloat16) for _ in range(rounds)]
    return pl.pallas_call(
        pick_kernel,
        out_shape=outs,
        in_specs=[pl.BlockSpec(memory_space=pltpu.HBM)] * 2,
        out_specs=[vspec()] * len(outs),
        scratch_shapes=[
            VMEM(send_rows.shape, jnp.int32),
            VMEM(features.shape, jnp.bfloat16),
            VMEM((width, rows), jnp.bfloat16),
            pltpu.SemaphoreType.DMA,
            pltpu.SemaphoreType.DMA,
        ],
        compiler_params=params(),
        cost_estimate=cost(2 * rows * boundary * rounds * width, 1_000_000),
    )(in_hbm(send_rows), in_hbm(features))


def densify_kernel(
    lc_hbm, hc_hbm, lt, ht, dl0, dl1, dh0, dh1, lslots, hslots, zeros, lc, hc, sems, zsems, csems
):
    half = lt.shape[0] // 2
    depth = lslots.shape[0]
    dense = (dl0, dl1, dh0, dh1)

    def fetch(i, slot):
        return [
            pltpu.make_async_copy(
                src.at[i + p * half], dst.at[slot, p], sems.at[slot, 2 * q + p]
            )
            for q, (src, dst) in enumerate(((lt, lslots), (ht, hslots)))
            for p in range(2)
        ]

    def clear(i, slot):
        rows = pl.ds(pl.multiple_of(i * TILE, TILE), TILE)
        return [
            pltpu.make_async_copy(
                zeros.at[pl.ds(0, d.shape[0])], d.at[:, rows, :], zsems.at[slot, k]
            )
            for k, d in enumerate(dense)
        ]

    for d in range(depth - 1):
        for copy in fetch(d, d):
            copy.start()
    columns = [
        pltpu.make_async_copy(lc_hbm, lc, csems.at[0]),
        pltpu.make_async_copy(hc_hbm, hc, csems.at[1]),
    ]
    for copy in columns:
        copy.start()
    zeros[...] = jnp.zeros_like(zeros)
    for copy in clear(0, 0):
        copy.start()
    for copy in columns:
        copy.wait()

    def body(i, carry):
        slot, zslot = lax.rem(i, depth), lax.rem(i, 2)

        @pl.when(i + depth - 1 < half)
        def _():
            for copy in fetch(i + depth - 1, lax.rem(i + depth - 1, depth)):
                copy.start()

        @pl.when(i + 1 < half)
        def _():
            for copy in clear(i + 1, 1 - zslot):
                copy.start()

        for copy in clear(i, zslot):
            copy.wait()
        for copy in fetch(i, slot):
            copy.wait()
        rows = pl.ds(pl.multiple_of(i * TILE, TILE), TILE)
        for t in range(max(lt.shape[1], ht.shape[1])):
            jobs = []
            if t < lt.shape[1]:
                jobs += [(dl0, lc[i, t], lslots, 0), (dl1, lc[i + half, t], lslots, 1)]
            if t < ht.shape[1]:
                jobs += [(dh0, hc[i, t], hslots, 0), (dh1, hc[i + half, t], hslots, 1)]
            sums = [d[c, rows, :] + s[slot, p, t] for d, c, s, p in jobs]
            for (d, c, _, _), total in zip(jobs, sums):
                d[c, rows, :] = total
        return carry

    lax.fori_loop(0, half, body, 0)


def densify(local_cols, halo_cols, local_tiles, halo_tiles, halo_blocks):
    nblocks, local_count = local_cols.shape
    halo_count = halo_cols.shape[1]
    half = nblocks // 2 * TILE
    depth = 3
    slabs = (nblocks, nblocks, halo_blocks, halo_blocks)
    return pl.pallas_call(
        densify_kernel,
        out_shape=[VMEM((n, half, TILE), jnp.bfloat16) for n in slabs],
        in_specs=[pl.BlockSpec(memory_space=pltpu.HBM)] * 4,
        out_specs=[vspec()] * 4,
        scratch_shapes=[
            VMEM((depth, 2, local_count, TILE, TILE), jnp.bfloat16),
            VMEM((depth, 2, halo_count, TILE, TILE), jnp.bfloat16),
            VMEM((max(slabs), TILE, TILE), jnp.bfloat16),
            pltpu.SMEM(local_cols.shape, jnp.int32),
            pltpu.SMEM(halo_cols.shape, jnp.int32),
            pltpu.SemaphoreType.DMA((depth, 4)),
            pltpu.SemaphoreType.DMA((2, 4)),
            pltpu.SemaphoreType.DMA((2,)),
        ],
        compiler_params=params(12 * 1024 * 1024),
        cost_estimate=cost(16_000_000, nblocks * (local_count + halo_count) * TILE * TILE * 2),
    )(in_hbm(local_cols), in_hbm(halo_cols), in_hbm(local_tiles), in_hbm(halo_tiles))


def local_sums_kernel(d0_ref, d1_ref, x_ref, out_ref):
    half, step = d0_ref.shape[1], 512
    for p, dense_ref in enumerate((d0_ref, d1_ref)):
        for j in range(0, half, step):
            left = jnp.concatenate(
                [dense_ref[c, j : j + step, :] for c in range(dense_ref.shape[0])], axis=1
            )
            out_ref[p * half + j : p * half + j + step, :] = nn_dot(left, x_ref[...])


def local_sums(d0, d1, features):
    rows, width = features.shape
    return pl.pallas_call(
        local_sums_kernel,
        out_shape=VMEM((rows, width), jnp.float32),
        in_specs=[vspec()] * 3,
        out_specs=vspec(),
        compiler_params=params(),
        cost_estimate=cost(2 * rows * rows * width, 1_500_000),
    )(pinned(d0), pinned(d1), features)


def middle_kernel(rounds, *refs):
    got, refs = refs[:rounds], refs[rounds:]
    d0, d1, sum_ref, x_ref, ct_ref, deg_ref, ws_ref, wn_ref, bias_ref = refs[:9]
    out_ref, gp_ref, st_ref, mine_ref, give_ref, both, halo, sums = refs[9:]
    core = lax.axis_index("dom") & 1
    half, step = d0.shape[1], 512
    boundary = got[0].shape[1]
    per = boundary // TILE
    for r in range(rounds):
        halo[r * boundary : (r + 1) * boundary, :] = got[r][...].T
    for p, dense_ref in enumerate((d0, d1)):
        for j in range(0, half, step):
            start = p * half + j
            total = sum_ref[start : start + step, :]
            for r in range(rounds):
                left = jnp.concatenate(
                    [dense_ref[c, j : j + step, :] for c in range(r * per, (r + 1) * per)], axis=1
                )
                total = total + nn_dot(left, halo[r * boundary : (r + 1) * boundary, :])
            sums[start : start + step, :] = total
    for start in range(0, 2 * half, step):
        total = sums[start : start + step, :]
        for i in range(start // TILE, (start + step) // TILE):
            rows = slice(i * TILE, (i + 1) * TILE)
            line = deg_ref[i : i + 1, :].astype(jnp.float32)
            column = jnp.broadcast_to(line, (TILE, TILE)).T
            agg = total[i * TILE - start : (i + 1) * TILE - start, :] / column
            agg = agg.astype(jnp.bfloat16)
            both[rows, :TILE] = x_ref[rows, :]
            both[rows, TILE:] = agg
            preact = nn_dot(x_ref[rows, :], ws_ref[...]) + nn_dot(agg, wn_ref[...])
            preact = preact + bias_ref[...]
            sig = jax.nn.sigmoid(preact)
            out_ref[rows, :] = (preact * sig).astype(jnp.bfloat16)
            grad = ct_ref[rows, :].astype(jnp.float32) * sig * (1.0 + preact * (1.0 - sig))
            grad = grad.astype(jnp.bfloat16)
            gp_ref[rows, :] = grad
            st_ref[:, rows] = (nt_dot(wn_ref[...], grad) / line).astype(jnp.bfloat16)
    parts = lax.dot_general(
        both[...], gp_ref[...], (((0,), (0,)), ((), ())), preferred_element_type=jnp.float32
    )
    mine_ref[...] = jnp.where(core == 0, parts[:TILE], parts[TILE:])
    give_ref[...] = jnp.where(core == 0, parts[TILE:], parts[:TILE])


def middle(received, d0, d1, summed, features, cotangent, degree, w_self, w_neigh, bias):
    rows, width = features.shape
    rounds, boundary = len(received), received[0].shape[1]
    half = jax.ShapeDtypeStruct((rows, width), jnp.bfloat16)
    part = VMEM((width, width), jnp.float32)
    return pl.pallas_call(
        functools.partial(middle_kernel, rounds),
        out_shape=[
            half,
            VMEM((rows, width), jnp.bfloat16),
            VMEM((width, rows), jnp.bfloat16),
            part,
            part,
        ],
        in_specs=[vspec()] * (rounds + 9),
        out_specs=[vspec()] * 5,
        scratch_shapes=[
            VMEM((rows, 2 * width), jnp.bfloat16),
            VMEM((rounds * boundary, width), jnp.bfloat16),
            VMEM((rows, width), jnp.float32),
        ],
        compiler_params=params(),
        cost_estimate=cost(2 * rows * rounds * boundary * width, 5_000_000, rows * width),
    )(
        *received,
        pinned(d0),
        pinned(d1),
        pinned(summed),
        features,
        cotangent,
        degree,
        w_self,
        w_neigh,
        bias,
    )


def beside(d0_ref, d1_ref, slab):
    return jnp.concatenate(
        [jnp.concatenate([d[slab], d[slab + 1]], axis=1) for d in (d0_ref, d1_ref)], axis=0
    )


def back_kernel(first, n, st_ref, d0_ref, d1_ref, before_ref, out_ref):
    for c in range(0, n, 2):
        product = nn_dot(st_ref[...], beside(d0_ref, d1_ref, first + c))
        out_ref[:, c * TILE : (c + 2) * TILE] = product.astype(jnp.bfloat16)


def back(first, n, scaled_t, d0, d1, before):
    width, rows = scaled_t.shape
    return pl.pallas_call(
        functools.partial(back_kernel, first, n),
        out_shape=jax.ShapeDtypeStruct((width, n * TILE), jnp.bfloat16),
        in_specs=[vspec()] * 3 + [pl.BlockSpec(memory_space=pl.ANY)],
        out_specs=vspec(),
        compiler_params=params(),
        cost_estimate=cost(1, 1),
    )(pinned(scaled_t), pinned(d0), pinned(d1), before)


def own_kernel(st_ref, d0_ref, d1_ref, gp_ref, ws_ref, before_ref, out_ref):
    for c in range(0, d0_ref.shape[0], 2):
        rows = slice(c * TILE, (c + 2) * TILE)
        product = nn_dot(st_ref[...], beside(d0_ref, d1_ref, c))
        out_ref[:, rows] = product + nt_dot(ws_ref[...], gp_ref[rows, :])


def own(scaled_t, d0, d1, grad_pre, w_self, before):
    width, rows = scaled_t.shape
    return pl.pallas_call(
        own_kernel,
        out_shape=VMEM((width, rows), jnp.float32),
        in_specs=[vspec()] * 5 + [pl.BlockSpec(memory_space=pl.ANY)],
        out_specs=vspec(),
        compiler_params=params(),
        cost_estimate=cost(1, 1),
    )(pinned(scaled_t), pinned(d0), pinned(d1), pinned(grad_pre), w_self, before)


def place_kernel(rounds, last, rows_ref, acc_ref, before_ref, *refs):
    returned, (out_ref, token_ref, listed) = refs[: len(rounds)], refs[len(rounds) :]
    token_ref[...] = jnp.zeros_like(token_ref)
    step, boundary = 2 * TILE, rows_ref.shape[1]
    for place, r in enumerate(rounds):
        for k in range(0, boundary, TILE):
            line = rows_ref[r : r + 1, k : k + TILE].astype(jnp.float32)
            listed[place, k : k + TILE, :] = jnp.broadcast_to(line, (TILE, TILE)).T
    numbers = lax.broadcasted_iota(jnp.int32, (boundary, TILE), 1).astype(jnp.float32)
    for j in range(0, acc_ref.shape[1], step):
        total = acc_ref[:, j : j + step]
        for place, got_ref in enumerate(returned):
            table = jnp.concatenate(
                [
                    jnp.where(listed[place] == numbers + float(n), 1.0, 0.0).astype(jnp.bfloat16)
                    for n in range(j, j + step, TILE)
                ],
                axis=1,
            )
            total = total + nn_dot(got_ref[...], table)
        if last:
            out_ref[j : j + step, :] = total.T
        else:
            out_ref[:, j : j + step] = total


def place_rows(rounds, last, send_rows, acc, returned, before):
    width, rows = acc.shape
    count, boundary = len(rounds), send_rows.shape[1]
    if last:
        out = jax.ShapeDtypeStruct((rows, width), jnp.float32)
    else:
        out = VMEM((width, rows), jnp.float32)
    return pl.pallas_call(
        functools.partial(place_kernel, rounds, last),
        out_shape=[out, VMEM((8, TILE), jnp.float32)],
        in_specs=[vspec()] * 2 + [pl.BlockSpec(memory_space=pl.ANY)] + [vspec()] * count,
        out_specs=[vspec()] * 2,
        scratch_shapes=[VMEM((count, boundary, TILE), jnp.float32)],
        compiler_params=params(),
        cost_estimate=cost(1, 1),
    )(send_rows, pinned(acc), before, *returned)


def add_kernel(left_ref, before_ref, *refs):
    others, out_ref = refs[:-1], refs[-1]
    total = left_ref[...] + others[0][...]
    if len(others) == 3:
        total = total + (others[1][...] + others[2][...])
    out_ref[...] = total


def added(left, others, before):
    return pl.pallas_call(
        add_kernel,
        out_shape=VMEM(left.shape, jnp.float32),
        in_specs=[vspec(), pl.BlockSpec(memory_space=pl.ANY)] + [vspec()] * len(others),
        out_specs=vspec(),
        compiler_params=params(1024 * 1024),
        cost_estimate=cost(1, 1),
    )(pinned(left), before, *others)


def halves_kernel(scale, total_ref, other_ref, before_ref, self_ref, neigh_ref):
    core = lax.axis_index("dom") & 1
    total, other = total_ref[...], other_ref[...]
    self_ref[...] = jnp.where(core == 0, total, other) * scale
    neigh_ref[...] = jnp.where(core == 0, other, total) * scale


def halves(scale, total, other, before):
    out = jax.ShapeDtypeStruct(total.shape, jnp.float32)
    return pl.pallas_call(
        functools.partial(halves_kernel, scale),
        out_shape=[out, out],
        in_specs=[vspec()] * 2 + [pl.BlockSpec(memory_space=pl.ANY)],
        out_specs=[vspec()] * 2,
        compiler_params=params(1024 * 1024),
        cost_estimate=cost(2 * total.size, 4 * total.size * 4),
    )(pinned(total), other, before)


def swapped(shard, mask):
    return lax.ppermute(shard, "dom", [(i, i ^ mask) for i in range(lax.axis_size("dom"))])


def local(
    node_features,
    w_self,
    w_neigh,
    output_bias,
    local_tiles,
    halo_tiles,
    local_cols,
    halo_cols,
    send_rows,
    degree,
    cotangent,
):
    row_count, width = node_features.shape
    nblocks = local_tiles.shape[0]
    round_count, boundary = send_rows.shape
    per = boundary // TILE
    picked = pick_rows(send_rows, node_features)
    received = [swapped(rows, 1 << r) for r, rows in enumerate(picked)]
    dl0, dl1, dh0, dh1 = densify(
        local_cols, halo_cols, local_tiles, halo_tiles, round_count * per
    )
    summed = local_sums(dl0, dl1, node_features)
    output, grad_pre, scaled_t, mine, give = middle(
        received,
        dh0,
        dh1,
        summed,
        node_features,
        cotangent,
        degree.reshape(nblocks, TILE),
        w_self,
        w_neigh,
        output_bias.reshape(1, width),
    )
    returned = {}

    def send_back(r, before):
        grads = back(r * per, per, scaled_t, dh0, dh1, before)
        returned[r] = swapped(grads, 1 << r)
        return grads

    def place(rounds, acc, before):
        got = [returned[r] for r in rounds]
        return place_rows(rounds, 0 in rounds, send_rows, acc, got, before)

    others = [swapped(give, 1)]
    last = send_back(2, scaled_t)
    last = send_back(4, last)
    total = added(mine, others, last)
    others = [swapped(total, mask) for mask in (32, 64, 96)]
    last = send_back(1, total)
    total = added(total, others, last)
    others = [swapped(total, mask) for mask in (8,)]
    last = send_back(3, total)
    last = send_back(0, last)
    total = added(total, others, last)
    others = [swapped(total, mask) for mask in (24,)]
    grads_t = own(scaled_t, dl0, dl1, grad_pre, w_self, total)
    grads_t, last = place((2,), grads_t, grads_t)
    total = added(total, others, last)
    others = [swapped(total, mask) for mask in (2, 4, 6)]
    grads_t, last = place((4,), grads_t, total)
    grads_t, last = place((3,1,), grads_t, last)
    total = added(total, others, last)
    other = swapped(total, 1)
    grads, last = place((0,), grads_t, total)
    grad_scale = 1.0 / math.sqrt(row_count * lax.axis_size("dom"))
    grad_self, grad_neigh = halves(grad_scale, total, other, last)
    return (output, grads, grad_self, grad_neigh)


def solution(mesh):
    in_specs = (
        P("dom", None),
        P(),
        P(),
        P(),
        P("dom", None, None, None),
        P("dom", None, None, None),
        P("dom", None),
        P("dom", None),
        P("dom", None),
        P("dom"),
        P("dom", None),
    )
    out_specs = (P("dom", None), P("dom", None), P(), P())
    return jax.shard_map(local, mesh=mesh, in_specs=in_specs, out_specs=out_specs, check_vma=False)
```
